512 devices in a mesh: seq: 64 (over y, z), head: 8 (over x, core).
Axes of the slice: x: 4, y: 8, z: 8, core: 2. Of those that a mesh axis runs over, the one named last changes fastest.
Arguments:
- queries: bfloat16 [32768, 4096], P('seq', 'head'), may hold values from -100 to 100
- key_rows: bfloat16 [32768, 1024], P('seq', 'head'), may hold values from -6.1 to 6.1
- value_rows: bfloat16 [32768, 1024], P('seq', 'head'), may hold values from -6 to 6
- doc_blocks: int32 [32], replicated, may hold values from 1 to 32, 256 in all
Outputs:
- attended: bfloat16 [32768, 4096], P(('seq', 'head'))
The draws below stay inside these ranges and needn't reach their ends.
Inputs may be any that keep to these rules, and one draw needn't show every extreme that they name: `doc_blocks`: lengths in blocks of 128 tokens, in order along the sequence; they sum to 256 and the longest is exactly 32.
All inputs are finite; a program needn't handle non-finite values.
Results may differ from the reference program's by a relative error of at most 0.005.
Values may be sent and summed in bfloat16 or wider, within the bound.
A program may use at most 64 MiB of HBM per device.

```python
import math
import jax
import jax.numpy as jnp
import numpy as np
from jax import lax

QH = 32
KVH = 8
HD = 128
B = 128
LONGB = 32
NB = 256
TOKENS = 32768
NDOCS = 32


def shared_keys(key):
    draws = jnp.clip(jax.random.normal(jax.random.fold_in(key, 11), (TOKENS, KVH * HD), jnp.float32), -6.0, 6.0)
    row_ids = jnp.arange(TOKENS)
    marked = row_ids % 64 == 4
    return jnp.where(marked[:, None], draws, draws)


def draw_key_rows(key, part):
    shared = shared_keys(key)
    return shared.astype(jnp.bfloat16)


def draw_queries(key, part):
    key = jax.random.fold_in(key, 3)
    drawn_draw = jax.random.normal(jax.random.fold_in(key, 1), (TOKENS, QH * HD), jnp.float32)
    return jnp.clip(drawn_draw, -6.0, 6.0).astype(jnp.bfloat16)


def levels(stream_key, extent, shards, smallest, high):
    level = 1.0
    for dim, blocks in shards:
        heights = jax.random.uniform(jax.random.fold_in(jax.random.fold_in(stream_key, 6), dim), (blocks,), jnp.float32, smallest / len(shards), high / len(shards))
        level = level * jnp.repeat(jnp.exp(heights), extent[dim] // blocks).reshape((-1,) + (1,) * (len(extent) - 1 - dim))
    return level


def split_up(count, total, reach, lean):
    portions = [(1 << 20) // math.isqrt(rank ** lean) + 1 for rank in range(2, count + 1)]
    spare, holding = total - reach - (count - 1), [1] * (count - 1)
    while spare > 0:
        movable = [i for i in range(count - 1) if holding[i] < reach]
        mass, budget = sum([portions[i] for i in movable]), spare
        for i in movable:
            addition = min(reach - holding[i], max(1, budget * portions[i] // mass), spare)
            holding[i] = holding[i] + addition
            spare = spare - addition
    return np.array([reach] + holding)


def ragged_sizes(stream_key, count, total, reach, slope):
    if count == 2:
        one = jax.random.randint(stream_key, (), max(1, total - reach), min(reach, total - 1) + 1)
        return jnp.stack([one, total - one])
    lengths = jnp.asarray(split_up(count, total, reach, slope), jnp.int32)
    twos = (count - 1) // 2
    giver, receiver = lengths[1:1 + 2 * twos:2], lengths[2:2 + 2 * twos:2]
    margin = jnp.minimum(giver - 1, reach - receiver)
    shifted = jax.random.randint(jax.random.fold_in(stream_key, 1), (twos,), 0, 1 << 20) % (margin + 1)
    lengths = lengths.at[1:1 + 2 * twos:2].set(giver - shifted).at[2:2 + 2 * twos:2].set(receiver + shifted)
    return lengths[jax.random.permutation(jax.random.fold_in(stream_key, 2), count)]


def scatter_about(own_key, extent, spread, most, shards=(), kind=jnp.bfloat16):
    array = spread * jax.random.normal(own_key, extent, jnp.float32)
    if shards:
        array = array * levels(own_key, extent, shards, -0.22, 0.18)
    return jnp.clip(array, -most, most).astype(kind)


def setup_inputs(seed: int = 0) -> dict:
    key_list = jax.random.split(jax.random.key(seed), 5)
    queries = draw_queries(jax.random.fold_in(key_list[4], 71), 0)
    key_rows = draw_key_rows(jax.random.fold_in(key_list[4], 71), 0)
    value_rows = scatter_about(key_list[2], (TOKENS, KVH * HD), 1.0, 6.0, ((0, 64), (1, 8)))
    doc_blocks = ragged_sizes(key_list[3], NDOCS, NB, LONGB, 2).astype(jnp.int32)
    return dict(queries=queries, key_rows=key_rows, value_rows=value_rows, doc_blocks=doc_blocks)


masked_score = -1e+30

def doc_index(positions, doc_ends):
    block_index = jnp.floor_divide(positions, B)
    return lax.optimization_barrier(jnp.sum((block_index[:, None] >= doc_ends[None, :]).astype(jnp.int32), axis=1))

def reference(queries, key_rows, value_rows, doc_blocks):
    doc_ends = jnp.cumsum(doc_blocks).astype(jnp.int32)
    group_size = QH // KVH
    reach_rows = LONGB * B
    score_scale = 1.0 / math.sqrt(HD)
    lead = jnp.zeros((reach_rows - B, KVH * HD), key_rows.dtype)
    padded_keys = jnp.concatenate([lead, key_rows], 0)
    padded_values = jnp.concatenate([lead, value_rows], 0)

    def one_block(block_id):
        row_start = (block_id * B).astype(jnp.int32)
        query_mat = lax.dynamic_slice_in_dim(queries, row_start, B, 0).astype(jnp.float32).reshape(B, KVH, group_size, HD)
        key_mat = lax.dynamic_slice_in_dim(padded_keys, row_start, reach_rows, 0).astype(jnp.float32).reshape(reach_rows, KVH, HD)
        value_mat = lax.dynamic_slice_in_dim(padded_values, row_start, reach_rows, 0).astype(jnp.float32).reshape(reach_rows, KVH, HD)
        query_pos = row_start + jnp.arange(B, dtype=jnp.int32)
        key_pos = row_start - (reach_rows - B) + jnp.arange(reach_rows, dtype=jnp.int32)
        query_doc = doc_index(query_pos, doc_ends)
        key_doc = doc_index(key_pos, doc_ends)
        visible = (key_doc[None, :] == query_doc[:, None]) & (key_pos[None, :] <= query_pos[:, None]) & (key_pos[None, :] >= 0)
        scores = jnp.einsum('qhgd,khd->hgqk', query_mat, key_mat) * score_scale
        scores = jnp.where(visible, scores, masked_score)
        row_max = lax.optimization_barrier(jnp.max(scores, axis=-1))
        weights = jnp.where(visible, jnp.exp(scores - row_max[..., None]), 0.0)
        row_total = lax.optimization_barrier(jnp.sum(weights, axis=-1))
        rounded = weights.astype(jnp.bfloat16).astype(jnp.float32)
        summed = jnp.einsum('hgqk,khd->hgqd', rounded, value_mat)
        result = summed / row_total[..., None]
        return jnp.transpose(result, (2, 0, 1, 3)).reshape(B, QH * HD).astype(jnp.bfloat16)
    blocks = lax.map(one_block, jnp.arange(NB, dtype=jnp.int32))
    return blocks.reshape(TOKENS, QH * HD)
```

```python
import functools
import math

import jax
import jax.numpy as jnp
from jax import lax
from jax.experimental import pallas as pl
from jax.experimental.pallas import tpu as pltpu
from jax.sharding import PartitionSpec as P

HD = 128
B = 128
GROUP = 4
ROWS = 8
PIECES = 4
FAR = 8
CORES = 2
COLS = GROUP * B
EXTRA = 16
LAG = 2

NEG = -1e30
SCALE = math.log2(math.e) / math.sqrt(HD)
MESH = pl.DeviceIdType.MESH


def kernel(
    n_seq,
    n_head,
    q_hbm,
    k_hbm,
    v_hbm,
    doc_hbm,
    out_ref,
    q_in,
    v_in,
    doc_in,
    q_t,
    kv,
    top,
    acc,
    reach,
    out_buf,
    load_sem,
    send_sem,
    recv_sem,
    out_send,
    out_recv,
):
    s = lax.axis_index("seq")
    h = lax.axis_index("head")
    z = lax.rem(s, ROWS)
    chips = n_head // CORES
    x = h // CORES

    def ring(distance):
        return lax.rem(s + distance + n_seq, n_seq)

    after, before = ring(1), ring(-1)
    up, down = ring(ROWS), ring(-ROWS)
    first_col = ring(-(ROWS - 1))
    last_col = ring(ROWS - 1)

    loads = [
        pltpu.make_async_copy(
            k_hbm.at[pl.ds(j * B, B), :], kv.at[0, j, 0], load_sem.at[j]
        )
        for j in range(PIECES)
    ]
    loads.append(pltpu.make_async_copy(v_hbm, v_in, load_sem.at[PIECES]))
    loads.append(pltpu.make_async_copy(doc_hbm, doc_in, load_sem.at[PIECES + 1]))
    loads.append(pltpu.make_async_copy(q_hbm, q_in, load_sem.at[PIECES + 2]))
    for copy in loads:
        copy.start()

    barrier = pltpu.get_barrier_semaphore()

    def greet(to_seq, to_head):
        pl.semaphore_signal(barrier, inc=1, device_id=(to_seq, to_head), device_id_type=MESH)

    for to in (after, before, up, down):
        greet(to, h)
    for step in range(1, n_head):
        greet(s, lax.rem(h + step, n_head))

    @pl.when(z == ROWS - 1)
    def _():
        greet(first_col, h)

    @pl.when(z == 0)
    def _():
        greet(last_col, h)

    for copy in loads[: PIECES + 1]:
        copy.wait()
    for j in range(PIECES):
        kv[0, j, 1] = v_in[pl.ds(j * B, B), :].T

    edge = jnp.where((z == 0) | (z == ROWS - 1), 1, 0)
    pl.semaphore_wait(barrier, 4 + n_head - 1 + edge)

    def move(src, dst, j, to):
        return pltpu.make_async_remote_copy(
            src_ref=kv.at[src, j],
            dst_ref=kv.at[dst, j],
            send_sem=send_sem.at[dst, j],
            recv_sem=recv_sem.at[dst, j],
            device_id=(to, h),
            device_id_type=MESH,
        )

    def send(src, dst, j, to):
        move(src, dst, j, to).start()

    def arrived(d, j):
        move(d, d, j, after).wait_recv()

    def sent(d, j):
        move(d, d, j, after).wait_send()

    for j in range(PIECES):
        send(0, FAR, j, up)

        send(0, 1, j, after)

        @pl.when(z == 0)
        def _():
            send(0, FAR - 1, j, last_col)

    loads[PIECES + 1].wait()
    lengths = doc_in[...]
    count = lengths.shape[1]
    shape = (count, count)
    upto = lax.broadcasted_iota(jnp.int32, shape, 1) <= lax.broadcasted_iota(jnp.int32, shape, 0)
    ends = jnp.sum(
        jnp.where(upto, jnp.broadcast_to(lengths, shape), 0).astype(jnp.float32),
        axis=1,
        keepdims=True,
    ).astype(jnp.int32)
    for i in range(PIECES):
        block = s * PIECES + i
        start = jnp.max(
            jnp.where(ends <= block, ends, 0).astype(jnp.float32), axis=0, keepdims=True
        ).astype(jnp.int32)
        reach[i] = jnp.broadcast_to(block - start, (1, COLS))

    loads[PIECES + 2].wait()
    for i in range(PIECES):
        for g in range(GROUP):
            rows = q_in[i * B : (i + 1) * B, g * HD : (g + 1) * HD]
            scaled = rows.astype(jnp.float32).T * SCALE
            high = scaled.astype(jnp.bfloat16)
            q_t[i, :HD, g * B : (g + 1) * B] = high
            q_t[i, HD:, g * B : (g + 1) * B] = (scaled - high.astype(jnp.float32)).astype(jnp.bfloat16)

    def update(i, chunks, first=False):
        queries = q_t[i]
        far = reach[i]
        scores, shown = [], []
        for d, blocks in chunks:
            n = len(blocks)
            keys = kv[d, blocks[0] : blocks[0] + n, 0].reshape(n * B, HD)
            pair = jnp.dot(
                jnp.concatenate([keys, keys], axis=1), queries, preferred_element_type=jnp.float32
            )
            for b, j in enumerate(blocks):
                block = pair[b * B : (b + 1) * B]
                delta = PIECES * d + i - j
                if first:
                    key = lax.broadcasted_iota(jnp.int32, (B, COLS), 0) + j * B
                    query = lax.rem(lax.broadcasted_iota(jnp.int32, (B, COLS), 1), B) + i * B
                    block = jnp.where(key <= query, block, NEG)
                    shown.append((delta <= far) & (delta >= 0))
                else:
                    shown.append(delta <= far)
                scores.append(block)
        peak = None
        for block, show in zip(scores, shown):
            here = jnp.where(show, jnp.max(block, axis=0, keepdims=True), NEG)
            peak = here if peak is None else jnp.maximum(peak, here)
        if not first:
            old = top[i]
            peak = jnp.maximum(old, peak)
            shrink = jnp.exp2(old - peak)
        top[i] = peak
        added = None
        at = 0
        ones = jnp.ones((EXTRA, B), jnp.bfloat16)
        for d, blocks in chunks:
            n = len(blocks)
            weights = [
                jnp.exp2(block - jnp.where(show, peak, -NEG)).astype(jnp.bfloat16)
                for block, show in zip(scores[at : at + n], shown[at : at + n])
            ]
            at += n
            values = jnp.concatenate(
                [jnp.concatenate([kv[d, j, 1], ones], axis=0) for j in blocks], axis=1
            )
            part = jnp.dot(
                values, jnp.concatenate(weights, axis=0), preferred_element_type=jnp.float32
            )
            added = part if added is None else added + part
        acc[i] = added if first else acc[i] * shrink + added

    every = tuple(range(PIECES))
    half = PIECES // 2

    @pl.loop(0, PIECES)
    def _(j):
        update(j, [(0, every)], first=True)

    far_steps = 4 * PIECES
    work_from = PIECES - 1 + LAG

    @pl.loop(0, 3 * PIECES + work_from)
    def _(t):
        j = lax.rem(t, PIECES)
        d = FAR - t // PIECES

        @pl.when(t < far_steps)
        def _():
            arrived(d, j)

            @pl.when((d > 5) & ((d < FAR) | (z != 0)))
            def _():
                send(d, d - 1, j, before)

        u = t - LAG
        near = u // PIECES + 1
        k = lax.rem(u + PIECES, PIECES)

        @pl.when(u >= 0)
        def _():
            arrived(near, k)

            @pl.when(near < 4)
            def _():
                send(near, near + 1, k, after)

        w = t - work_from

        @pl.when(w >= 0)
        def _():
            p = w // PIECES + 1
            update(lax.rem(w, PIECES), [(p, every), (FAR + 1 - p, every)])

    @pl.loop(0, PIECES)
    def _(j):
        update(j, [(5, every[:half]), (4, every[:half])])

    for u in range(3 * PIECES + work_from - LAG, 4 * PIECES):
        arrived(u // PIECES + 1, u % PIECES)

    own = pltpu.make_async_copy(
        out_buf.at[h],
        out_ref.at[:, pl.ds(pl.multiple_of(h * COLS, COLS), COLS)],
        load_sem.at[0],
    )
    for hop in (2, 1, 3, 0):
        to_x = lax.rem(x + hop, chips)
        i = to_x
        update(i, [(5, every[half:]), (4, every[half:])])
        final = acc[i, :HD] * (1.0 / acc[i, HD : HD + 1])
        for g in range(GROUP):
            rows = final[:, g * B : (g + 1) * B].T.astype(jnp.bfloat16)
            for core in range(CORES):
                part = B // CORES
                out_buf[to_x * CORES + core, :, g * HD : (g + 1) * HD] = rows[
                    core * part : (core + 1) * part
                ]
        for core in range(CORES):
            target = to_x * CORES + core
            step = lax.rem(target - h + n_head, n_head)
            there = pltpu.make_async_remote_copy(
                src_ref=out_buf.at[target],
                dst_ref=out_ref.at[:, pl.ds(pl.multiple_of(h * COLS, COLS), COLS)],
                send_sem=out_send.at[target],
                recv_sem=out_recv.at[h],
                device_id=(s, target),
                device_id_type=MESH,
            )
            if hop == 0:

                @pl.when(step != 0)
                def _():
                    there.start()

                @pl.when(step == 0)
                def _():
                    own.start()

            else:
                there.start()

    @pl.loop(1, FAR + 1)
    def _(d):
        @pl.loop(0, PIECES)
        def _(j):
            sent(d, j)

    for step in range(1, n_head):
        peer = lax.rem(h + step, n_head)
        other = pltpu.make_async_remote_copy(
            src_ref=out_buf.at[peer],
            dst_ref=out_ref.at[:, pl.ds(pl.multiple_of(peer * COLS, COLS), COLS)],
            send_sem=out_send.at[peer],
            recv_sem=out_recv.at[peer],
            device_id=(s, peer),
            device_id_type=MESH,
        )
        other.wait_send()
        other.wait_recv()
    own.wait()


def body(n_seq, n_head, queries, key_rows, value_rows, doc_blocks):
    tokens = queries.shape[0]
    part = tokens // n_head
    any_space = pl.BlockSpec(memory_space=pl.ANY)
    bf16, f32 = jnp.bfloat16, jnp.float32
    pairs = tokens * PIECES * FAR * B * GROUP
    return pl.pallas_call(
        functools.partial(kernel, n_seq, n_head),
        out_shape=jax.ShapeDtypeStruct((part, n_head * COLS), bf16),
        in_specs=[any_space] * 4,
        out_specs=any_space,
        scratch_shapes=[
            pltpu.VMEM((tokens, COLS), bf16),
            pltpu.VMEM((tokens, HD), bf16),
            pltpu.VMEM((1, doc_blocks.shape[0]), jnp.int32),
            pltpu.VMEM((PIECES, 2 * HD, COLS), bf16),
            pltpu.VMEM((FAR + 1, PIECES, 2, B, HD), bf16),
            pltpu.VMEM((PIECES, 1, COLS), f32),
            pltpu.VMEM((PIECES, HD + EXTRA, COLS), f32),
            pltpu.VMEM((PIECES, 1, COLS), jnp.int32),
            pltpu.VMEM((n_head, part, COLS), bf16),
            pltpu.SemaphoreType.DMA((PIECES + 3,)),
            pltpu.SemaphoreType.DMA((FAR + 1, PIECES)),
            pltpu.SemaphoreType.DMA((FAR + 1, PIECES)),
            pltpu.SemaphoreType.DMA((n_head,)),
            pltpu.SemaphoreType.DMA((n_head,)),
        ],
        compiler_params=pltpu.CompilerParams(
            collective_id=0, has_side_effects=True, vmem_limit_bytes=62 << 20
        ),
        cost_estimate=pl.CostEstimate(
            flops=4 * pairs * HD, bytes_accessed=2 << 20, transcendentals=pairs
        ),
        name="attend",
    )(queries, key_rows, value_rows, doc_blocks.reshape(1, -1))


def solution(mesh):
    in_specs = (P("seq", "head"), P("seq", "head"), P("seq", "head"), P())
    out_specs = P(("seq", "head"), None)
    return jax.shard_map(
        functools.partial(body, mesh.shape["seq"], mesh.shape["head"]),
        mesh=mesh,
        in_specs=in_specs,
        out_specs=out_specs,
        check_vma=False,
    )
```

```python
import functools
import math

import jax
import jax.numpy as jnp
from jax import lax
from jax.experimental import pallas as pl
from jax.experimental.pallas import tpu as pltpu
from jax.sharding import PartitionSpec as P

HD = 128
B = 128
GROUP = 4
ROWS = 8
PIECES = 4
FAR = 8
CORES = 2
COLS = GROUP * B
EXTRA = 16
WINDOW = 2
SHARE = 1

NEG = -1e30
SCALE = math.log2(math.e) / math.sqrt(HD)
MESH = pl.DeviceIdType.MESH


def kernel(
    n_seq,
    n_head,
    q_hbm,
    k_hbm,
    v_hbm,
    doc_hbm,
    out_ref,
    q_in,
    v_in,
    doc_in,
    q_t,
    kv,
    top,
    acc,
    reach,
    out_buf,
    relay_buf,
    load_sem,
    send_sem,
    recv_sem,
    out_send,
    out_recv,
    relay_sem,
):
    s = lax.axis_index("seq")
    h = lax.axis_index("head")
    z = lax.rem(s, ROWS)
    chips = n_head // CORES
    x = h // CORES

    def ring(distance):
        return lax.rem(s + distance + n_seq, n_seq)

    after, before = ring(1), ring(-1)
    up, down = ring(ROWS), ring(-ROWS)
    ahead, behind = ring(ROWS - 1), ring(1 - ROWS)

    loads = [
        pltpu.make_async_copy(
            k_hbm.at[pl.ds(j * B, B), :], kv.at[0, j, 0], load_sem.at[j]
        )
        for j in range(PIECES)
    ]
    loads.append(pltpu.make_async_copy(v_hbm, v_in, load_sem.at[PIECES]))
    loads.append(pltpu.make_async_copy(doc_hbm, doc_in, load_sem.at[PIECES + 1]))
    loads.append(pltpu.make_async_copy(q_hbm, q_in, load_sem.at[PIECES + 2]))
    for copy in loads:
        copy.start()

    barrier = pltpu.get_barrier_semaphore()

    def greet(to_seq, to_head):
        pl.semaphore_signal(barrier, inc=1, device_id=(to_seq, to_head), device_id_type=MESH)

    for to in (after, before, up, down, ahead, behind):
        greet(to, h)
    for step in range(1, n_head):
        greet(s, lax.rem(h + step, n_head))

    for copy in loads[: PIECES + 1]:
        copy.wait()
    for j in range(PIECES):
        kv[0, j, 1] = v_in[pl.ds(j * B, B), :].T

    pl.semaphore_wait(barrier, 6 + n_head - 1)

    def move(src, dst, j, to):
        return pltpu.make_async_remote_copy(
            src_ref=kv.at[src, j],
            dst_ref=kv.at[dst, j],
            send_sem=send_sem.at[dst, j],
            recv_sem=recv_sem.at[dst, j],
            device_id=(to, h),
            device_id_type=MESH,
        )

    def send(src, dst, j, to):
        move(src, dst, j, to).start()

    def arrived(d, j):
        move(d, d, j, after).wait_recv()

    def sent(d, j):
        move(d, d, j, after).wait_send()

    whole = 3 * PIECES
    n_forward = whole + SHARE
    n_backward = whole + PIECES - SHARE

    def forward(n):
        return 1 + n // PIECES, lax.rem(n, PIECES)

    def backward(n):
        return FAR - 1 - n // PIECES, lax.rem(n, PIECES) + jnp.where(n >= whole, SHARE, 0)

    for j in range(WINDOW):
        send(0, 1, j, after)
        send(0, FAR - 1, j, ahead)

    loads[PIECES + 1].wait()
    lengths = doc_in[...]
    count = lengths.shape[1]
    shape = (count, count)
    upto = lax.broadcasted_iota(jnp.int32, shape, 1) <= lax.broadcasted_iota(jnp.int32, shape, 0)
    ends = jnp.sum(
        jnp.where(upto, jnp.broadcast_to(lengths, shape), 0).astype(jnp.float32),
        axis=1,
        keepdims=True,
    ).astype(jnp.int32)
    for i in range(PIECES):
        block = s * PIECES + i
        start = jnp.max(
            jnp.where(ends <= block, ends, 0).astype(jnp.float32), axis=0, keepdims=True
        ).astype(jnp.int32)
        reach[i] = jnp.broadcast_to(block - start, (1, COLS))

    loads[PIECES + 2].wait()
    for i in range(PIECES):
        for g in range(GROUP):
            rows = q_in[i * B : (i + 1) * B, g * HD : (g + 1) * HD]
            scaled = rows.astype(jnp.float32).T * SCALE
            high = scaled.astype(jnp.bfloat16)
            q_t[i, :HD, g * B : (g + 1) * B] = high
            q_t[i, HD:, g * B : (g + 1) * B] = (scaled - high.astype(jnp.float32)).astype(jnp.bfloat16)

    def update(i, chunks, first=False):
        queries = q_t[i]
        far = reach[i]
        scores, shown = [], []
        for d, blocks in chunks:
            n = len(blocks)
            keys = kv[d, blocks[0] : blocks[0] + n, 0].reshape(n * B, HD)
            pair = jnp.dot(
                jnp.concatenate([keys, keys], axis=1), queries, preferred_element_type=jnp.float32
            )
            for b, j in enumerate(blocks):
                block = pair[b * B : (b + 1) * B]
                delta = PIECES * d + i - j
                if first:
                    key = lax.broadcasted_iota(jnp.int32, (B, COLS), 0) + j * B
                    query = lax.rem(lax.broadcasted_iota(jnp.int32, (B, COLS), 1), B) + i * B
                    block = jnp.where(key <= query, block, NEG)
                    shown.append((delta <= far) & (delta >= 0))
                else:
                    shown.append(delta <= far)
                scores.append(block)
        peak = None
        for block, show in zip(scores, shown):
            here = jnp.where(show, jnp.max(block, axis=0, keepdims=True), NEG)
            peak = here if peak is None else jnp.maximum(peak, here)
        if not first:
            old = top[i]
            peak = jnp.maximum(old, peak)
            shrink = jnp.exp2(old - peak)
        top[i] = peak
        added = None
        at = 0
        ones = jnp.ones((EXTRA, B), jnp.bfloat16)
        for d, blocks in chunks:
            n = len(blocks)
            weights = [
                jnp.exp2(block - jnp.where(show, peak, -NEG)).astype(jnp.bfloat16)
                for block, show in zip(scores[at : at + n], shown[at : at + n])
            ]
            at += n
            values = jnp.concatenate(
                [jnp.concatenate([kv[d, j, 1], ones], axis=0) for j in blocks], axis=1
            )
            part = jnp.dot(
                values, jnp.concatenate(weights, axis=0), preferred_element_type=jnp.float32
            )
            added = part if added is None else added + part
        acc[i] = added if first else acc[i] * shrink + added

    every = tuple(range(PIECES))

    late = PIECES - WINDOW
    turn = whole - WINDOW
    first_pair = PIECES + late - 1
    steps = first_pair + whole
    leaf = first_pair
    leaf_work = leaf + PIECES + 1

    @pl.loop(0, steps)
    def _(t):
        n = t + WINDOW

        @pl.when(t < n_forward)
        def _():
            sent(*forward(t))

        @pl.when((t >= late) & (t - late < n_forward))
        def _():
            arrived(*forward(t - late))

        @pl.when(n < PIECES)
        def _():
            send(0, 1, n, after)

        @pl.when((n >= PIECES) & (n < n_forward))
        def _():
            d, j = forward(n)
            send(d - 1, d, j, after)

        @pl.when(t < n_backward)
        def _():
            sent(*backward(t))

        @pl.when((t >= late) & (t <= turn))
        def _():
            arrived(*backward(t - late))

        for k in range(SHARE):

            @pl.when((t == turn) if k + 1 < SHARE else ((t >= turn) & (t < n_backward)))
            def _():
                arrived(*backward(t - late + 1 + k))

        @pl.when(n < PIECES)
        def _():
            send(0, FAR - 1, n, ahead)

        @pl.when((n >= PIECES) & (n < n_backward))
        def _():
            d, j = backward(n)
            send(d + 1, d, j, before)

        @pl.when((t > leaf) & (t < leaf + PIECES - 1))
        def _():
            sent(FAR, t - leaf)

        @pl.when((t >= leaf) & (t < leaf + PIECES - 1))
        def _():
            send(0, FAR, t - leaf + 1, up)

        @pl.when(t < PIECES)
        def _():
            update(t, [(0, every)], first=True)

        @pl.when(t >= first_pair)
        def _():
            m = 1 + (t - first_pair) // PIECES
            update(lax.rem(t - first_pair, PIECES), [(FAR - m, every), (m, every)])

        @pl.when(t == leaf_work)
        def _():
            for j in range(1, PIECES):
                arrived(FAR, j)

        @pl.when((t >= leaf_work) & (t < leaf_work + PIECES))
        def _():
            update(t - leaf_work, [(FAR, every[1:])])

    sent(FAR, PIECES - 1)

    for n in range(n_backward - late + SHARE, n_backward):
        arrived(*backward(n))

    def columns(who):
        return pl.ds(pl.multiple_of(who * COLS, COLS), COLS)

    own = pltpu.make_async_copy(out_buf.at[h], out_ref.at[:, columns(h)], load_sem.at[0])
    core_here = lax.rem(h, CORES)

    def chip(hop):
        return lax.rem(x + hop, chips)

    def deliver(src, whose, target, send_at):
        return pltpu.make_async_remote_copy(
            src_ref=src,
            dst_ref=out_ref.at[:, columns(whose)],
            send_sem=send_at,
            recv_sem=out_recv.at[whose],
            device_id=(s, target),
            device_id_type=MESH,
        )

    relay_in = pltpu.make_async_remote_copy(
        src_ref=out_buf.at[chip(2) * CORES + 1],
        dst_ref=relay_buf,
        send_sem=out_send.at[chip(2) * CORES + 1],
        recv_sem=relay_sem.at[0],
        device_id=(s, chip(chips - 1) * CORES + core_here),
        device_id_type=MESH,
    )
    relay_out = deliver(
        relay_buf, chip(1) * CORES + core_here, chip(chips - 1) * CORES + 1, relay_sem.at[1]
    )

    for hop in (2, 3, 1, 0):
        i = chip(hop)
        update(i, [(4, every)])
        final = acc[i, :HD] * (1.0 / acc[i, HD : HD + 1])
        for g in range(GROUP):
            rows = final[:, g * B : (g + 1) * B].T.astype(jnp.bfloat16)
            for core in range(CORES):
                part = B // CORES
                out_buf[i * CORES + core, :, g * HD : (g + 1) * HD] = rows[
                    core * part : (core + 1) * part
                ]
        for core in range(CORES):
            target = i * CORES + core
            there = deliver(out_buf.at[target], h, target, out_send.at[target])
            if hop == 2 and core == 1:
                relay_in.start()
            elif hop:
                there.start()
            else:

                @pl.when(core_here != core)
                def _():
                    there.start()

                @pl.when(core_here == core)
                def _():
                    own.start()

    relay_in.wait_recv()
    relay_out.start()

    for step in range(1, n_head):
        peer = lax.rem(h + step, n_head)
        other = deliver(out_buf.at[peer], peer, peer, out_send.at[peer])
        other.wait_send()
        other.wait_recv()
    relay_out.wait_send()
    own.wait()


def body(n_seq, n_head, queries, key_rows, value_rows, doc_blocks):
    tokens = queries.shape[0]
    part = tokens // n_head
    in_hbm = pl.BlockSpec(memory_space=pltpu.HBM)
    bf16, f32 = jnp.bfloat16, jnp.float32
    pairs = tokens * PIECES * FAR * B * GROUP
    return pl.pallas_call(
        functools.partial(kernel, n_seq, n_head),
        out_shape=jax.ShapeDtypeStruct((part, n_head * COLS), bf16),
        in_specs=[in_hbm] * 4,
        out_specs=pl.BlockSpec(memory_space=pl.ANY),
        scratch_shapes=[
            pltpu.VMEM((tokens, COLS), bf16),
            pltpu.VMEM((tokens, HD), bf16),
            pltpu.VMEM((1, doc_blocks.shape[0]), jnp.int32),
            pltpu.VMEM((PIECES, 2 * HD, COLS), bf16),
            pltpu.VMEM((FAR + 1, PIECES, 2, B, HD), bf16),
            pltpu.VMEM((PIECES, 1, COLS), f32),
            pltpu.VMEM((PIECES, HD + EXTRA, COLS), f32),
            pltpu.VMEM((PIECES, 1, COLS), jnp.int32),
            pltpu.VMEM((n_head, part, COLS), bf16),
            pltpu.VMEM((part, COLS), bf16),
            pltpu.SemaphoreType.DMA((PIECES + 3,)),
            pltpu.SemaphoreType.DMA((FAR + 1, PIECES)),
            pltpu.SemaphoreType.DMA((FAR + 1, PIECES)),
            pltpu.SemaphoreType.DMA((n_head,)),
            pltpu.SemaphoreType.DMA((n_head,)),
            pltpu.SemaphoreType.DMA((2,)),
        ],
        compiler_params=pltpu.CompilerParams(
            collective_id=0, has_side_effects=True, vmem_limit_bytes=62 << 20
        ),
        cost_estimate=pl.CostEstimate(
            flops=4 * pairs * HD, bytes_accessed=2 << 20, transcendentals=pairs
        ),
        name="attend",
    )(queries, key_rows, value_rows, doc_blocks.reshape(1, -1))


def solution(mesh):
    in_specs = (P("seq", "head"), P("seq", "head"), P("seq", "head"), P())
    out_specs = P(("seq", "head"), None)
    return jax.shard_map(
        functools.partial(body, mesh.shape["seq"], mesh.shape["head"]),
        mesh=mesh,
        in_specs=in_specs,
        out_specs=out_specs,
        check_vma=False,
    )
```

```python
import functools
import math

import jax
import jax.numpy as jnp
from jax import lax
from jax.experimental import pallas as pl
from jax.experimental.pallas import tpu as pltpu
from jax.sharding import PartitionSpec as P

HD = 128
B = 128
GROUP = 4
ROWS = 8
PIECES = 4
FAR = 8
CORES = 2
COLS = GROUP * B
EXTRA = 16
WINDOW = 2

NEG = -1e30
SCALE = math.log2(math.e) / math.sqrt(HD)
MESH = pl.DeviceIdType.MESH


def kernel(
    n_seq,
    n_head,
    q_hbm,
    k_hbm,
    v_hbm,
    doc_hbm,
    out_ref,
    q_in,
    v_in,
    doc_in,
    q_t,
    kv,
    top,
    acc,
    reach,
    out_buf,
    relay_buf,
    load_sem,
    send_sem,
    recv_sem,
    out_send,
    out_recv,
    relay_sem,
):
    s = lax.axis_index("seq")
    h = lax.axis_index("head")
    z = lax.rem(s, ROWS)
    chips = n_head // CORES
    x = h // CORES

    def ring(distance):
        return lax.rem(s + distance + n_seq, n_seq)

    after, before = ring(1), ring(-1)
    up, down = ring(ROWS), ring(-ROWS)
    ahead, behind = ring(ROWS - 1), ring(1 - ROWS)

    loads = [
        pltpu.make_async_copy(
            k_hbm.at[pl.ds(j * B, B), :], kv.at[0, j, 0], load_sem.at[j]
        )
        for j in range(PIECES)
    ]
    loads.append(pltpu.make_async_copy(v_hbm, v_in, load_sem.at[PIECES]))
    loads.append(pltpu.make_async_copy(doc_hbm, doc_in, load_sem.at[PIECES + 1]))
    loads.append(pltpu.make_async_copy(q_hbm, q_in, load_sem.at[PIECES + 2]))
    for copy in loads:
        copy.start()

    barrier = pltpu.get_barrier_semaphore()

    def greet(to_seq, to_head):
        pl.semaphore_signal(barrier, inc=1, device_id=(to_seq, to_head), device_id_type=MESH)

    for to in (after, before, up, down, ahead, behind):
        greet(to, h)
    for step in range(1, n_head):
        greet(s, lax.rem(h + step, n_head))

    for copy in loads[: PIECES + 1]:
        copy.wait()
    for j in range(PIECES):
        kv[0, j, 1] = v_in[pl.ds(j * B, B), :].T

    pl.semaphore_wait(barrier, 6 + n_head - 1)

    def move(src, dst, j, to):
        return pltpu.make_async_remote_copy(
            src_ref=kv.at[src, j],
            dst_ref=kv.at[dst, j],
            send_sem=send_sem.at[dst, j],
            recv_sem=recv_sem.at[dst, j],
            device_id=(to, h),
            device_id_type=MESH,
        )

    def send(src, dst, j, to):
        move(src, dst, j, to).start()

    def arrived(d, j):
        move(d, d, j, after).wait_recv()

    def sent(d, j):
        move(d, d, j, after).wait_send()

    whole = 3 * PIECES
    longest = 4 * PIECES
    forward_end = jnp.where(z == ROWS - 2, longest, whole)
    backward_end = jnp.where(z == 0, whole, longest)

    def forward(n):
        return 1 + n // PIECES, lax.rem(n, PIECES)

    def backward(n):
        return FAR - 1 - n // PIECES, lax.rem(n, PIECES)

    for j in range(WINDOW):
        send(0, 1, j, after)
        send(0, FAR - 1, j, ahead)

    loads[PIECES + 1].wait()
    lengths = doc_in[...]
    count = lengths.shape[1]
    shape = (count, count)
    upto = lax.broadcasted_iota(jnp.int32, shape, 1) <= lax.broadcasted_iota(jnp.int32, shape, 0)
    ends = jnp.sum(
        jnp.where(upto, jnp.broadcast_to(lengths, shape), 0).astype(jnp.float32),
        axis=1,
        keepdims=True,
    ).astype(jnp.int32)
    for i in range(PIECES):
        block = s * PIECES + i
        start = jnp.max(
            jnp.where(ends <= block, ends, 0).astype(jnp.float32), axis=0, keepdims=True
        ).astype(jnp.int32)
        reach[i] = jnp.broadcast_to(block - start, (1, COLS))

    loads[PIECES + 2].wait()
    for i in range(PIECES):
        for g in range(GROUP):
            rows = q_in[i * B : (i + 1) * B, g * HD : (g + 1) * HD]
            scaled = rows.astype(jnp.float32).T * SCALE
            high = scaled.astype(jnp.bfloat16)
            q_t[i, :HD, g * B : (g + 1) * B] = high
            q_t[i, HD:, g * B : (g + 1) * B] = (scaled - high.astype(jnp.float32)).astype(jnp.bfloat16)

    def update(i, chunks, first=False):
        queries = q_t[i]
        far = reach[i]
        scores, shown = [], []
        for d, blocks in chunks:
            n = len(blocks)
            keys = kv[d, blocks[0] : blocks[0] + n, 0].reshape(n * B, HD)
            pair = jnp.dot(
                jnp.concatenate([keys, keys], axis=1), queries, preferred_element_type=jnp.float32
            )
            for b, j in enumerate(blocks):
                block = pair[b * B : (b + 1) * B]
                delta = PIECES * d + i - j
                if first:
                    key = lax.broadcasted_iota(jnp.int32, (B, COLS), 0) + j * B
                    query = lax.rem(lax.broadcasted_iota(jnp.int32, (B, COLS), 1), B) + i * B
                    block = jnp.where(key <= query, block, NEG)
                    shown.append((delta <= far) & (delta >= 0))
                else:
                    shown.append(delta <= far)
                scores.append(block)
        peak = None
        for block, show in zip(scores, shown):
            here = jnp.where(show, jnp.max(block, axis=0, keepdims=True), NEG)
            peak = here if peak is None else jnp.maximum(peak, here)
        if not first:
            old = top[i]
            peak = jnp.maximum(old, peak)
            shrink = jnp.exp2(old - peak)
        top[i] = peak
        added = None
        at = 0
        ones = jnp.ones((EXTRA, B), jnp.bfloat16)
        for d, blocks in chunks:
            n = len(blocks)
            weights = [
                jnp.exp2(block - jnp.where(show, peak, -NEG)).astype(jnp.bfloat16)
                for block, show in zip(scores[at : at + n], shown[at : at + n])
            ]
            at += n
            values = jnp.concatenate(
                [jnp.concatenate([kv[d, j, 1], ones], axis=0) for j in blocks], axis=1
            )
            part = jnp.dot(
                values, jnp.concatenate(weights, axis=0), preferred_element_type=jnp.float32
            )
            added = part if added is None else added + part
        acc[i] = added if first else acc[i] * shrink + added

    every = tuple(range(PIECES))

    late = PIECES - WINDOW
    first_pair = PIECES + late - 1
    steps = first_pair + whole
    leaf_work = steps - PIECES
    leaf = leaf_work - PIECES - 1

    @pl.loop(0, steps)
    def _(t):
        n = t + WINDOW
        here = t - late

        @pl.when(t < forward_end)
        def _():
            sent(*forward(t))

        @pl.when((here >= 0) & (here < whole))
        def _():
            arrived(*forward(here))

        @pl.when(n < PIECES)
        def _():
            send(0, 1, n, after)

        @pl.when((n >= PIECES) & (n < forward_end))
        def _():
            d, j = forward(n)
            send(d - 1, d, j, after)

        @pl.when(t < backward_end)
        def _():
            sent(*backward(t))

        @pl.when((here >= 0) & (here < whole))
        def _():
            arrived(*backward(here))

        @pl.when(n < PIECES)
        def _():
            send(0, FAR - 1, n, ahead)

        @pl.when((n >= PIECES) & (n < backward_end))
        def _():
            d, j = backward(n)
            send(d + 1, d, j, before)

        @pl.when((t > leaf) & (t < leaf + PIECES - 1))
        def _():
            sent(FAR, t - leaf)

        @pl.when((t >= leaf) & (t < leaf + PIECES - 1))
        def _():
            send(0, FAR, t - leaf + 1, up)

        @pl.when(t < PIECES)
        def _():
            update(t, [(0, every)], first=True)

        @pl.when(t >= first_pair)
        def _():
            m = 1 + (t - first_pair) // PIECES
            update(lax.rem(t - first_pair, PIECES), [(FAR - m, every), (m, every)])

        @pl.when(t == leaf_work)
        def _():
            for j in range(1, PIECES):
                arrived(FAR, j)

        @pl.when(t >= leaf_work)
        def _():
            update(t - leaf_work, [(FAR, every[1:])])

    sent(FAR, PIECES - 1)
    for j in every:
        arrived(4, j)

    def columns(who):
        return pl.ds(pl.multiple_of(who * COLS, COLS), COLS)

    own = pltpu.make_async_copy(out_buf.at[h], out_ref.at[:, columns(h)], load_sem.at[0])
    core_here = lax.rem(h, CORES)

    def chip(hop):
        return lax.rem(x + hop, chips)

    def deliver(src, whose, target, send_at):
        return pltpu.make_async_remote_copy(
            src_ref=src,
            dst_ref=out_ref.at[:, columns(whose)],
            send_sem=send_at,
            recv_sem=out_recv.at[whose],
            device_id=(s, target),
            device_id_type=MESH,
        )

    relay_in = pltpu.make_async_remote_copy(
        src_ref=out_buf.at[chip(2) * CORES + 1],
        dst_ref=relay_buf,
        send_sem=out_send.at[chip(2) * CORES + 1],
        recv_sem=relay_sem.at[0],
        device_id=(s, chip(1) * CORES + core_here),
        device_id_type=MESH,
    )
    relay_out = deliver(
        relay_buf, chip(chips - 1) * CORES + core_here, chip(1) * CORES + 1, relay_sem.at[1]
    )

    for hop in (2, 1, 3, 0):
        i = chip(hop)
        update(i, [(4, every)])
        final = acc[i, :HD] * (1.0 / acc[i, HD : HD + 1])
        for g in range(GROUP):
            rows = final[:, g * B : (g + 1) * B].T.astype(jnp.bfloat16)
            for core in range(CORES):
                part = B // CORES
                out_buf[i * CORES + core, :, g * HD : (g + 1) * HD] = rows[
                    core * part : (core + 1) * part
                ]
        for core in range(CORES):
            target = i * CORES + core
            there = deliver(out_buf.at[target], h, target, out_send.at[target])
            if hop == 2 and core == 1:
                relay_in.start()
            elif hop:
                there.start()
            else:

                @pl.when(core_here != core)
                def _():
                    there.start()

                @pl.when(core_here == core)
                def _():
                    own.start()

    relay_in.wait_recv()
    relay_out.start()

    for step in range(1, n_head):
        peer = lax.rem(h + step, n_head)
        other = deliver(out_buf.at[peer], peer, peer, out_send.at[peer])
        other.wait_send()
        other.wait_recv()
    relay_out.wait_send()
    own.wait()


def body(n_seq, n_head, queries, key_rows, value_rows, doc_blocks):
    tokens = queries.shape[0]
    part = tokens // n_head
    in_hbm = pl.BlockSpec(memory_space=pltpu.HBM)
    bf16, f32 = jnp.bfloat16, jnp.float32
    pairs = tokens * PIECES * FAR * B * GROUP
    return pl.pallas_call(
        functools.partial(kernel, n_seq, n_head),
        out_shape=jax.ShapeDtypeStruct((part, n_head * COLS), bf16),
        in_specs=[in_hbm] * 4,
        out_specs=pl.BlockSpec(memory_space=pl.ANY),
        scratch_shapes=[
            pltpu.VMEM((tokens, COLS), bf16),
            pltpu.VMEM((tokens, HD), bf16),
            pltpu.VMEM((1, doc_blocks.shape[0]), jnp.int32),
            pltpu.VMEM((PIECES, 2 * HD, COLS), bf16),
            pltpu.VMEM((FAR + 1, PIECES, 2, B, HD), bf16),
            pltpu.VMEM((PIECES, 1, COLS), f32),
            pltpu.VMEM((PIECES, HD + EXTRA, COLS), f32),
            pltpu.VMEM((PIECES, 1, COLS), jnp.int32),
            pltpu.VMEM((n_head, part, COLS), bf16),
            pltpu.VMEM((part, COLS), bf16),
            pltpu.SemaphoreType.DMA((PIECES + 3,)),
            pltpu.SemaphoreType.DMA((FAR + 1, PIECES)),
            pltpu.SemaphoreType.DMA((FAR + 1, PIECES)),
            pltpu.SemaphoreType.DMA((n_head,)),
            pltpu.SemaphoreType.DMA((n_head,)),
            pltpu.SemaphoreType.DMA((2,)),
        ],
        compiler_params=pltpu.CompilerParams(
            collective_id=0, has_side_effects=True, vmem_limit_bytes=62 << 20
        ),
        cost_estimate=pl.CostEstimate(
            flops=4 * pairs * HD, bytes_accessed=2 << 20, transcendentals=pairs
        ),
        name="attend",
    )(queries, key_rows, value_rows, doc_blocks.reshape(1, -1))


def solution(mesh):
    in_specs = (P("seq", "head"), P("seq", "head"), P("seq", "head"), P())
    out_specs = P(("seq", "head"), None)
    return jax.shard_map(
        functools.partial(body, mesh.shape["seq"], mesh.shape["head"]),
        mesh=mesh,
        in_specs=in_specs,
        out_specs=out_specs,
        check_vma=False,
    )
```

```python
import functools
import math

import jax
import jax.numpy as jnp
from jax import lax
from jax.experimental import pallas as pl
from jax.experimental.pallas import tpu as pltpu
from jax.sharding import PartitionSpec as P

HD = 128
B = 128
GROUP = 4
ROWS = 8
PIECES = 4
FAR = 8
CORES = 2
COLS = GROUP * B
EXTRA = 16
HALF = COLS // 2
LAG = 2

NEG = -1e30
SCALE = math.log2(math.e) / math.sqrt(HD)
MESH = pl.DeviceIdType.MESH


def kernel(
    n_seq,
    n_head,
    q_hbm,
    k_hbm,
    v_hbm,
    doc_hbm,
    out_ref,
    q_in,
    v_in,
    doc_in,
    q_t,
    kv,
    top,
    acc,
    reach,
    out_buf,
    load_sem,
    send_sem,
    recv_sem,
    out_send,
    out_recv,
):
    s = lax.axis_index("seq")
    h = lax.axis_index("head")
    z = lax.rem(s, ROWS)
    chips = n_head // CORES
    x = h // CORES

    def ring(distance):
        return lax.rem(s + distance + n_seq, n_seq)

    after, before = ring(1), ring(-1)
    up, down = ring(ROWS), ring(-ROWS)
    first_col = ring(-(ROWS - 1))
    last_col = ring(ROWS - 1)

    loads = [
        pltpu.make_async_copy(
            k_hbm.at[pl.ds(j * B, B), :], kv.at[0, j, 0], load_sem.at[j]
        )
        for j in range(PIECES)
    ]
    loads.append(pltpu.make_async_copy(v_hbm, v_in, load_sem.at[PIECES]))
    loads.append(pltpu.make_async_copy(doc_hbm, doc_in, load_sem.at[PIECES + 1]))
    loads.append(pltpu.make_async_copy(q_hbm, q_in, load_sem.at[PIECES + 2]))
    for copy in loads:
        copy.start()

    barrier = pltpu.get_barrier_semaphore()

    def greet(to_seq, to_head):
        pl.semaphore_signal(barrier, inc=1, device_id=(to_seq, to_head), device_id_type=MESH)

    for to in (after, before, up, down):
        greet(to, h)
    for step in range(1, n_head):
        greet(s, lax.rem(h + step, n_head))

    @pl.when(z == ROWS - 1)
    def _():
        greet(first_col, h)

    @pl.when(z == 0)
    def _():
        greet(last_col, h)

    for copy in loads[: PIECES + 1]:
        copy.wait()
    for j in range(PIECES):
        kv[0, j, 1] = v_in[pl.ds(j * B, B), :].T

    edge = jnp.where((z == 0) | (z == ROWS - 1), 1, 0)
    pl.semaphore_wait(barrier, 4 + n_head - 1 + edge)

    def move(src, dst, j, to):
        return pltpu.make_async_remote_copy(
            src_ref=kv.at[src, j],
            dst_ref=kv.at[dst, j],
            send_sem=send_sem.at[dst, j],
            recv_sem=recv_sem.at[dst, j],
            device_id=(to, h),
            device_id_type=MESH,
        )

    def send(src, dst, j, to):
        move(src, dst, j, to).start()

    def arrived(d, j):
        move(d, d, j, after).wait_recv()

    def sent(d, j):
        move(d, d, j, after).wait_send()

    for j in range(PIECES):
        send(0, FAR, j, up)

        send(0, 1, j, after)

        @pl.when(z == 0)
        def _():
            send(0, FAR - 1, j, last_col)

    loads[PIECES + 1].wait()
    lengths = doc_in[...]
    count = lengths.shape[1]
    shape = (count, count)
    upto = lax.broadcasted_iota(jnp.int32, shape, 1) <= lax.broadcasted_iota(jnp.int32, shape, 0)
    ends = jnp.sum(
        jnp.where(upto, jnp.broadcast_to(lengths, shape), 0).astype(jnp.float32),
        axis=1,
        keepdims=True,
    ).astype(jnp.int32)
    for i in range(PIECES):
        block = s * PIECES + i
        start = jnp.max(
            jnp.where(ends <= block, ends, 0).astype(jnp.float32), axis=0, keepdims=True
        ).astype(jnp.int32)
        reach[i] = jnp.broadcast_to(block - start, (1, COLS))

    loads[PIECES + 2].wait()
    for i in range(PIECES):
        for g in range(GROUP):
            rows = q_in[i * B : (i + 1) * B, g * HD : (g + 1) * HD]
            scaled = rows.astype(jnp.float32).T * SCALE
            high = scaled.astype(jnp.bfloat16)
            q_t[i, :HD, g * B : (g + 1) * B] = high
            q_t[i, HD:, g * B : (g + 1) * B] = (scaled - high.astype(jnp.float32)).astype(jnp.bfloat16)

    def update(i, chunks, first=False):
        far = reach[i][:, :HALF]
        ones = jnp.ones((EXTRA, B), jnp.bfloat16)
        keys, values, pairs = [], [], []
        for d, blocks in chunks:
            n = len(blocks)
            part = kv[d, blocks[0] : blocks[0] + n, 0].reshape(n * B, HD)
            keys.append(jnp.concatenate([part, part], axis=1))
            values.append(
                jnp.concatenate(
                    [jnp.concatenate([kv[d, j, 1], ones], axis=0) for j in blocks], axis=1
                )
            )
            pairs += [(d, j) for j in blocks]
        keys = jnp.concatenate(keys, axis=0)
        values = jnp.concatenate(values, axis=1)
        halves = [slice(c * HALF, (c + 1) * HALF) for c in range(COLS // HALF)]
        products = [
            jnp.dot(keys, q_t[i, :, half], preferred_element_type=jnp.float32) for half in halves
        ]
        for half, product in zip(halves, products):
            scores, shown = [], []
            for b, (d, j) in enumerate(pairs):
                block = product[b * B : (b + 1) * B]
                delta = PIECES * d + i - j
                show = delta <= far
                if first:
                    key = lax.broadcasted_iota(jnp.int32, (B, HALF), 0) + j * B
                    query = lax.rem(lax.broadcasted_iota(jnp.int32, (B, HALF), 1), B) + i * B
                    block = jnp.where(key <= query, block, NEG)
                    show = show & (delta >= 0)
                shown.append(show)
                scores.append(block)
            peak = None
            for block, show in zip(scores, shown):
                here = jnp.where(show, jnp.max(block, axis=0, keepdims=True), NEG)
                peak = here if peak is None else jnp.maximum(peak, here)
            if not first:
                old = top[i, :, half]
                peak = jnp.maximum(old, peak)
                shrink = jnp.exp2(old - peak)
            top[i, :, half] = peak
            weights = [
                jnp.exp2(block - jnp.where(show, peak, -NEG)).astype(jnp.bfloat16)
                for block, show in zip(scores, shown)
            ]
            added = jnp.dot(
                values, jnp.concatenate(weights, axis=0), preferred_element_type=jnp.float32
            )
            acc[i, :, half] = added if first else acc[i, :, half] * shrink + added

    every = tuple(range(PIECES))
    half = PIECES // 2

    @pl.loop(0, PIECES)
    def _(j):
        update(j, [(0, every)], first=True)

    far_steps = 4 * PIECES
    work_from = PIECES - 1 + LAG

    @pl.loop(0, 3 * PIECES + work_from)
    def _(t):
        j = lax.rem(t, PIECES)
        d = FAR - t // PIECES

        @pl.when(t < far_steps)
        def _():
            arrived(d, j)

            @pl.when((d > 5) & ((d < FAR) | (z != 0)))
            def _():
                send(d, d - 1, j, before)

        u = t - LAG
        near = u // PIECES + 1
        k = lax.rem(u + PIECES, PIECES)

        @pl.when(u >= 0)
        def _():
            arrived(near, k)

            @pl.when(near < 4)
            def _():
                send(near, near + 1, k, after)

        w = t - work_from

        @pl.when(w >= 0)
        def _():
            p = w // PIECES + 1
            update(lax.rem(w, PIECES), [(p, every), (FAR + 1 - p, every)])

    @pl.loop(0, PIECES)
    def _(j):
        update(j, [(5, every[:half]), (4, every[:half])])

    for u in range(3 * PIECES + work_from - LAG, 4 * PIECES):
        arrived(u // PIECES + 1, u % PIECES)

    own = pltpu.make_async_copy(
        out_buf.at[h],
        out_ref.at[:, pl.ds(pl.multiple_of(h * COLS, COLS), COLS)],
        load_sem.at[0],
    )
    for hop in (2, 1, 3, 0):
        to_x = lax.rem(x + hop, chips)
        i = to_x
        update(i, [(5, every[half:]), (4, every[half:])])
        final = acc[i, :HD] * (1.0 / acc[i, HD : HD + 1])
        for g in range(GROUP):
            rows = final[:, g * B : (g + 1) * B].T.astype(jnp.bfloat16)
            for core in range(CORES):
                part = B // CORES
                out_buf[to_x * CORES + core, :, g * HD : (g + 1) * HD] = rows[
                    core * part : (core + 1) * part
                ]
        for core in range(CORES):
            target = to_x * CORES + core
            step = lax.rem(target - h + n_head, n_head)
            there = pltpu.make_async_remote_copy(
                src_ref=out_buf.at[target],
                dst_ref=out_ref.at[:, pl.ds(pl.multiple_of(h * COLS, COLS), COLS)],
                send_sem=out_send.at[target],
                recv_sem=out_recv.at[h],
                device_id=(s, target),
                device_id_type=MESH,
            )
            if hop == 0:

                @pl.when(step != 0)
                def _():
                    there.start()

                @pl.when(step == 0)
                def _():
                    own.start()

            else:
                there.start()

    @pl.loop(1, FAR + 1)
    def _(d):
        @pl.loop(0, PIECES)
        def _(j):
            sent(d, j)

    for step in range(1, n_head):
        peer = lax.rem(h + step, n_head)
        other = pltpu.make_async_remote_copy(
            src_ref=out_buf.at[peer],
            dst_ref=out_ref.at[:, pl.ds(pl.multiple_of(peer * COLS, COLS), COLS)],
            send_sem=out_send.at[peer],
            recv_sem=out_recv.at[peer],
            device_id=(s, peer),
            device_id_type=MESH,
        )
        other.wait_send()
        other.wait_recv()
    own.wait()


def body(n_seq, n_head, queries, key_rows, value_rows, doc_blocks):
    tokens = queries.shape[0]
    part = tokens // n_head
    any_space = pl.BlockSpec(memory_space=pl.ANY)
    bf16, f32 = jnp.bfloat16, jnp.float32
    pairs = tokens * PIECES * FAR * B * GROUP
    return pl.pallas_call(
        functools.partial(kernel, n_seq, n_head),
        out_shape=jax.ShapeDtypeStruct((part, n_head * COLS), bf16),
        in_specs=[any_space] * 4,
        out_specs=any_space,
        scratch_shapes=[
            pltpu.VMEM((tokens, COLS), bf16),
            pltpu.VMEM((tokens, HD), bf16),
            pltpu.VMEM((1, doc_blocks.shape[0]), jnp.int32),
            pltpu.VMEM((PIECES, 2 * HD, COLS), bf16),
            pltpu.VMEM((FAR + 1, PIECES, 2, B, HD), bf16),
            pltpu.VMEM((PIECES, 1, COLS), f32),
            pltpu.VMEM((PIECES, HD + EXTRA, COLS), f32),
            pltpu.VMEM((PIECES, 1, COLS), jnp.int32),
            pltpu.VMEM((n_head, part, COLS), bf16),
            pltpu.SemaphoreType.DMA((PIECES + 3,)),
            pltpu.SemaphoreType.DMA((FAR + 1, PIECES)),
            pltpu.SemaphoreType.DMA((FAR + 1, PIECES)),
            pltpu.SemaphoreType.DMA((n_head,)),
            pltpu.SemaphoreType.DMA((n_head,)),
        ],
        compiler_params=pltpu.CompilerParams(
            collective_id=0, has_side_effects=True, vmem_limit_bytes=62 << 20
        ),
        cost_estimate=pl.CostEstimate(
            flops=4 * pairs * HD, bytes_accessed=2 << 20, transcendentals=pairs
        ),
        name="attend",
    )(queries, key_rows, value_rows, doc_blocks.reshape(1, -1))


def solution(mesh):
    in_specs = (P("seq", "head"), P("seq", "head"), P("seq", "head"), P())
    out_specs = P(("seq", "head"), None)
    return jax.shard_map(
        functools.partial(body, mesh.shape["seq"], mesh.shape["head"]),
        mesh=mesh,
        in_specs=in_specs,
        out_specs=out_specs,
        check_vma=False,
    )
```

```python
import functools
import math

import jax
import jax.numpy as jnp
from jax import lax
from jax.experimental import pallas as pl
from jax.experimental.pallas import tpu as pltpu
from jax.sharding import PartitionSpec as P

HD = 128
B = 128
GROUP = 4
ROWS = 8
PIECES = 4
FAR = 8
CORES = 2
COLS = GROUP * B
EXTRA = 16
LAG_FORWARD = 2
LAG_BACKWARD = 1

NEG = -1e30
SCALE = math.log2(math.e) / math.sqrt(HD)
MESH = pl.DeviceIdType.MESH


def kernel(
    n_seq,
    n_head,
    q_hbm,
    k_hbm,
    v_hbm,
    doc_hbm,
    out_ref,
    q_in,
    v_in,
    doc_in,
    q_t,
    kv,
    top,
    acc,
    reach,
    out_buf,
    load_sem,
    send_sem,
    recv_sem,
    out_send,
    out_recv,
):
    s = lax.axis_index("seq")
    h = lax.axis_index("head")
    z = lax.rem(s, ROWS)
    chips = n_head // CORES
    x = h // CORES

    def ring(distance):
        return lax.rem(s + distance + n_seq, n_seq)

    after, before = ring(1), ring(-1)
    up, down = ring(ROWS), ring(-ROWS)
    ahead, behind = ring(ROWS - 1), ring(1 - ROWS)

    loads = [
        pltpu.make_async_copy(
            k_hbm.at[pl.ds(j * B, B), :], kv.at[0, j, 0], load_sem.at[j]
        )
        for j in range(PIECES)
    ]
    loads.append(pltpu.make_async_copy(v_hbm, v_in, load_sem.at[PIECES]))
    loads.append(pltpu.make_async_copy(doc_hbm, doc_in, load_sem.at[PIECES + 1]))
    loads.append(pltpu.make_async_copy(q_hbm, q_in, load_sem.at[PIECES + 2]))
    barrier = pltpu.get_barrier_semaphore()

    def greet(to_seq, to_head):
        pl.semaphore_signal(barrier, inc=1, device_id=(to_seq, to_head), device_id_type=MESH)

    for to in (after, before, up, down, ahead, behind):
        greet(to, h)
    for step in range(1, n_head):
        greet(s, lax.rem(h + step, n_head))

    for copy in loads:
        copy.start()
    for copy in loads[: PIECES + 1]:
        copy.wait()
    for j in range(PIECES):
        kv[0, j, 1] = v_in[pl.ds(j * B, B), :].T

    pl.semaphore_wait(barrier, 6 + n_head - 1)

    def move(src, dst, j, to, lane=None):
        return pltpu.make_async_remote_copy(
            src_ref=kv.at[src, j],
            dst_ref=kv.at[dst, j],
            send_sem=send_sem.at[dst if lane is None else lane, j],
            recv_sem=recv_sem.at[dst, j],
            device_id=(to, h),
            device_id_type=MESH,
        )

    def send(src, dst, j, to, lane=None):
        move(src, dst, j, to, lane).start()

    def arrived(d, j):
        move(d, d, j, after).wait_recv()

    def sent(d, j):
        move(d, d, j, after).wait_send()

    whole = 3 * PIECES

    def forward(n):
        return 1 + n // PIECES, lax.rem(n, PIECES)

    def backward(n):
        return FAR - 1 - n // PIECES, lax.rem(n, PIECES)

    for j in range(PIECES):
        send(0, 1, j, after)
        send(0, FAR - 1, j, ahead)

    loads[PIECES + 1].wait()
    lengths = doc_in[...]
    count = lengths.shape[1]
    shape = (count, count)
    upto = lax.broadcasted_iota(jnp.int32, shape, 1) <= lax.broadcasted_iota(jnp.int32, shape, 0)
    ends = jnp.sum(
        jnp.where(upto, jnp.broadcast_to(lengths, shape), 0).astype(jnp.float32),
        axis=1,
        keepdims=True,
    ).astype(jnp.int32)
    for i in range(PIECES):
        block = s * PIECES + i
        start = jnp.max(
            jnp.where(ends <= block, ends, 0).astype(jnp.float32), axis=0, keepdims=True
        ).astype(jnp.int32)
        reach[i] = jnp.broadcast_to(block - start, (1, COLS))

    loads[PIECES + 2].wait()
    for i in range(PIECES):
        for g in range(GROUP):
            rows = q_in[i * B : (i + 1) * B, g * HD : (g + 1) * HD]
            scaled = rows.astype(jnp.float32).T * SCALE
            high = scaled.astype(jnp.bfloat16)
            q_t[i, :HD, g * B : (g + 1) * B] = high
            q_t[i, HD:, g * B : (g + 1) * B] = (scaled - high.astype(jnp.float32)).astype(jnp.bfloat16)

    def update(i, chunks, first=False):
        queries = q_t[i]
        far = reach[i]
        scores, shown = [], []
        for d, blocks in chunks:
            n = len(blocks)
            keys = kv[d, blocks[0] : blocks[0] + n, 0].reshape(n * B, HD)
            pair = jnp.dot(
                jnp.concatenate([keys, keys], axis=1), queries, preferred_element_type=jnp.float32
            )
            for b, j in enumerate(blocks):
                block = pair[b * B : (b + 1) * B]
                delta = PIECES * d + i - j
                if first:
                    key = lax.broadcasted_iota(jnp.int32, (B, COLS), 0) + j * B
                    query = lax.rem(lax.broadcasted_iota(jnp.int32, (B, COLS), 1), B) + i * B
                    block = jnp.where(key <= query, block, NEG)
                    shown.append((delta <= far) & (delta >= 0))
                else:
                    shown.append(delta <= far)
                scores.append(block)
        peak = None
        for block, show in zip(scores, shown):
            here = jnp.where(show, jnp.max(block, axis=0, keepdims=True), NEG)
            peak = here if peak is None else jnp.maximum(peak, here)
        if not first:
            old = top[i]
            peak = jnp.maximum(old, peak)
            shrink = jnp.exp2(old - peak)
        top[i] = peak
        added = None
        at = 0
        ones = jnp.ones((EXTRA, B), jnp.bfloat16)
        for d, blocks in chunks:
            n = len(blocks)
            weights = [
                jnp.exp2(block - jnp.where(show, peak, -NEG)).astype(jnp.bfloat16)
                for block, show in zip(scores[at : at + n], shown[at : at + n])
            ]
            at += n
            values = jnp.concatenate(
                [jnp.concatenate([kv[d, j, 1], ones], axis=0) for j in blocks], axis=1
            )
            part = jnp.dot(
                values, jnp.concatenate(weights, axis=0), preferred_element_type=jnp.float32
            )
            added = part if added is None else added + part
        acc[i] = added if first else acc[i] * shrink + added

    every = tuple(range(PIECES))
    half = PIECES // 2

    first_pair = PIECES - 1 + LAG_FORWARD
    leaf = first_pair
    leaf_work = first_pair + PIECES + 1

    @pl.loop(0, PIECES)
    def _(i):
        update(i, [(0, every)], first=True)

    @pl.loop(0, first_pair + whole)
    def _(t):
        back = t - LAG_BACKWARD
        ahead_n = t - LAG_FORWARD

        @pl.when((back >= 0) & (back < whole))
        def _():
            d, j = backward(back)
            arrived(d, j)

            @pl.when((d > 5) | (z != 0))
            def _():
                send(d, d - 1, j, before)

        @pl.when((ahead_n >= 0) & (ahead_n < whole))
        def _():
            d, j = forward(ahead_n)
            arrived(d, j)

            @pl.when((d < 3) | (z == ROWS - 2))
            def _():
                send(d, d + 1, j, after, lax.rem(d + 1, 4))

        @pl.when((t >= leaf) & (t < leaf + PIECES - 1))
        def _():
            send(0, FAR, t - leaf + 1, up)

        @pl.when(t >= first_pair)
        def _():
            m = 1 + (t - first_pair) // PIECES
            update(lax.rem(t - first_pair, PIECES), [(FAR - m, every), (m, every)])

        @pl.when(t == leaf_work)
        def _():
            for j in range(1, PIECES):
                arrived(FAR, j)

        @pl.when((t >= leaf_work) & (t < leaf_work + PIECES))
        def _():
            update(t - leaf_work, [(FAR, every[1:])])

    for j in every[:half]:
        arrived(4, j)

    @pl.loop(0, PIECES)
    def _(i):
        update(i, [(4, every[:half])])

    for j in every[half:]:
        arrived(4, j)

    def columns(who):
        return pl.ds(pl.multiple_of(who * COLS, COLS), COLS)

    own = pltpu.make_async_copy(out_buf.at[h], out_ref.at[:, columns(h)], load_sem.at[0])
    core_here = lax.rem(h, CORES)

    def chip(hop):
        return lax.rem(x + hop, chips)

    def deliver(src, whose, target, send_at):
        return pltpu.make_async_remote_copy(
            src_ref=src,
            dst_ref=out_ref.at[:, columns(whose)],
            send_sem=send_at,
            recv_sem=out_recv.at[whose],
            device_id=(s, target),
            device_id_type=MESH,
        )

    for hop in (2, 1, 3, 0):
        i = chip(hop)
        update(i, [(4, every[half:])])
        final = (acc[i, :HD] * (1.0 / acc[i, HD : HD + 1])).astype(jnp.bfloat16)
        for g in range(GROUP):
            rows = final[:, g * B : (g + 1) * B].T
            for core in range(CORES):
                part = B // CORES
                out_buf[i * CORES + core, :, g * HD : (g + 1) * HD] = rows[
                    core * part : (core + 1) * part
                ]
        for core in range(CORES):
            target = i * CORES + core
            there = deliver(out_buf.at[target], h, target, out_send.at[target])
            if hop:
                there.start()
            else:

                @pl.when(core_here != core)
                def _():
                    there.start()

                @pl.when(core_here == core)
                def _():
                    own.start()

    @pl.loop(0, PIECES)
    def _(j):
        for d in (1, 2, 3, 5, 6, 7):
            sent(d, j)

        @pl.when(z != 0)
        def _():
            sent(4, j)

        @pl.when(z == ROWS - 2)
        def _():
            sent(0, j)

        @pl.when(j > 0)
        def _():
            sent(FAR, j)

    for step in range(1, n_head):
        peer = lax.rem(h + step, n_head)
        other = deliver(out_buf.at[peer], peer, peer, out_send.at[peer])
        other.wait_send()
        other.wait_recv()
    own.wait()


def body(n_seq, n_head, queries, key_rows, value_rows, doc_blocks):
    tokens = queries.shape[0]
    part = tokens // n_head
    in_hbm = pl.BlockSpec(memory_space=pltpu.HBM)
    bf16, f32 = jnp.bfloat16, jnp.float32
    pairs = tokens * PIECES * FAR * B * GROUP
    return pl.pallas_call(
        functools.partial(kernel, n_seq, n_head),
        out_shape=jax.ShapeDtypeStruct((part, n_head * COLS), bf16),
        in_specs=[in_hbm] * 4,
        out_specs=pl.BlockSpec(memory_space=pl.ANY),
        scratch_shapes=[
            pltpu.VMEM((tokens, COLS), bf16),
            pltpu.VMEM((tokens, HD), bf16),
            pltpu.VMEM((1, doc_blocks.shape[0]), jnp.int32),
            pltpu.VMEM((PIECES, 2 * HD, COLS), bf16),
            pltpu.VMEM((FAR + 1, PIECES, 2, B, HD), bf16),
            pltpu.VMEM((PIECES, 1, COLS), f32),
            pltpu.VMEM((PIECES, HD + EXTRA, COLS), f32),
            pltpu.VMEM((PIECES, 1, COLS), jnp.int32),
            pltpu.VMEM((n_head, part, COLS), bf16),
            pltpu.SemaphoreType.DMA((PIECES + 3,)),
            pltpu.SemaphoreType.DMA((FAR + 1, PIECES)),
            pltpu.SemaphoreType.DMA((FAR + 1, PIECES)),
            pltpu.SemaphoreType.DMA((n_head,)),
            pltpu.SemaphoreType.DMA((n_head,)),
        ],
        compiler_params=pltpu.CompilerParams(
            collective_id=0, has_side_effects=True, vmem_limit_bytes=62 << 20
        ),
        cost_estimate=pl.CostEstimate(
            flops=4 * pairs * HD, bytes_accessed=2 << 20, transcendentals=pairs
        ),
        name="attend",
    )(queries, key_rows, value_rows, doc_blocks.reshape(1, -1))


def solution(mesh):
    in_specs = (P("seq", "head"), P("seq", "head"), P("seq", "head"), P())
    out_specs = P(("seq", "head"), None)
    return jax.shard_map(
        functools.partial(body, mesh.shape["seq"], mesh.shape["head"]),
        mesh=mesh,
        in_specs=in_specs,
        out_specs=out_specs,
        check_vma=False,
    )
```

```python
import functools
import math

import jax
import jax.numpy as jnp
from jax import lax
from jax.experimental import pallas as pl
from jax.experimental.pallas import tpu as pltpu
from jax.sharding import PartitionSpec as P

HD = 128
B = 128
GROUP = 4
ROWS = 8
PIECES = 4
FAR = 8
CORES = 2
COLS = GROUP * B
EXTRA = 16
LAG = 2

NEG = -1e30
SCALE = math.log2(math.e) / math.sqrt(HD)
MESH = pl.DeviceIdType.MESH


def kernel(
    n_seq,
    n_head,
    q_hbm,
    k_hbm,
    v_hbm,
    doc_hbm,
    out_ref,
    q_in,
    v_in,
    doc_in,
    q_t,
    kv,
    top,
    acc,
    reach,
    out_buf,
    load_sem,
    send_sem,
    recv_sem,
    out_send,
    out_recv,
):
    s = lax.axis_index("seq")
    h = lax.axis_index("head")
    z = lax.rem(s, ROWS)
    chips = n_head // CORES
    x = h // CORES

    def ring(distance):
        return lax.rem(s + distance + n_seq, n_seq)

    after, before = ring(1), ring(-1)
    up, down = ring(ROWS), ring(-ROWS)
    first_col = ring(-(ROWS - 1))
    last_col = ring(ROWS - 1)

    loads = [
        pltpu.make_async_copy(
            k_hbm.at[pl.ds(j * B, B), :], kv.at[0, j, 0], load_sem.at[j]
        )
        for j in range(PIECES)
    ]
    loads.append(pltpu.make_async_copy(v_hbm, v_in, load_sem.at[PIECES]))
    loads.append(pltpu.make_async_copy(doc_hbm, doc_in, load_sem.at[PIECES + 1]))
    loads.append(pltpu.make_async_copy(q_hbm, q_in, load_sem.at[PIECES + 2]))
    barrier = pltpu.get_barrier_semaphore()

    def greet(to_seq, to_head):
        pl.semaphore_signal(barrier, inc=1, device_id=(to_seq, to_head), device_id_type=MESH)

    for to in (after, before, up, down):
        greet(to, h)
    for step in range(1, n_head):
        greet(s, lax.rem(h + step, n_head))

    @pl.when(z == ROWS - 1)
    def _():
        greet(first_col, h)

    @pl.when(z == 0)
    def _():
        greet(last_col, h)

    for copy in loads:
        copy.start()
    for copy in loads[: PIECES + 1]:
        copy.wait()
    for j in range(PIECES):
        kv[0, j, 1] = v_in[pl.ds(j * B, B), :].T

    edge = jnp.where((z == 0) | (z == ROWS - 1), 1, 0)
    pl.semaphore_wait(barrier, 4 + n_head - 1 + edge)

    def move(src, dst, j, to, lane=None):
        return pltpu.make_async_remote_copy(
            src_ref=kv.at[src, j],
            dst_ref=kv.at[dst, j],
            send_sem=send_sem.at[dst if lane is None else lane, j],
            recv_sem=recv_sem.at[dst, j],
            device_id=(to, h),
            device_id_type=MESH,
        )

    def send(src, dst, j, to, lane=None):
        move(src, dst, j, to, lane).start()

    def arrived(d, j):
        move(d, d, j, after).wait_recv()

    def sent(d, j):
        move(d, d, j, after).wait_send()

    for j in range(PIECES):
        send(0, FAR, j, up)

        send(0, 1, j, after)

        @pl.when(z == 0)
        def _():
            send(0, FAR - 1, j, last_col)

    loads[PIECES + 1].wait()
    lengths = doc_in[...]
    count = lengths.shape[1]
    shape = (count, count)
    upto = lax.broadcasted_iota(jnp.int32, shape, 1) <= lax.broadcasted_iota(jnp.int32, shape, 0)
    ends = jnp.sum(
        jnp.where(upto, jnp.broadcast_to(lengths, shape), 0).astype(jnp.float32),
        axis=1,
        keepdims=True,
    ).astype(jnp.int32)
    for i in range(PIECES):
        block = s * PIECES + i
        start = jnp.max(
            jnp.where(ends <= block, ends, 0).astype(jnp.float32), axis=0, keepdims=True
        ).astype(jnp.int32)
        reach[i] = jnp.broadcast_to(block - start, (1, COLS))

    loads[PIECES + 2].wait()
    for i in range(PIECES):
        for g in range(GROUP):
            rows = q_in[i * B : (i + 1) * B, g * HD : (g + 1) * HD]
            scaled = rows.astype(jnp.float32).T * SCALE
            high = scaled.astype(jnp.bfloat16)
            q_t[i, :HD, g * B : (g + 1) * B] = high
            q_t[i, HD:, g * B : (g + 1) * B] = (scaled - high.astype(jnp.float32)).astype(jnp.bfloat16)

    def update(i, chunks, first=False):
        queries = q_t[i]
        far = reach[i]
        scores, shown = [], []
        for d, blocks in chunks:
            n = len(blocks)
            keys = kv[d, blocks[0] : blocks[0] + n, 0].reshape(n * B, HD)
            pair = jnp.dot(
                jnp.concatenate([keys, keys], axis=1), queries, preferred_element_type=jnp.float32
            )
            for b, j in enumerate(blocks):
                block = pair[b * B : (b + 1) * B]
                delta = PIECES * d + i - j
                if first:
                    key = lax.broadcasted_iota(jnp.int32, (B, COLS), 0) + j * B
                    query = lax.rem(lax.broadcasted_iota(jnp.int32, (B, COLS), 1), B) + i * B
                    block = jnp.where(key <= query, block, NEG)
                    shown.append((delta <= far) & (delta >= 0))
                else:
                    shown.append(delta <= far)
                scores.append(block)
        peak = None
        for block, show in zip(scores, shown):
            here = jnp.where(show, jnp.max(block, axis=0, keepdims=True), NEG)
            peak = here if peak is None else jnp.maximum(peak, here)
        if not first:
            old = top[i]
            peak = jnp.maximum(old, peak)
            shrink = jnp.exp2(old - peak)
        top[i] = peak
        added = None
        at = 0
        ones = jnp.ones((EXTRA, B), jnp.bfloat16)
        for d, blocks in chunks:
            n = len(blocks)
            weights = [
                jnp.exp2(block - jnp.where(show, peak, -NEG)).astype(jnp.bfloat16)
                for block, show in zip(scores[at : at + n], shown[at : at + n])
            ]
            at += n
            values = jnp.concatenate(
                [jnp.concatenate([kv[d, j, 1], ones], axis=0) for j in blocks], axis=1
            )
            part = jnp.dot(
                values, jnp.concatenate(weights, axis=0), preferred_element_type=jnp.float32
            )
            added = part if added is None else added + part
        acc[i] = added if first else acc[i] * shrink + added

    every = tuple(range(PIECES))
    half = PIECES // 2

    @pl.loop(0, PIECES)
    def _(j):
        update(j, [(0, every)], first=True)

    far_steps = 4 * PIECES
    work_from = PIECES - 1 + LAG

    @pl.loop(0, 3 * PIECES + work_from)
    def _(t):
        j = lax.rem(t, PIECES)
        d = FAR - t // PIECES

        @pl.when(t < far_steps)
        def _():
            arrived(d, j)

            @pl.when((d > 5) & ((d < FAR) | (z != 0)))
            def _():
                send(d, d - 1, j, before)

            @pl.when((d == 5) & (z == 1))
            def _():
                send(5, 4, j, before, 0)

        u = t - LAG
        near = u // PIECES + 1
        k = lax.rem(u + PIECES, PIECES)

        @pl.when(u >= 0)
        def _():
            arrived(near, k)

            @pl.when((near < 3) | ((near == 3) & (z != ROWS - 1)))
            def _():
                send(near, near + 1, k, after)

        w = t - work_from

        @pl.when(w >= 0)
        def _():
            p = w // PIECES + 1
            update(lax.rem(w, PIECES), [(p, every), (FAR + 1 - p, every)])

    @pl.loop(0, PIECES)
    def _(j):
        update(j, [(5, every[:half]), (4, every[:half])])

    for u in range(3 * PIECES + work_from - LAG, 4 * PIECES):
        arrived(u // PIECES + 1, u % PIECES)

    own = pltpu.make_async_copy(
        out_buf.at[h],
        out_ref.at[:, pl.ds(pl.multiple_of(h * COLS, COLS), COLS)],
        load_sem.at[0],
    )
    for hop in (2, 1, 3, 0):
        to_x = lax.rem(x + hop, chips)
        i = to_x
        update(i, [(5, every[half:]), (4, every[half:])])
        final = (acc[i, :HD] * (1.0 / acc[i, HD : HD + 1])).astype(jnp.bfloat16)
        for g in range(GROUP):
            rows = final[:, g * B : (g + 1) * B].T
            for core in range(CORES):
                part = B // CORES
                out_buf[to_x * CORES + core, :, g * HD : (g + 1) * HD] = rows[
                    core * part : (core + 1) * part
                ]
        for core in range(CORES):
            target = to_x * CORES + core
            step = lax.rem(target - h + n_head, n_head)
            there = pltpu.make_async_remote_copy(
                src_ref=out_buf.at[target],
                dst_ref=out_ref.at[:, pl.ds(pl.multiple_of(h * COLS, COLS), COLS)],
                send_sem=out_send.at[target],
                recv_sem=out_recv.at[h],
                device_id=(s, target),
                device_id_type=MESH,
            )
            if hop == 0:

                @pl.when(step != 0)
                def _():
                    there.start()

                @pl.when(step == 0)
                def _():
                    own.start()

            else:
                there.start()

    @pl.loop(0, PIECES)
    def _(j):
        for d in (1, 2, 3, 5, 6, 7, 8):
            sent(d, j)

        @pl.when(z != ROWS - 1)
        def _():
            sent(4, j)

        @pl.when(z == 1)
        def _():
            sent(0, j)

    for step in range(1, n_head):
        peer = lax.rem(h + step, n_head)
        other = pltpu.make_async_remote_copy(
            src_ref=out_buf.at[peer],
            dst_ref=out_ref.at[:, pl.ds(pl.multiple_of(peer * COLS, COLS), COLS)],
            send_sem=out_send.at[peer],
            recv_sem=out_recv.at[peer],
            device_id=(s, peer),
            device_id_type=MESH,
        )
        other.wait_send()
        other.wait_recv()
    own.wait()


def body(n_seq, n_head, queries, key_rows, value_rows, doc_blocks):
    tokens = queries.shape[0]
    part = tokens // n_head
    any_space = pl.BlockSpec(memory_space=pl.ANY)
    bf16, f32 = jnp.bfloat16, jnp.float32
    pairs = tokens * PIECES * FAR * B * GROUP
    return pl.pallas_call(
        functools.partial(kernel, n_seq, n_head),
        out_shape=jax.ShapeDtypeStruct((part, n_head * COLS), bf16),
        in_specs=[any_space] * 4,
        out_specs=any_space,
        scratch_shapes=[
            pltpu.VMEM((tokens, COLS), bf16),
            pltpu.VMEM((tokens, HD), bf16),
            pltpu.VMEM((1, doc_blocks.shape[0]), jnp.int32),
            pltpu.VMEM((PIECES, 2 * HD, COLS), bf16),
            pltpu.VMEM((FAR + 1, PIECES, 2, B, HD), bf16),
            pltpu.VMEM((PIECES, 1, COLS), f32),
            pltpu.VMEM((PIECES, HD + EXTRA, COLS), f32),
            pltpu.VMEM((PIECES, 1, COLS), jnp.int32),
            pltpu.VMEM((n_head, part, COLS), bf16),
            pltpu.SemaphoreType.DMA((PIECES + 3,)),
            pltpu.SemaphoreType.DMA((FAR + 1, PIECES)),
            pltpu.SemaphoreType.DMA((FAR + 1, PIECES)),
            pltpu.SemaphoreType.DMA((n_head,)),
            pltpu.SemaphoreType.DMA((n_head,)),
        ],
        compiler_params=pltpu.CompilerParams(
            collective_id=0, has_side_effects=True, vmem_limit_bytes=62 << 20
        ),
        cost_estimate=pl.CostEstimate(
            flops=4 * pairs * HD, bytes_accessed=2 << 20, transcendentals=pairs
        ),
        name="attend",
    )(queries, key_rows, value_rows, doc_blocks.reshape(1, -1))


def solution(mesh):
    in_specs = (P("seq", "head"), P("seq", "head"), P("seq", "head"), P())
    out_specs = P(("seq", "head"), None)
    return jax.shard_map(
        functools.partial(body, mesh.shape["seq"], mesh.shape["head"]),
        mesh=mesh,
        in_specs=in_specs,
        out_specs=out_specs,
        check_vma=False,
    )
```

```python
import functools
import math

import jax
import jax.numpy as jnp
from jax import lax
from jax.experimental import pallas as pl
from jax.experimental.pallas import tpu as pltpu
from jax.sharding import PartitionSpec as P

HD = 128
B = 128
GROUP = 4
ROWS = 8
PIECES = 4
FAR = 8
CORES = 2
COLS = GROUP * B
EXTRA = 16
LAG = 2
LAG_WRAP = 4

NEG = -1e30
SCALE = math.log2(math.e) / math.sqrt(HD)
MESH = pl.DeviceIdType.MESH


def kernel(
    n_seq,
    n_head,
    q_hbm,
    k_hbm,
    v_hbm,
    doc_hbm,
    out_ref,
    q_in,
    v_in,
    doc_in,
    q_t,
    kv,
    top,
    acc,
    reach,
    out_buf,
    load_sem,
    send_sem,
    recv_sem,
    out_send,
    out_recv,
):
    s = lax.axis_index("seq")
    h = lax.axis_index("head")
    z = lax.rem(s, ROWS)
    chips = n_head // CORES
    x = h // CORES

    def ring(distance):
        return lax.rem(s + distance + n_seq, n_seq)

    after, before = ring(1), ring(-1)
    up, down = ring(ROWS), ring(-ROWS)
    first_col = ring(-(ROWS - 1))
    last_col = ring(ROWS - 1)

    def wanted(who, d):
        beyond = d - who
        return (beyond <= 0) | (beyond == ROWS - 2) | (beyond == ROWS - 1)

    @pl.when(s < ROWS)
    def _():
        @pl.loop(1, FAR + 1)
        def _(d):
            kv[d] = jnp.zeros(kv.shape[1:], kv.dtype)

    loads = [
        pltpu.make_async_copy(
            k_hbm.at[pl.ds(j * B, B), :], kv.at[0, j, 0], load_sem.at[j]
        )
        for j in range(PIECES)
    ]
    loads.append(pltpu.make_async_copy(v_hbm, v_in, load_sem.at[PIECES]))
    loads.append(pltpu.make_async_copy(doc_hbm, doc_in, load_sem.at[PIECES + 1]))
    loads.append(pltpu.make_async_copy(q_hbm, q_in, load_sem.at[PIECES + 2]))
    barrier = pltpu.get_barrier_semaphore()

    def greet(to_seq, to_head):
        pl.semaphore_signal(barrier, inc=1, device_id=(to_seq, to_head), device_id_type=MESH)

    for to in (after, before, up, down):
        greet(to, h)
    for step in range(1, n_head):
        greet(s, lax.rem(h + step, n_head))

    @pl.when(z == ROWS - 1)
    def _():
        greet(first_col, h)

    @pl.when(z == 0)
    def _():
        greet(last_col, h)

    for copy in loads:
        copy.start()
    for copy in loads[: PIECES + 1]:
        copy.wait()
    for j in range(PIECES):
        kv[0, j, 1] = v_in[pl.ds(j * B, B), :].T

    edge = jnp.where((z == 0) | (z == ROWS - 1), 1, 0)
    pl.semaphore_wait(barrier, 4 + n_head - 1 + edge)

    def move(src, dst, j, to, lane=None):
        return pltpu.make_async_remote_copy(
            src_ref=kv.at[src, j],
            dst_ref=kv.at[dst, j],
            send_sem=send_sem.at[dst if lane is None else lane, j],
            recv_sem=recv_sem.at[dst, j],
            device_id=(to, h),
            device_id_type=MESH,
        )

    def send(src, dst, j, to, lane=None):
        @pl.when(wanted(to, dst))
        def _():
            move(src, dst, j, to, lane).start()

    def arrived(d, j):
        @pl.when(wanted(s, d))
        def _():
            move(d, d, j, after).wait_recv()

    def sent(d, j, to, lane=None):
        @pl.when(wanted(to, d))
        def _():
            move(d, d, j, to, lane).wait_send()

    for j in range(PIECES):
        send(0, FAR, j, up)

        send(0, 1, j, after)

        @pl.when(z == 0)
        def _():
            send(0, FAR - 1, j, last_col)

    loads[PIECES + 1].wait()
    lengths = doc_in[...]
    count = lengths.shape[1]
    shape = (count, count)
    upto = lax.broadcasted_iota(jnp.int32, shape, 1) <= lax.broadcasted_iota(jnp.int32, shape, 0)
    ends = jnp.sum(
        jnp.where(upto, jnp.broadcast_to(lengths, shape), 0).astype(jnp.float32),
        axis=1,
        keepdims=True,
    ).astype(jnp.int32)
    for i in range(PIECES):
        block = s * PIECES + i
        start = jnp.max(
            jnp.where(ends <= block, ends, 0).astype(jnp.float32), axis=0, keepdims=True
        ).astype(jnp.int32)
        reach[i] = jnp.broadcast_to(block - start, (1, COLS))

    loads[PIECES + 2].wait()
    for i in range(PIECES):
        for g in range(GROUP):
            rows = q_in[i * B : (i + 1) * B, g * HD : (g + 1) * HD]
            scaled = rows.astype(jnp.float32).T * SCALE
            high = scaled.astype(jnp.bfloat16)
            q_t[i, :HD, g * B : (g + 1) * B] = high
            q_t[i, HD:, g * B : (g + 1) * B] = (scaled - high.astype(jnp.float32)).astype(jnp.bfloat16)

    def update(i, chunks, first=False):
        queries = q_t[i]
        far = reach[i]
        scores, shown = [], []
        for d, blocks in chunks:
            n = len(blocks)
            keys = kv[d, blocks[0] : blocks[0] + n, 0].reshape(n * B, HD)
            pair = jnp.dot(
                jnp.concatenate([keys, keys], axis=1), queries, preferred_element_type=jnp.float32
            )
            for b, j in enumerate(blocks):
                block = pair[b * B : (b + 1) * B]
                delta = PIECES * d + i - j
                if first:
                    key = lax.broadcasted_iota(jnp.int32, (B, COLS), 0) + j * B
                    query = lax.rem(lax.broadcasted_iota(jnp.int32, (B, COLS), 1), B) + i * B
                    block = jnp.where(key <= query, block, NEG)
                    shown.append((delta <= far) & (delta >= 0))
                else:
                    shown.append(delta <= far)
                scores.append(block)
        peak = None
        for block, show in zip(scores, shown):
            here = jnp.where(show, jnp.max(block, axis=0, keepdims=True), NEG)
            peak = here if peak is None else jnp.maximum(peak, here)
        if not first:
            old = top[i]
            peak = jnp.maximum(old, peak)
            shrink = jnp.exp2(old - peak)
        top[i] = peak
        added = None
        at = 0
        ones = jnp.ones((EXTRA, B), jnp.bfloat16)
        for d, blocks in chunks:
            n = len(blocks)
            weights = [
                jnp.exp2(block - jnp.where(show, peak, -NEG)).astype(jnp.bfloat16)
                for block, show in zip(scores[at : at + n], shown[at : at + n])
            ]
            at += n
            values = jnp.concatenate(
                [jnp.concatenate([kv[d, j, 1], ones], axis=0) for j in blocks], axis=1
            )
            part = jnp.dot(
                values, jnp.concatenate(weights, axis=0), preferred_element_type=jnp.float32
            )
            added = part if added is None else added + part
        acc[i] = added if first else acc[i] * shrink + added

    every = tuple(range(PIECES))
    half = PIECES // 2

    @pl.loop(0, PIECES)
    def _(j):
        update(j, [(0, every)], first=True)

    far_steps = 4 * PIECES
    lag = jnp.where(z < 2, LAG_WRAP, LAG)
    work_from = PIECES - 1 + lag

    @pl.loop(0, 4 * PIECES - 1 + LAG_WRAP)
    def _(t):
        j = lax.rem(t, PIECES)
        d = FAR - t // PIECES

        @pl.when(t < far_steps)
        def _():
            arrived(d, j)

            @pl.when((d > 5) & ((d < FAR) | (z != 0)))
            def _():
                send(d, d - 1, j, before)

            @pl.when((d == 5) & (z == 1))
            def _():
                send(5, 4, j, before, 0)

        u = t - lag
        near = u // PIECES + 1
        k = lax.rem(u + PIECES, PIECES)

        @pl.when((u >= 0) & (u < 4 * PIECES - 1))
        def _():
            arrived(near, k)

            @pl.when((near < 3) | ((near == 3) & (z != ROWS - 1)))
            def _():
                send(near, near + 1, k, after)

        w = t - work_from

        @pl.when((w >= 0) & (w < 3 * PIECES))
        def _():
            p = w // PIECES + 1
            update(lax.rem(w, PIECES), [(p, every), (FAR + 1 - p, every)])

    @pl.loop(0, PIECES)
    def _(j):
        update(j, [(5, every[:half]), (4, every[:half])])

    arrived(4, PIECES - 1)

    own = pltpu.make_async_copy(
        out_buf.at[h],
        out_ref.at[:, pl.ds(pl.multiple_of(h * COLS, COLS), COLS)],
        load_sem.at[0],
    )
    for hop in (2, 1, 3, 0):
        to_x = lax.rem(x + hop, chips)
        i = to_x
        update(i, [(5, every[half:]), (4, every[half:])])
        final = (acc[i, :HD] * (1.0 / acc[i, HD : HD + 1])).astype(jnp.bfloat16)
        for g in range(GROUP):
            rows = final[:, g * B : (g + 1) * B].T
            for core in range(CORES):
                part = B // CORES
                out_buf[to_x * CORES + core, :, g * HD : (g + 1) * HD] = rows[
                    core * part : (core + 1) * part
                ]
        for core in range(CORES):
            target = to_x * CORES + core
            step = lax.rem(target - h + n_head, n_head)
            there = pltpu.make_async_remote_copy(
                src_ref=out_buf.at[target],
                dst_ref=out_ref.at[:, pl.ds(pl.multiple_of(h * COLS, COLS), COLS)],
                send_sem=out_send.at[target],
                recv_sem=out_recv.at[h],
                device_id=(s, target),
                device_id_type=MESH,
            )
            if hop == 0:

                @pl.when(step != 0)
                def _():
                    there.start()

                @pl.when(step == 0)
                def _():
                    own.start()

            else:
                there.start()

    @pl.loop(0, PIECES)
    def _(j):
        for d in (1, 2, 3):
            sent(d, j, after)
        for d in (5, 6):
            sent(d, j, before)
        sent(7, j, jnp.where(z == 0, last_col, before))
        sent(FAR, j, up)

        @pl.when(z != ROWS - 1)
        def _():
            sent(4, j, after)

        @pl.when(z == 1)
        def _():
            sent(4, j, before, 0)

    for step in range(1, n_head):
        peer = lax.rem(h + step, n_head)
        other = pltpu.make_async_remote_copy(
            src_ref=out_buf.at[peer],
            dst_ref=out_ref.at[:, pl.ds(pl.multiple_of(peer * COLS, COLS), COLS)],
            send_sem=out_send.at[peer],
            recv_sem=out_recv.at[peer],
            device_id=(s, peer),
            device_id_type=MESH,
        )
        other.wait_send()
        other.wait_recv()
    own.wait()


def body(n_seq, n_head, queries, key_rows, value_rows, doc_blocks):
    tokens = queries.shape[0]
    part = tokens // n_head
    any_space = pl.BlockSpec(memory_space=pl.ANY)
    bf16, f32 = jnp.bfloat16, jnp.float32
    pairs = tokens * PIECES * FAR * B * GROUP
    return pl.pallas_call(
        functools.partial(kernel, n_seq, n_head),
        out_shape=jax.ShapeDtypeStruct((part, n_head * COLS), bf16),
        in_specs=[any_space] * 4,
        out_specs=any_space,
        scratch_shapes=[
            pltpu.VMEM((tokens, COLS), bf16),
            pltpu.VMEM((tokens, HD), bf16),
            pltpu.VMEM((1, doc_blocks.shape[0]), jnp.int32),
            pltpu.VMEM((PIECES, 2 * HD, COLS), bf16),
            pltpu.VMEM((FAR + 1, PIECES, 2, B, HD), bf16),
            pltpu.VMEM((PIECES, 1, COLS), f32),
            pltpu.VMEM((PIECES, HD + EXTRA, COLS), f32),
            pltpu.VMEM((PIECES, 1, COLS), jnp.int32),
            pltpu.VMEM((n_head, part, COLS), bf16),
            pltpu.SemaphoreType.DMA((PIECES + 3,)),
            pltpu.SemaphoreType.DMA((FAR + 1, PIECES)),
            pltpu.SemaphoreType.DMA((FAR + 1, PIECES)),
            pltpu.SemaphoreType.DMA((n_head,)),
            pltpu.SemaphoreType.DMA((n_head,)),
        ],
        compiler_params=pltpu.CompilerParams(
            collective_id=0, has_side_effects=True, vmem_limit_bytes=62 << 20
        ),
        cost_estimate=pl.CostEstimate(
            flops=4 * pairs * HD, bytes_accessed=2 << 20, transcendentals=pairs
        ),
        name="attend",
    )(queries, key_rows, value_rows, doc_blocks.reshape(1, -1))


def solution(mesh):
    in_specs = (P("seq", "head"), P("seq", "head"), P("seq", "head"), P())
    out_specs = P(("seq", "head"), None)
    return jax.shard_map(
        functools.partial(body, mesh.shape["seq"], mesh.shape["head"]),
        mesh=mesh,
        in_specs=in_specs,
        out_specs=out_specs,
        check_vma=False,
    )
```

```python
import functools
import math

import jax
import jax.numpy as jnp
from jax import lax
from jax.experimental import pallas as pl
from jax.experimental.pallas import tpu as pltpu
from jax.sharding import PartitionSpec as P

HD = 128
B = 128
GROUP = 4
ROWS = 8
PIECES = 4
FAR = 8
CORES = 2
COLS = GROUP * B
EXTRA = 16
WINDOW = 2
LAG = 2
LAG_WRAP = 4

NEG = -1e30
SCALE = math.log2(math.e) / math.sqrt(HD)
MESH = pl.DeviceIdType.MESH


def kernel(
    n_seq,
    n_head,
    q_hbm,
    k_hbm,
    v_hbm,
    doc_hbm,
    out_ref,
    q_in,
    v_in,
    doc_in,
    q_t,
    kv,
    top,
    acc,
    reach,
    out_buf,
    load_sem,
    send_sem,
    recv_sem,
    out_send,
    out_recv,
):
    s = lax.axis_index("seq")
    h = lax.axis_index("head")
    z = lax.rem(s, ROWS)
    chips = n_head // CORES
    x = h // CORES

    def ring(distance):
        return lax.rem(s + distance + n_seq, n_seq)

    after, before = ring(1), ring(-1)
    up, down = ring(ROWS), ring(-ROWS)
    first_col = ring(-(ROWS - 1))
    last_col = ring(ROWS - 1)

    def wanted(who, d):
        beyond = d - who
        return (beyond <= 0) | (beyond == ROWS - 2) | (beyond == ROWS - 1)

    @pl.when(s < ROWS)
    def _():
        @pl.loop(1, FAR + 1)
        def _(d):
            kv[d] = jnp.zeros(kv.shape[1:], kv.dtype)

    loads = [
        pltpu.make_async_copy(
            k_hbm.at[pl.ds(j * B, B), :], kv.at[0, j, 0], load_sem.at[j]
        )
        for j in range(PIECES)
    ]
    loads.append(pltpu.make_async_copy(v_hbm, v_in, load_sem.at[PIECES]))
    loads.append(pltpu.make_async_copy(doc_hbm, doc_in, load_sem.at[PIECES + 1]))
    loads.append(pltpu.make_async_copy(q_hbm, q_in, load_sem.at[PIECES + 2]))
    barrier = pltpu.get_barrier_semaphore()

    def greet(to_seq, to_head):
        pl.semaphore_signal(barrier, inc=1, device_id=(to_seq, to_head), device_id_type=MESH)

    for to in (after, before, up, down):
        greet(to, h)
    for step in range(1, n_head):
        greet(s, lax.rem(h + step, n_head))

    @pl.when(z == ROWS - 1)
    def _():
        greet(first_col, h)

    @pl.when(z == 0)
    def _():
        greet(last_col, h)

    for copy in loads:
        copy.start()
    for copy in loads[: PIECES + 1]:
        copy.wait()
    for j in range(PIECES):
        kv[0, j, 1] = v_in[pl.ds(j * B, B), :].T

    edge = jnp.where((z == 0) | (z == ROWS - 1), 1, 0)
    pl.semaphore_wait(barrier, 4 + n_head - 1 + edge)

    def move(src, dst, j, to, lane=None):
        return pltpu.make_async_remote_copy(
            src_ref=kv.at[src, j],
            dst_ref=kv.at[dst, j],
            send_sem=send_sem.at[dst if lane is None else lane, j],
            recv_sem=recv_sem.at[dst, j],
            device_id=(to, h),
            device_id_type=MESH,
        )

    def send(src, dst, j, to, lane=None):
        @pl.when(wanted(to, dst))
        def _():
            move(src, dst, j, to, lane).start()

    def arrived(d, j):
        @pl.when(wanted(s, d))
        def _():
            move(d, d, j, after).wait_recv()

    def sent(d, j, to, lane=None):
        @pl.when(wanted(to, d))
        def _():
            move(d, d, j, to, lane).wait_send()

    for j in range(PIECES):
        if j < WINDOW:

            @pl.when(z != 0)
            def _():
                send(0, FAR, j, up)

        send(0, 1, j, after)

        @pl.when(z == 0)
        def _():
            send(0, FAR - 1, j, last_col)

    loads[PIECES + 1].wait()
    lengths = doc_in[...]
    count = lengths.shape[1]
    shape = (count, count)
    upto = lax.broadcasted_iota(jnp.int32, shape, 1) <= lax.broadcasted_iota(jnp.int32, shape, 0)
    ends = jnp.sum(
        jnp.where(upto, jnp.broadcast_to(lengths, shape), 0).astype(jnp.float32),
        axis=1,
        keepdims=True,
    ).astype(jnp.int32)
    for i in range(PIECES):
        block = s * PIECES + i
        start = jnp.max(
            jnp.where(ends <= block, ends, 0).astype(jnp.float32), axis=0, keepdims=True
        ).astype(jnp.int32)
        reach[i] = jnp.broadcast_to(block - start, (1, COLS))

    loads[PIECES + 2].wait()
    for i in range(PIECES):
        for g in range(GROUP):
            rows = q_in[i * B : (i + 1) * B, g * HD : (g + 1) * HD]
            scaled = rows.astype(jnp.float32).T * SCALE
            high = scaled.astype(jnp.bfloat16)
            q_t[i, :HD, g * B : (g + 1) * B] = high
            q_t[i, HD:, g * B : (g + 1) * B] = (scaled - high.astype(jnp.float32)).astype(jnp.bfloat16)

    def update(i, chunks, first=False):
        queries = q_t[i]
        far = reach[i]
        scores, shown = [], []
        for d, blocks in chunks:
            n = len(blocks)
            keys = kv[d, blocks[0] : blocks[0] + n, 0].reshape(n * B, HD)
            pair = jnp.dot(
                jnp.concatenate([keys, keys], axis=1), queries, preferred_element_type=jnp.float32
            )
            for b, j in enumerate(blocks):
                block = pair[b * B : (b + 1) * B]
                delta = PIECES * d + i - j
                if first:
                    key = lax.broadcasted_iota(jnp.int32, (B, COLS), 0) + j * B
                    query = lax.rem(lax.broadcasted_iota(jnp.int32, (B, COLS), 1), B) + i * B
                    block = jnp.where(key <= query, block, NEG)
                    shown.append((delta <= far) & (delta >= 0))
                else:
                    shown.append(delta <= far)
                scores.append(block)
        peak = None
        for block, show in zip(scores, shown):
            here = jnp.where(show, jnp.max(block, axis=0, keepdims=True), NEG)
            peak = here if peak is None else jnp.maximum(peak, here)
        if not first:
            old = top[i]
            peak = jnp.maximum(old, peak)
            shrink = jnp.exp2(old - peak)
        top[i] = peak
        added = None
        at = 0
        ones = jnp.ones((EXTRA, B), jnp.bfloat16)
        for d, blocks in chunks:
            n = len(blocks)
            weights = [
                jnp.exp2(block - jnp.where(show, peak, -NEG)).astype(jnp.bfloat16)
                for block, show in zip(scores[at : at + n], shown[at : at + n])
            ]
            at += n
            values = jnp.concatenate(
                [jnp.concatenate([kv[d, j, 1], ones], axis=0) for j in blocks], axis=1
            )
            part = jnp.dot(
                values, jnp.concatenate(weights, axis=0), preferred_element_type=jnp.float32
            )
            added = part if added is None else added + part
        acc[i] = added if first else acc[i] * shrink + added

    every = tuple(range(PIECES))
    half = PIECES // 2

    @pl.loop(0, PIECES)
    def _(i):
        update(i, [(0, every)], first=True)

        @pl.when((z != 0) & (i < PIECES - WINDOW))
        def _():
            sent(FAR, i, up)
            send(0, FAR, i + WINDOW, up)

    lag = jnp.where(z < 2, LAG_WRAP, LAG)
    work_from = 2 * PIECES - 1

    @pl.loop(0, 3 * PIECES + work_from)
    def _(t):
        j = lax.rem(t, PIECES)
        d = FAR - t // PIECES

        @pl.when((t < 4 * PIECES) & ((d < FAR) | (z != 0)))
        def _():
            arrived(d, j)

            @pl.when(d > 5)
            def _():
                send(d, d - 1, j, before)

            @pl.when((d == 5) & (z == 1))
            def _():
                send(5, 4, j, before, 0)

        @pl.when((z == 0) & (t > PIECES) & (t < 2 * PIECES))
        def _():
            send(0, FAR, j, up)

        u = t - lag
        near = u // PIECES + 1
        k = lax.rem(u + PIECES, PIECES)

        @pl.when((u >= 0) & (u < 3 * PIECES))
        def _():
            arrived(near, k)

            @pl.when((near < 3) | (z != ROWS - 1))
            def _():
                send(near, near + 1, k, after)

        w = t - work_from

        @pl.when(w >= 0)
        def _():
            p = w // PIECES + 1
            update(lax.rem(w, PIECES), [(p, every), (FAR - p, every)])

    for j in every[1:]:

        @pl.when(z == 0)
        def _():
            arrived(FAR, j)

    for j in every[:half]:
        arrived(4, j)

    @pl.loop(0, PIECES)
    def _(i):
        update(i, [(FAR, every[1:]), (4, every[:half])])

    for j in every[half:]:
        arrived(4, j)

    own = pltpu.make_async_copy(
        out_buf.at[h],
        out_ref.at[:, pl.ds(pl.multiple_of(h * COLS, COLS), COLS)],
        load_sem.at[0],
    )
    for hop in (2, 1, 3, 0):
        to_x = lax.rem(x + hop, chips)
        i = to_x
        update(i, [(4, every[half:])])
        final = (acc[i, :HD] * (1.0 / acc[i, HD : HD + 1])).astype(jnp.bfloat16)
        for g in range(GROUP):
            rows = final[:, g * B : (g + 1) * B].T
            for core in range(CORES):
                part = B // CORES
                out_buf[to_x * CORES + core, :, g * HD : (g + 1) * HD] = rows[
                    core * part : (core + 1) * part
                ]
        for core in range(CORES):
            target = to_x * CORES + core
            step = lax.rem(target - h + n_head, n_head)
            there = pltpu.make_async_remote_copy(
                src_ref=out_buf.at[target],
                dst_ref=out_ref.at[:, pl.ds(pl.multiple_of(h * COLS, COLS), COLS)],
                send_sem=out_send.at[target],
                recv_sem=out_recv.at[h],
                device_id=(s, target),
                device_id_type=MESH,
            )
            if hop == 0:

                @pl.when(step != 0)
                def _():
                    there.start()

                @pl.when(step == 0)
                def _():
                    own.start()

            else:
                there.start()

    @pl.loop(0, PIECES)
    def _(j):
        for d in (1, 2, 3):
            sent(d, j, after)
        for d in (5, 6):
            sent(d, j, before)
        sent(7, j, jnp.where(z == 0, last_col, before))

        @pl.when(jnp.where(z == 0, j > 0, j >= PIECES - WINDOW))
        def _():
            sent(FAR, j, up)

        @pl.when(z != ROWS - 1)
        def _():
            sent(4, j, after)

        @pl.when(z == 1)
        def _():
            sent(4, j, before, 0)

    for step in range(1, n_head):
        peer = lax.rem(h + step, n_head)
        other = pltpu.make_async_remote_copy(
            src_ref=out_buf.at[peer],
            dst_ref=out_ref.at[:, pl.ds(pl.multiple_of(peer * COLS, COLS), COLS)],
            send_sem=out_send.at[peer],
            recv_sem=out_recv.at[peer],
            device_id=(s, peer),
            device_id_type=MESH,
        )
        other.wait_send()
        other.wait_recv()
    own.wait()


def body(n_seq, n_head, queries, key_rows, value_rows, doc_blocks):
    tokens = queries.shape[0]
    part = tokens // n_head
    any_space = pl.BlockSpec(memory_space=pl.ANY)
    bf16, f32 = jnp.bfloat16, jnp.float32
    pairs = tokens * PIECES * FAR * B * GROUP
    return pl.pallas_call(
        functools.partial(kernel, n_seq, n_head),
        out_shape=jax.ShapeDtypeStruct((part, n_head * COLS), bf16),
        in_specs=[any_space] * 4,
        out_specs=any_space,
        scratch_shapes=[
            pltpu.VMEM((tokens, COLS), bf16),
            pltpu.VMEM((tokens, HD), bf16),
            pltpu.VMEM((1, doc_blocks.shape[0]), jnp.int32),
            pltpu.VMEM((PIECES, 2 * HD, COLS), bf16),
            pltpu.VMEM((FAR + 1, PIECES, 2, B, HD), bf16),
            pltpu.VMEM((PIECES, 1, COLS), f32),
            pltpu.VMEM((PIECES, HD + EXTRA, COLS), f32),
            pltpu.VMEM((PIECES, 1, COLS), jnp.int32),
            pltpu.VMEM((n_head, part, COLS), bf16),
            pltpu.SemaphoreType.DMA((PIECES + 3,)),
            pltpu.SemaphoreType.DMA((FAR + 1, PIECES)),
            pltpu.SemaphoreType.DMA((FAR + 1, PIECES)),
            pltpu.SemaphoreType.DMA((n_head,)),
            pltpu.SemaphoreType.DMA((n_head,)),
        ],
        compiler_params=pltpu.CompilerParams(
            collective_id=0, has_side_effects=True, vmem_limit_bytes=62 << 20
        ),
        cost_estimate=pl.CostEstimate(
            flops=4 * pairs * HD, bytes_accessed=2 << 20, transcendentals=pairs
        ),
        name="attend",
    )(queries, key_rows, value_rows, doc_blocks.reshape(1, -1))


def solution(mesh):
    in_specs = (P("seq", "head"), P("seq", "head"), P("seq", "head"), P())
    out_specs = P(("seq", "head"), None)
    return jax.shard_map(
        functools.partial(body, mesh.shape["seq"], mesh.shape["head"]),
        mesh=mesh,
        in_specs=in_specs,
        out_specs=out_specs,
        check_vma=False,
    )
```

```python
import functools
import math

import jax
import jax.numpy as jnp
from jax import lax
from jax.experimental import pallas as pl
from jax.experimental.pallas import tpu as pltpu
from jax.sharding import PartitionSpec as P

HD = 128
B = 128
GROUP = 4
ROWS = 8
PIECES = 4
FAR = 8
CORES = 2
COLS = GROUP * B
EXTRA = 16
LAG = 2
LAG_WRAP = 4

NEG = -1e30
SCALE = math.log2(math.e) / math.sqrt(HD)
MESH = pl.DeviceIdType.MESH


def kernel(
    n_seq,
    n_head,
    q_hbm,
    k_hbm,
    v_hbm,
    doc_hbm,
    out_ref,
    q_in,
    v_in,
    doc_in,
    q_t,
    kv,
    top,
    acc,
    reach,
    out_buf,
    load_sem,
    send_sem,
    recv_sem,
    out_send,
    out_recv,
):
    s = lax.axis_index("seq")
    h = lax.axis_index("head")
    z = lax.rem(s, ROWS)
    chips = n_head // CORES
    x = h // CORES

    def ring(distance):
        return lax.rem(s + distance + n_seq, n_seq)

    after, before = ring(1), ring(-1)
    up, down = ring(ROWS), ring(-ROWS)
    first_col = ring(-(ROWS - 1))
    last_col = ring(ROWS - 1)

    def wanted(who, d):
        beyond = d - who
        return (beyond <= 0) | (beyond == ROWS - 2) | (beyond == ROWS - 1)

    @pl.when(s < ROWS)
    def _():
        @pl.loop(1, FAR + 1)
        def _(d):
            kv[d] = jnp.zeros(kv.shape[1:], kv.dtype)

    loads = [
        pltpu.make_async_copy(
            k_hbm.at[pl.ds(j * B, B), :], kv.at[0, j, 0], load_sem.at[j]
        )
        for j in range(PIECES)
    ]
    loads.append(pltpu.make_async_copy(v_hbm, v_in, load_sem.at[PIECES]))
    loads.append(pltpu.make_async_copy(doc_hbm, doc_in, load_sem.at[PIECES + 1]))
    loads.append(pltpu.make_async_copy(q_hbm, q_in, load_sem.at[PIECES + 2]))
    barrier = pltpu.get_barrier_semaphore()

    def greet(to_seq, to_head):
        pl.semaphore_signal(barrier, inc=1, device_id=(to_seq, to_head), device_id_type=MESH)

    for to in (after, before, up, down):
        greet(to, h)
    for step in range(1, n_head):
        greet(s, lax.rem(h + step, n_head))

    @pl.when(z == ROWS - 1)
    def _():
        greet(first_col, h)

    @pl.when(z == 0)
    def _():
        greet(last_col, h)

    for copy in loads:
        copy.start()
    for copy in loads[: PIECES + 1]:
        copy.wait()
    for j in range(PIECES):
        kv[0, j, 1] = v_in[pl.ds(j * B, B), :].T

    edge = jnp.where((z == 0) | (z == ROWS - 1), 1, 0)
    pl.semaphore_wait(barrier, 4 + n_head - 1 + edge)

    def move(src, dst, j, to, lane=None):
        return pltpu.make_async_remote_copy(
            src_ref=kv.at[src, j],
            dst_ref=kv.at[dst, j],
            send_sem=send_sem.at[dst if lane is None else lane, j],
            recv_sem=recv_sem.at[dst, j],
            device_id=(to, h),
            device_id_type=MESH,
        )

    def send(src, dst, j, to, lane=None):
        @pl.when(wanted(to, dst))
        def _():
            move(src, dst, j, to, lane).start()

    def arrived(d, j):
        @pl.when(wanted(s, d))
        def _():
            move(d, d, j, after).wait_recv()

    def sent(d, j, to, lane=None):
        @pl.when(wanted(to, d))
        def _():
            move(d, d, j, to, lane).wait_send()

    for j in range(PIECES):
        send(0, FAR, j, up)

        send(0, 1, j, after)

        @pl.when(z == 0)
        def _():
            send(0, FAR - 1, j, last_col)

    loads[PIECES + 1].wait()
    lengths = doc_in[...]
    count = lengths.shape[1]
    shape = (count, count)
    upto = lax.broadcasted_iota(jnp.int32, shape, 1) <= lax.broadcasted_iota(jnp.int32, shape, 0)
    ends = jnp.sum(
        jnp.where(upto, jnp.broadcast_to(lengths, shape), 0).astype(jnp.float32),
        axis=1,
        keepdims=True,
    ).astype(jnp.int32)
    for i in range(PIECES):
        block = s * PIECES + i
        start = jnp.max(
            jnp.where(ends <= block, ends, 0).astype(jnp.float32), axis=0, keepdims=True
        ).astype(jnp.int32)
        reach[i] = jnp.broadcast_to(block - start, (1, COLS))

    loads[PIECES + 2].wait()
    for i in range(PIECES):
        for g in range(GROUP):
            rows = q_in[i * B : (i + 1) * B, g * HD : (g + 1) * HD]
            scaled = rows.astype(jnp.float32).T * SCALE
            high = scaled.astype(jnp.bfloat16)
            q_t[i, :HD, g * B : (g + 1) * B] = high
            q_t[i, HD:, g * B : (g + 1) * B] = (scaled - high.astype(jnp.float32)).astype(jnp.bfloat16)

    def update(which, chunks, first=False):
        ones = jnp.ones((EXTRA, B), jnp.bfloat16)
        keys, values, pairs = [], [], []
        for d, blocks in chunks:
            n = len(blocks)
            part = kv[d, blocks[0] : blocks[0] + n, 0].reshape(n * B, HD)
            keys.append(jnp.concatenate([part, part], axis=1))
            values += [jnp.concatenate([kv[d, j, 1], ones], axis=0) for j in blocks]
            pairs += [(d, j) for j in blocks]
        keys = jnp.concatenate(keys, axis=0)
        values = jnp.concatenate(values, axis=1)
        queries = [q_t[i] for i in which]
        reaches = [reach[i] for i in which]
        if not first:
            peaks = [top[i] for i in which]
            sums = [acc[i] for i in which]
        products = [jnp.dot(keys, q, preferred_element_type=jnp.float32) for q in queries]
        results = []
        for n, (i, far, product) in enumerate(zip(which, reaches, products)):
            scores, shown = [], []
            for b, (d, j) in enumerate(pairs):
                block = product[b * B : (b + 1) * B]
                delta = PIECES * d + i - j
                show = delta <= far
                if first:
                    key = lax.broadcasted_iota(jnp.int32, (B, COLS), 0) + j * B
                    query = lax.rem(lax.broadcasted_iota(jnp.int32, (B, COLS), 1), B) + i * B
                    block = jnp.where(key <= query, block, NEG)
                    show = show & (delta >= 0)
                shown.append(show)
                scores.append(block)
            peak = None
            for block, show in zip(scores, shown):
                here = jnp.where(show, jnp.max(block, axis=0, keepdims=True), NEG)
                peak = here if peak is None else jnp.maximum(peak, here)
            if not first:
                peak = jnp.maximum(peaks[n], peak)
                shrink = jnp.exp2(peaks[n] - peak)
            weights = [
                jnp.exp2(block - jnp.where(show, peak, -NEG)).astype(jnp.bfloat16)
                for block, show in zip(scores, shown)
            ]
            added = jnp.dot(
                values, jnp.concatenate(weights, axis=0), preferred_element_type=jnp.float32
            )
            results.append((peak, added if first else sums[n] * shrink + added))
        for i, (peak, total) in zip(which, results):
            top[i] = peak
            acc[i] = total
        return [total for _, total in results]

    every = tuple(range(PIECES))
    half = PIECES // 2

    @pl.loop(0, PIECES // 2)
    def _(i):
        update((2 * i, 2 * i + 1), [(0, every)], first=True)

    far_steps = 4 * PIECES
    lag = jnp.where(z < 2, LAG_WRAP, LAG)
    work_from = PIECES - 1 + lag

    @pl.loop(0, 4 * PIECES - 1 + LAG_WRAP)
    def _(t):
        j = lax.rem(t, PIECES)
        d = FAR - t // PIECES

        @pl.when(t < far_steps)
        def _():
            arrived(d, j)

            @pl.when((d > 5) & ((d < FAR) | (z != 0)))
            def _():
                send(d, d - 1, j, before)

            @pl.when((d == 5) & (z == 1))
            def _():
                send(5, 4, j, before, 0)

        u = t - lag
        near = u // PIECES + 1
        k = lax.rem(u + PIECES, PIECES)

        @pl.when((u >= 0) & (u < 4 * PIECES - 1))
        def _():
            arrived(near, k)

            @pl.when((near < 3) | ((near == 3) & (z != ROWS - 1)))
            def _():
                send(near, near + 1, k, after)

        w = t - work_from

        @pl.when((w >= 0) & (w < 3 * PIECES))
        def _():
            p = w // PIECES + 1
            i = 2 * lax.rem(w, 2)
            chunk = jnp.where(lax.rem(w, PIECES) < 2, FAR + 1 - p, p)
            update((i, i + 1), [(chunk, every)])

    @pl.loop(0, PIECES // 2)
    def _(i):
        update((2 * i, 2 * i + 1), [(5, every[:half]), (4, every[:half])])

    arrived(4, PIECES - 1)

    own = pltpu.make_async_copy(
        out_buf.at[h],
        out_ref.at[:, pl.ds(pl.multiple_of(h * COLS, COLS), COLS)],
        load_sem.at[0],
    )
    for hops in ((2, 1), (3, 0)):
        which = [lax.rem(x + hop, chips) for hop in hops]
        totals = update(which, [(5, every[half:]), (4, every[half:])])
        for hop, i, total in zip(hops, which, totals):
            final = (total[:HD] * (1.0 / total[HD : HD + 1])).astype(jnp.bfloat16)
            part = B // CORES
            for g in range(GROUP):
                rows = final[:, g * B : (g + 1) * B].T
                for core in range(CORES):
                    out_buf[i * CORES + core, :, g * HD : (g + 1) * HD] = rows[
                        core * part : (core + 1) * part
                    ]
            for core in range(CORES):
                target = i * CORES + core
                there = pltpu.make_async_remote_copy(
                    src_ref=out_buf.at[target],
                    dst_ref=out_ref.at[:, pl.ds(pl.multiple_of(h * COLS, COLS), COLS)],
                    send_sem=out_send.at[target],
                    recv_sem=out_recv.at[h],
                    device_id=(s, target),
                    device_id_type=MESH,
                )
                if hop:
                    there.start()
                else:

                    @pl.when(h != target)
                    def _():
                        there.start()

                    @pl.when(h == target)
                    def _():
                        own.start()

    @pl.loop(0, PIECES)
    def _(j):
        for d in (1, 2, 3):
            sent(d, j, after)
        for d in (5, 6):
            sent(d, j, before)
        sent(7, j, jnp.where(z == 0, last_col, before))
        sent(FAR, j, up)

        @pl.when(z != ROWS - 1)
        def _():
            sent(4, j, after)

        @pl.when(z == 1)
        def _():
            sent(4, j, before, 0)

    for step in range(1, n_head):
        peer = lax.rem(h + step, n_head)
        other = pltpu.make_async_remote_copy(
            src_ref=out_buf.at[peer],
            dst_ref=out_ref.at[:, pl.ds(pl.multiple_of(peer * COLS, COLS), COLS)],
            send_sem=out_send.at[peer],
            recv_sem=out_recv.at[peer],
            device_id=(s, peer),
            device_id_type=MESH,
        )
        other.wait_send()
        other.wait_recv()
    own.wait()


def body(n_seq, n_head, queries, key_rows, value_rows, doc_blocks):
    tokens = queries.shape[0]
    part = tokens // n_head
    any_space = pl.BlockSpec(memory_space=pl.ANY)
    bf16, f32 = jnp.bfloat16, jnp.float32
    pairs = tokens * PIECES * FAR * B * GROUP
    return pl.pallas_call(
        functools.partial(kernel, n_seq, n_head),
        out_shape=jax.ShapeDtypeStruct((part, n_head * COLS), bf16),
        in_specs=[any_space] * 4,
        out_specs=any_space,
        scratch_shapes=[
            pltpu.VMEM((tokens, COLS), bf16),
            pltpu.VMEM((tokens, HD), bf16),
            pltpu.VMEM((1, doc_blocks.shape[0]), jnp.int32),
            pltpu.VMEM((PIECES, 2 * HD, COLS), bf16),
            pltpu.VMEM((FAR + 1, PIECES, 2, B, HD), bf16),
            pltpu.VMEM((PIECES, 1, COLS), f32),
            pltpu.VMEM((PIECES, HD + EXTRA, COLS), f32),
            pltpu.VMEM((PIECES, 1, COLS), jnp.int32),
            pltpu.VMEM((n_head, part, COLS), bf16),
            pltpu.SemaphoreType.DMA((PIECES + 3,)),
            pltpu.SemaphoreType.DMA((FAR + 1, PIECES)),
            pltpu.SemaphoreType.DMA((FAR + 1, PIECES)),
            pltpu.SemaphoreType.DMA((n_head,)),
            pltpu.SemaphoreType.DMA((n_head,)),
        ],
        compiler_params=pltpu.CompilerParams(
            collective_id=0, has_side_effects=True, vmem_limit_bytes=62 << 20
        ),
        cost_estimate=pl.CostEstimate(
            flops=4 * pairs * HD, bytes_accessed=2 << 20, transcendentals=pairs
        ),
        name="attend",
    )(queries, key_rows, value_rows, doc_blocks.reshape(1, -1))


def solution(mesh):
    in_specs = (P("seq", "head"), P("seq", "head"), P("seq", "head"), P())
    out_specs = P(("seq", "head"), None)
    return jax.shard_map(
        functools.partial(body, mesh.shape["seq"], mesh.shape["head"]),
        mesh=mesh,
        in_specs=in_specs,
        out_specs=out_specs,
        check_vma=False,
    )
```

```python
import functools
import math

import jax
import jax.numpy as jnp
from jax import lax
from jax.experimental import pallas as pl
from jax.experimental.pallas import tpu as pltpu
from jax.sharding import PartitionSpec as P

HD = 128
B = 128
GROUP = 4
ROWS = 8
PIECES = 4
FAR = 8
CORES = 2
COLS = GROUP * B
EXTRA = 16
LAG = 2
LAG_WRAP = 4

NEG = -1e30
SCALE = math.log2(math.e) / math.sqrt(HD)
MESH = pl.DeviceIdType.MESH


def kernel(
    n_seq,
    n_head,
    q_hbm,
    k_hbm,
    v_hbm,
    doc_hbm,
    out_ref,
    q_in,
    v_in,
    doc_in,
    q_t,
    kv,
    top,
    acc,
    reach,
    out_buf,
    load_sem,
    send_sem,
    recv_sem,
    out_send,
    out_recv,
):
    s = lax.axis_index("seq")
    h = lax.axis_index("head")
    z = lax.rem(s, ROWS)
    chips = n_head // CORES
    x = h // CORES

    def ring(distance):
        return lax.rem(s + distance + n_seq, n_seq)

    after, before = ring(1), ring(-1)
    up, down = ring(ROWS), ring(-ROWS)
    first_col = ring(-(ROWS - 1))
    last_col = ring(ROWS - 1)

    def wanted(who, d):
        beyond = d - who
        return (beyond <= 0) | (beyond == ROWS - 2) | (beyond == ROWS - 1)

    @pl.when(s < ROWS)
    def _():
        @pl.loop(1, FAR + 1)
        def _(d):
            kv[d] = jnp.zeros(kv.shape[1:], kv.dtype)

    loads = [
        pltpu.make_async_copy(
            k_hbm.at[pl.ds(j * B, B), :], kv.at[0, j, 0], load_sem.at[j]
        )
        for j in range(PIECES)
    ]
    loads.append(pltpu.make_async_copy(v_hbm, v_in, load_sem.at[PIECES]))
    loads.append(pltpu.make_async_copy(doc_hbm, doc_in, load_sem.at[PIECES + 1]))
    loads.append(pltpu.make_async_copy(q_hbm, q_in, load_sem.at[PIECES + 2]))
    barrier = pltpu.get_barrier_semaphore()

    def greet(to_seq, to_head):
        pl.semaphore_signal(barrier, inc=1, device_id=(to_seq, to_head), device_id_type=MESH)

    for to in (after, before, up, down):
        greet(to, h)
    for step in range(1, n_head):
        greet(s, lax.rem(h + step, n_head))

    @pl.when(z == ROWS - 1)
    def _():
        greet(first_col, h)

    @pl.when(z == 0)
    def _():
        greet(last_col, h)

    for copy in loads:
        copy.start()
    for copy in loads[: PIECES + 1]:
        copy.wait()
    for j in range(PIECES):
        kv[0, j, 1] = v_in[pl.ds(j * B, B), :].T

    edge = jnp.where((z == 0) | (z == ROWS - 1), 1, 0)
    pl.semaphore_wait(barrier, 4 + n_head - 1 + edge)

    def move(src, dst, j, to, lane=None):
        return pltpu.make_async_remote_copy(
            src_ref=kv.at[src, j],
            dst_ref=kv.at[dst, j],
            send_sem=send_sem.at[dst if lane is None else lane, j],
            recv_sem=recv_sem.at[dst, j],
            device_id=(to, h),
            device_id_type=MESH,
        )

    def send(src, dst, j, to, lane=None):
        @pl.when(wanted(to, dst))
        def _():
            move(src, dst, j, to, lane).start()

    def arrived(d, j):
        @pl.when(wanted(s, d))
        def _():
            move(d, d, j, after).wait_recv()

    def sent(d, j, to, lane=None):
        @pl.when(wanted(to, d))
        def _():
            move(d, d, j, to, lane).wait_send()

    for j in range(PIECES):
        send(0, FAR, j, up)

        send(0, 1, j, after)

        @pl.when(z == 0)
        def _():
            send(0, FAR - 1, j, last_col)

    loads[PIECES + 1].wait()
    lengths = doc_in[...]
    count = lengths.shape[1]
    shape = (count, count)
    upto = lax.broadcasted_iota(jnp.int32, shape, 1) <= lax.broadcasted_iota(jnp.int32, shape, 0)
    ends = jnp.sum(
        jnp.where(upto, jnp.broadcast_to(lengths, shape), 0).astype(jnp.float32),
        axis=1,
        keepdims=True,
    ).astype(jnp.int32)
    for i in range(PIECES):
        block = s * PIECES + i
        start = jnp.max(
            jnp.where(ends <= block, ends, 0).astype(jnp.float32), axis=0, keepdims=True
        ).astype(jnp.int32)
        reach[i] = jnp.broadcast_to(block - start, (1, COLS))

    loads[PIECES + 2].wait()
    for i in range(PIECES):
        for g in range(GROUP):
            rows = q_in[i * B : (i + 1) * B, g * HD : (g + 1) * HD]
            scaled = rows.astype(jnp.float32).T * SCALE
            high = scaled.astype(jnp.bfloat16)
            q_t[i, :HD, g * B : (g + 1) * B] = high
            q_t[i, HD:, g * B : (g + 1) * B] = (scaled - high.astype(jnp.float32)).astype(jnp.bfloat16)

    def update(which, chunks, first=False):
        ones = jnp.ones((EXTRA, B), jnp.bfloat16)
        keys, values, pairs = [], [], []
        for d, blocks in chunks:
            n = len(blocks)
            part = kv[d, blocks[0] : blocks[0] + n, 0].reshape(n * B, HD)
            keys.append(jnp.concatenate([part, part], axis=1))
            values += [jnp.concatenate([kv[d, j, 1], ones], axis=0) for j in blocks]
            pairs += [(d, j) for j in blocks]
        keys = jnp.concatenate(keys, axis=0)
        values = jnp.concatenate(values, axis=1)
        queries = [q_t[i] for i in which]
        reaches = [reach[i] for i in which]
        if not first:
            peaks = [top[i] for i in which]
            sums = [acc[i] for i in which]
        products = [jnp.dot(keys, q, preferred_element_type=jnp.float32) for q in queries]
        results = []
        for n, (i, far, product) in enumerate(zip(which, reaches, products)):
            scores, shown = [], []
            for b, (d, j) in enumerate(pairs):
                block = product[b * B : (b + 1) * B]
                delta = PIECES * d + i - j
                show = delta <= far
                if first:
                    key = lax.broadcasted_iota(jnp.int32, (B, COLS), 0) + j * B
                    query = lax.rem(lax.broadcasted_iota(jnp.int32, (B, COLS), 1), B) + i * B
                    block = jnp.where(key <= query, block, NEG)
                    show = show & (delta >= 0)
                shown.append(show)
                scores.append(block)
            peak = None
            for block, show in zip(scores, shown):
                here = jnp.where(show, jnp.max(block, axis=0, keepdims=True), NEG)
                peak = here if peak is None else jnp.maximum(peak, here)
            if not first:
                peak = jnp.maximum(peaks[n], peak)
                shrink = jnp.exp2(peaks[n] - peak)
            weights = [
                jnp.exp2(block - jnp.where(show, peak, -NEG)).astype(jnp.bfloat16)
                for block, show in zip(scores, shown)
            ]
            added = jnp.dot(
                values, jnp.concatenate(weights, axis=0), preferred_element_type=jnp.float32
            )
            results.append((peak, added if first else sums[n] * shrink + added))
        for i, (peak, total) in zip(which, results):
            top[i] = peak
            acc[i] = total
        return [total for _, total in results]

    every = tuple(range(PIECES))
    half = PIECES // 2

    @pl.loop(0, PIECES // 2)
    def _(i):
        update((2 * i, 2 * i + 1), [(0, every)], first=True)

    far_steps = 4 * PIECES
    lag = jnp.where(z < 2, LAG_WRAP, LAG)
    work_from = lag + 1

    @pl.loop(0, 3 * PIECES + 1 + LAG_WRAP)
    def _(t):
        j = lax.rem(t, PIECES)
        d = FAR - t // PIECES

        @pl.when((t < far_steps) & ((d < FAR) | (z != 0)))
        def _():
            arrived(d, j)

            @pl.when(d > 5)
            def _():
                send(d, d - 1, j, before)

            @pl.when((d == 5) & (z == 1))
            def _():
                send(5, 4, j, before, 0)

        @pl.when((z == 0) & (t == work_from))
        def _():
            for k in range(PIECES):
                arrived(FAR, k)

        u = t - lag
        near = u // PIECES + 1
        k = lax.rem(u + PIECES, PIECES)

        @pl.when((u >= 0) & (u < 3 * PIECES))
        def _():
            arrived(near, k)

            @pl.when((near < 3) | (z != ROWS - 1))
            def _():
                send(near, near + 1, k, after)

        w = t - work_from

        @pl.when((w >= 0) & (w < 3 * PIECES))
        def _():
            p = w // PIECES + 1
            i = 2 * lax.rem(w, 2)
            chunk = jnp.where(lax.rem(w, PIECES) < 2, FAR + 1 - p, p)
            update((i, i + 1), [(chunk, every)])

    @pl.loop(0, PIECES // 2)
    def _(i):
        update((2 * i, 2 * i + 1), [(5, every)])

    for j in every[:half]:
        arrived(4, j)

    @pl.loop(0, PIECES // 2)
    def _(i):
        update((2 * i, 2 * i + 1), [(4, every[:half])])

    for j in every[half:]:
        arrived(4, j)

    own = pltpu.make_async_copy(
        out_buf.at[h],
        out_ref.at[:, pl.ds(pl.multiple_of(h * COLS, COLS), COLS)],
        load_sem.at[0],
    )
    for hops in ((2, 1), (3, 0)):
        which = [lax.rem(x + hop, chips) for hop in hops]
        totals = update(which, [(4, every[half:])])
        for hop, i, total in zip(hops, which, totals):
            final = (total[:HD] * (1.0 / total[HD : HD + 1])).astype(jnp.bfloat16)
            part = B // CORES
            for g in range(GROUP):
                rows = final[:, g * B : (g + 1) * B].T
                for core in range(CORES):
                    out_buf[i * CORES + core, :, g * HD : (g + 1) * HD] = rows[
                        core * part : (core + 1) * part
                    ]
            for core in range(CORES):
                target = i * CORES + core
                there = pltpu.make_async_remote_copy(
                    src_ref=out_buf.at[target],
                    dst_ref=out_ref.at[:, pl.ds(pl.multiple_of(h * COLS, COLS), COLS)],
                    send_sem=out_send.at[target],
                    recv_sem=out_recv.at[h],
                    device_id=(s, target),
                    device_id_type=MESH,
                )
                if hop:
                    there.start()
                else:

                    @pl.when(h != target)
                    def _():
                        there.start()

                    @pl.when(h == target)
                    def _():
                        own.start()

    @pl.loop(0, PIECES)
    def _(j):
        for d in (1, 2, 3):
            sent(d, j, after)
        for d in (5, 6):
            sent(d, j, before)
        sent(7, j, jnp.where(z == 0, last_col, before))
        sent(FAR, j, up)

        @pl.when(z != ROWS - 1)
        def _():
            sent(4, j, after)

        @pl.when(z == 1)
        def _():
            sent(4, j, before, 0)

    for step in range(1, n_head):
        peer = lax.rem(h + step, n_head)
        other = pltpu.make_async_remote_copy(
            src_ref=out_buf.at[peer],
            dst_ref=out_ref.at[:, pl.ds(pl.multiple_of(peer * COLS, COLS), COLS)],
            send_sem=out_send.at[peer],
            recv_sem=out_recv.at[peer],
            device_id=(s, peer),
            device_id_type=MESH,
        )
        other.wait_send()
        other.wait_recv()
    own.wait()


def body(n_seq, n_head, queries, key_rows, value_rows, doc_blocks):
    tokens = queries.shape[0]
    part = tokens // n_head
    any_space = pl.BlockSpec(memory_space=pl.ANY)
    bf16, f32 = jnp.bfloat16, jnp.float32
    pairs = tokens * PIECES * FAR * B * GROUP
    return pl.pallas_call(
        functools.partial(kernel, n_seq, n_head),
        out_shape=jax.ShapeDtypeStruct((part, n_head * COLS), bf16),
        in_specs=[any_space] * 4,
        out_specs=any_space,
        scratch_shapes=[
            pltpu.VMEM((tokens, COLS), bf16),
            pltpu.VMEM((tokens, HD), bf16),
            pltpu.VMEM((1, doc_blocks.shape[0]), jnp.int32),
            pltpu.VMEM((PIECES, 2 * HD, COLS), bf16),
            pltpu.VMEM((FAR + 1, PIECES, 2, B, HD), bf16),
            pltpu.VMEM((PIECES, 1, COLS), f32),
            pltpu.VMEM((PIECES, HD + EXTRA, COLS), f32),
            pltpu.VMEM((PIECES, 1, COLS), jnp.int32),
            pltpu.VMEM((n_head, part, COLS), bf16),
            pltpu.SemaphoreType.DMA((PIECES + 3,)),
            pltpu.SemaphoreType.DMA((FAR + 1, PIECES)),
            pltpu.SemaphoreType.DMA((FAR + 1, PIECES)),
            pltpu.SemaphoreType.DMA((n_head,)),
            pltpu.SemaphoreType.DMA((n_head,)),
        ],
        compiler_params=pltpu.CompilerParams(
            collective_id=0, has_side_effects=True, vmem_limit_bytes=62 << 20
        ),
        cost_estimate=pl.CostEstimate(
            flops=4 * pairs * HD, bytes_accessed=2 << 20, transcendentals=pairs
        ),
        name="attend",
    )(queries, key_rows, value_rows, doc_blocks.reshape(1, -1))


def solution(mesh):
    in_specs = (P("seq", "head"), P("seq", "head"), P("seq", "head"), P())
    out_specs = P(("seq", "head"), None)
    return jax.shard_map(
        functools.partial(body, mesh.shape["seq"], mesh.shape["head"]),
        mesh=mesh,
        in_specs=in_specs,
        out_specs=out_specs,
        check_vma=False,
    )
```

```python
import functools
import math

import jax
import jax.numpy as jnp
from jax import lax
from jax.experimental import pallas as pl
from jax.experimental.pallas import tpu as pltpu
from jax.sharding import PartitionSpec as P

HD = 128
B = 128
GROUP = 4
ROWS = 8
PIECES = 4
FAR = 8
CORES = 2
COLS = GROUP * B
EXTRA = 16
WINDOW = PIECES // 2
LAG = 2
LAG_WRAP = 4

NEG = -1e30
SCALE = math.log2(math.e) / math.sqrt(HD)
MESH = pl.DeviceIdType.MESH


def kernel(
    n_seq,
    n_head,
    q_hbm,
    k_hbm,
    v_hbm,
    doc_hbm,
    out_ref,
    q_in,
    v_in,
    doc_in,
    q_t,
    kv,
    top,
    acc,
    reach,
    out_buf,
    load_sem,
    send_sem,
    recv_sem,
    out_send,
    out_recv,
):
    s = lax.axis_index("seq")
    h = lax.axis_index("head")
    z = lax.rem(s, ROWS)
    chips = n_head // CORES
    x = h // CORES

    def ring(distance):
        return lax.rem(s + distance + n_seq, n_seq)

    after, before = ring(1), ring(-1)
    up, down = ring(ROWS), ring(-ROWS)
    first_col = ring(-(ROWS - 1))
    last_col = ring(ROWS - 1)

    def wanted(who, d):
        beyond = d - who
        return (beyond <= 0) | (beyond == ROWS - 2) | (beyond == ROWS - 1)

    @pl.when(s < ROWS)
    def _():
        @pl.loop(1, FAR + 1)
        def _(d):
            kv[d] = jnp.zeros(kv.shape[1:], kv.dtype)

    loads = [
        pltpu.make_async_copy(
            k_hbm.at[pl.ds(j * B, B), :], kv.at[0, j, 0], load_sem.at[j]
        )
        for j in range(PIECES)
    ]
    loads.append(pltpu.make_async_copy(v_hbm, v_in, load_sem.at[PIECES]))
    loads.append(pltpu.make_async_copy(doc_hbm, doc_in, load_sem.at[PIECES + 1]))
    loads.append(pltpu.make_async_copy(q_hbm, q_in, load_sem.at[PIECES + 2]))
    barrier = pltpu.get_barrier_semaphore()

    def greet(to_seq, to_head):
        pl.semaphore_signal(barrier, inc=1, device_id=(to_seq, to_head), device_id_type=MESH)

    for to in (after, before, up, down):
        greet(to, h)
    for step in range(1, n_head):
        greet(s, lax.rem(h + step, n_head))

    @pl.when(z == ROWS - 1)
    def _():
        greet(first_col, h)

    @pl.when(z == 0)
    def _():
        greet(last_col, h)

    for copy in loads:
        copy.start()
    for copy in loads[: PIECES + 1]:
        copy.wait()
    for j in range(PIECES):
        kv[0, j, 1] = v_in[pl.ds(j * B, B), :].T

    edge = jnp.where((z == 0) | (z == ROWS - 1), 1, 0)
    pl.semaphore_wait(barrier, 4 + n_head - 1 + edge)

    def move(src, dst, j, to, lane=None):
        return pltpu.make_async_remote_copy(
            src_ref=kv.at[src, j],
            dst_ref=kv.at[dst, j],
            send_sem=send_sem.at[dst if lane is None else lane, j],
            recv_sem=recv_sem.at[dst, j],
            device_id=(to, h),
            device_id_type=MESH,
        )

    def send(src, dst, j, to, lane=None):
        @pl.when(wanted(to, dst))
        def _():
            move(src, dst, j, to, lane).start()

    def arrived(d, j):
        @pl.when(wanted(s, d))
        def _():
            move(d, d, j, after).wait_recv()

    def sent(d, j, to, lane=None):
        @pl.when(wanted(to, d))
        def _():
            move(d, d, j, to, lane).wait_send()

    for j in range(PIECES):
        if j < WINDOW:
            send(0, FAR, j, up)
        else:

            @pl.when(z == 0)
            def _():
                send(0, FAR, j, up)

        send(0, 1, j, after)

        @pl.when(z == 0)
        def _():
            send(0, FAR - 1, j, last_col)

    loads[PIECES + 1].wait()
    lengths = doc_in[...]
    count = lengths.shape[1]
    shape = (count, count)
    upto = lax.broadcasted_iota(jnp.int32, shape, 1) <= lax.broadcasted_iota(jnp.int32, shape, 0)
    ends = jnp.sum(
        jnp.where(upto, jnp.broadcast_to(lengths, shape), 0).astype(jnp.float32),
        axis=1,
        keepdims=True,
    ).astype(jnp.int32)
    for i in range(PIECES):
        block = s * PIECES + i
        start = jnp.max(
            jnp.where(ends <= block, ends, 0).astype(jnp.float32), axis=0, keepdims=True
        ).astype(jnp.int32)
        reach[i] = jnp.broadcast_to(block - start, (1, COLS))

    loads[PIECES + 2].wait()
    for i in range(PIECES):
        for g in range(GROUP):
            rows = q_in[i * B : (i + 1) * B, g * HD : (g + 1) * HD]
            scaled = rows.astype(jnp.float32).T * SCALE
            high = scaled.astype(jnp.bfloat16)
            q_t[i, :HD, g * B : (g + 1) * B] = high
            q_t[i, HD:, g * B : (g + 1) * B] = (scaled - high.astype(jnp.float32)).astype(jnp.bfloat16)

    def update(which, chunks, first=False):
        ones = jnp.ones((EXTRA, B), jnp.bfloat16)
        keys, values, pairs = [], [], []
        for d, blocks in chunks:
            n = len(blocks)
            part = kv[d, blocks[0] : blocks[0] + n, 0].reshape(n * B, HD)
            keys.append(jnp.concatenate([part, part], axis=1))
            values += [jnp.concatenate([kv[d, j, 1], ones], axis=0) for j in blocks]
            pairs += [(d, j) for j in blocks]
        keys = jnp.concatenate(keys, axis=0)
        values = jnp.concatenate(values, axis=1)
        queries = [q_t[i] for i in which]
        reaches = [reach[i] for i in which]
        if not first:
            peaks = [top[i] for i in which]
            sums = [acc[i] for i in which]
        products = [jnp.dot(keys, q, preferred_element_type=jnp.float32) for q in queries]
        results = []
        for n, (i, far, product) in enumerate(zip(which, reaches, products)):
            scores, shown = [], []
            for b, (d, j) in enumerate(pairs):
                block = product[b * B : (b + 1) * B]
                delta = PIECES * d + i - j
                show = delta <= far
                if first:
                    key = lax.broadcasted_iota(jnp.int32, (B, COLS), 0) + j * B
                    query = lax.rem(lax.broadcasted_iota(jnp.int32, (B, COLS), 1), B) + i * B
                    block = jnp.where(key <= query, block, NEG)
                    show = show & (delta >= 0)
                shown.append(show)
                scores.append(block)
            peak = None
            for block, show in zip(scores, shown):
                here = jnp.where(show, jnp.max(block, axis=0, keepdims=True), NEG)
                peak = here if peak is None else jnp.maximum(peak, here)
            if not first:
                peak = jnp.maximum(peaks[n], peak)
                shrink = jnp.exp2(peaks[n] - peak)
            weights = [
                jnp.exp2(block - jnp.where(show, peak, -NEG)).astype(jnp.bfloat16)
                for block, show in zip(scores, shown)
            ]
            added = jnp.dot(
                values, jnp.concatenate(weights, axis=0), preferred_element_type=jnp.float32
            )
            results.append((peak, added if first else sums[n] * shrink + added))
        for i, (peak, total) in zip(which, results):
            top[i] = peak
            acc[i] = total
        return [total for _, total in results]

    every = tuple(range(PIECES))
    half = PIECES // 2

    @pl.loop(0, PIECES // 2)
    def _(i):
        update((2 * i, 2 * i + 1), [(0, every)], first=True)

        @pl.when(z != 0)
        def _():
            sent(FAR, i, up)
            send(0, FAR, i + WINDOW, up)

    far_steps = 4 * PIECES
    lag = jnp.where(z < 2, LAG_WRAP, LAG)
    work_from = lag + 1

    @pl.loop(0, 3 * PIECES + 1 + LAG_WRAP)
    def _(t):
        j = lax.rem(t, PIECES)
        d = FAR - t // PIECES

        @pl.when((t < far_steps) & ((d < FAR) | (z != 0)))
        def _():
            arrived(d, j)

            @pl.when(d > 5)
            def _():
                send(d, d - 1, j, before)

            @pl.when((d == 5) & (z == 1))
            def _():
                send(5, 4, j, before, 0)

        @pl.when((z == 0) & (t == work_from))
        def _():
            for k in range(PIECES):
                arrived(FAR, k)

        u = t - lag
        near = u // PIECES + 1
        k = lax.rem(u + PIECES, PIECES)

        @pl.when((u >= 0) & (u < 3 * PIECES))
        def _():
            arrived(near, k)

            @pl.when((near < 3) | (z != ROWS - 1))
            def _():
                send(near, near + 1, k, after)

        w = t - work_from

        @pl.when((w >= 0) & (w < 3 * PIECES))
        def _():
            p = w // PIECES + 1
            i = 2 * lax.rem(w, 2)
            chunk = jnp.where(lax.rem(w, PIECES) < 2, FAR + 1 - p, p)
            update((i, i + 1), [(chunk, every)])

    @pl.loop(0, PIECES // 2)
    def _(i):
        update((2 * i, 2 * i + 1), [(5, every)])

    for j in every[:half]:
        arrived(4, j)

    @pl.loop(0, PIECES // 2)
    def _(i):
        update((2 * i, 2 * i + 1), [(4, every[:half])])

    for j in every[half:]:
        arrived(4, j)

    own = pltpu.make_async_copy(
        out_buf.at[h],
        out_ref.at[:, pl.ds(pl.multiple_of(h * COLS, COLS), COLS)],
        load_sem.at[0],
    )
    for hops in ((2, 1), (3, 0)):
        which = [lax.rem(x + hop, chips) for hop in hops]
        totals = update(which, [(4, every[half:])])
        for hop, i, total in zip(hops, which, totals):
            final = (total[:HD] * (1.0 / total[HD : HD + 1])).astype(jnp.bfloat16)
            part = B // CORES
            for g in range(GROUP):
                rows = final[:, g * B : (g + 1) * B].T
                for core in range(CORES):
                    out_buf[i * CORES + core, :, g * HD : (g + 1) * HD] = rows[
                        core * part : (core + 1) * part
                    ]
            for core in range(CORES):
                target = i * CORES + core
                there = pltpu.make_async_remote_copy(
                    src_ref=out_buf.at[target],
                    dst_ref=out_ref.at[:, pl.ds(pl.multiple_of(h * COLS, COLS), COLS)],
                    send_sem=out_send.at[target],
                    recv_sem=out_recv.at[h],
                    device_id=(s, target),
                    device_id_type=MESH,
                )
                if hop:
                    there.start()
                else:

                    @pl.when(h != target)
                    def _():
                        there.start()

                    @pl.when(h == target)
                    def _():
                        own.start()

    @pl.loop(0, PIECES)
    def _(j):
        for d in (1, 2, 3):
            sent(d, j, after)
        for d in (5, 6):
            sent(d, j, before)
        sent(7, j, jnp.where(z == 0, last_col, before))

        @pl.when((z == 0) | (j >= PIECES - WINDOW))
        def _():
            sent(FAR, j, up)

        @pl.when(z != ROWS - 1)
        def _():
            sent(4, j, after)

        @pl.when(z == 1)
        def _():
            sent(4, j, before, 0)

    for step in range(1, n_head):
        peer = lax.rem(h + step, n_head)
        other = pltpu.make_async_remote_copy(
            src_ref=out_buf.at[peer],
            dst_ref=out_ref.at[:, pl.ds(pl.multiple_of(peer * COLS, COLS), COLS)],
            send_sem=out_send.at[peer],
            recv_sem=out_recv.at[peer],
            device_id=(s, peer),
            device_id_type=MESH,
        )
        other.wait_send()
        other.wait_recv()
    own.wait()


def body(n_seq, n_head, queries, key_rows, value_rows, doc_blocks):
    tokens = queries.shape[0]
    part = tokens // n_head
    any_space = pl.BlockSpec(memory_space=pl.ANY)
    bf16, f32 = jnp.bfloat16, jnp.float32
    pairs = tokens * PIECES * FAR * B * GROUP
    return pl.pallas_call(
        functools.partial(kernel, n_seq, n_head),
        out_shape=jax.ShapeDtypeStruct((part, n_head * COLS), bf16),
        in_specs=[any_space] * 4,
        out_specs=any_space,
        scratch_shapes=[
            pltpu.VMEM((tokens, COLS), bf16),
            pltpu.VMEM((tokens, HD), bf16),
            pltpu.VMEM((1, doc_blocks.shape[0]), jnp.int32),
            pltpu.VMEM((PIECES, 2 * HD, COLS), bf16),
            pltpu.VMEM((FAR + 1, PIECES, 2, B, HD), bf16),
            pltpu.VMEM((PIECES, 1, COLS), f32),
            pltpu.VMEM((PIECES, HD + EXTRA, COLS), f32),
            pltpu.VMEM((PIECES, 1, COLS), jnp.int32),
            pltpu.VMEM((n_head, part, COLS), bf16),
            pltpu.SemaphoreType.DMA((PIECES + 3,)),
            pltpu.SemaphoreType.DMA((FAR + 1, PIECES)),
            pltpu.SemaphoreType.DMA((FAR + 1, PIECES)),
            pltpu.SemaphoreType.DMA((n_head,)),
            pltpu.SemaphoreType.DMA((n_head,)),
        ],
        compiler_params=pltpu.CompilerParams(
            collective_id=0, has_side_effects=True, vmem_limit_bytes=62 << 20
        ),
        cost_estimate=pl.CostEstimate(
            flops=4 * pairs * HD, bytes_accessed=2 << 20, transcendentals=pairs
        ),
        name="attend",
    )(queries, key_rows, value_rows, doc_blocks.reshape(1, -1))


def solution(mesh):
    in_specs = (P("seq", "head"), P("seq", "head"), P("seq", "head"), P())
    out_specs = P(("seq", "head"), None)
    return jax.shard_map(
        functools.partial(body, mesh.shape["seq"], mesh.shape["head"]),
        mesh=mesh,
        in_specs=in_specs,
        out_specs=out_specs,
        check_vma=False,
    )
```

```python
import functools
import math

import jax
import jax.numpy as jnp
from jax import lax
from jax.experimental import pallas as pl
from jax.experimental.pallas import tpu as pltpu
from jax.sharding import PartitionSpec as P

HD = 128
B = 128
GROUP = 4
ROWS = 8
PIECES = 4
FAR = 8
CORES = 2
COLS = GROUP * B
EXTRA = 16
LAG = 2
LAG_WRAP = 4

NEG = -1e30
SCALE = math.log2(math.e) / math.sqrt(HD)
MESH = pl.DeviceIdType.MESH


def kernel(
    n_seq,
    n_head,
    q_hbm,
    k_hbm,
    v_hbm,
    doc_hbm,
    out_ref,
    q_in,
    v_in,
    doc_in,
    q_t,
    kv,
    top,
    acc,
    reach,
    out_buf,
    load_sem,
    send_sem,
    recv_sem,
    out_send,
    out_recv,
):
    s = lax.axis_index("seq")
    h = lax.axis_index("head")
    z = lax.rem(s, ROWS)
    chips = n_head // CORES
    x = h // CORES

    def ring(distance):
        return lax.rem(s + distance + n_seq, n_seq)

    after, before = ring(1), ring(-1)
    up, down = ring(ROWS), ring(-ROWS)
    first_col = ring(-(ROWS - 1))
    last_col = ring(ROWS - 1)

    def wanted(who, d):
        beyond = d - who
        return (beyond <= 0) | (beyond == ROWS - 2) | (beyond == ROWS - 1)

    @pl.when(s < ROWS)
    def _():
        @pl.loop(1, FAR + 1)
        def _(d):
            kv[d] = jnp.zeros(kv.shape[1:], kv.dtype)

    loads = [
        pltpu.make_async_copy(
            k_hbm.at[pl.ds(j * B, B), :], kv.at[0, j, 0], load_sem.at[j]
        )
        for j in range(PIECES)
    ]
    loads.append(pltpu.make_async_copy(v_hbm, v_in, load_sem.at[PIECES]))
    loads.append(pltpu.make_async_copy(doc_hbm, doc_in, load_sem.at[PIECES + 1]))
    loads.append(pltpu.make_async_copy(q_hbm, q_in, load_sem.at[PIECES + 2]))
    barrier = pltpu.get_barrier_semaphore()

    def greet(to_seq, to_head):
        pl.semaphore_signal(barrier, inc=1, device_id=(to_seq, to_head), device_id_type=MESH)

    for to in (after, before, up, down):
        greet(to, h)
    for step in range(1, n_head):
        greet(s, lax.rem(h + step, n_head))

    @pl.when(z == ROWS - 1)
    def _():
        greet(first_col, h)

    @pl.when(z == 0)
    def _():
        greet(last_col, h)

    for copy in loads:
        copy.start()
    for copy in loads[: PIECES + 1]:
        copy.wait()
    for j in range(PIECES):
        kv[0, j, 1] = v_in[pl.ds(j * B, B), :].T

    edge = jnp.where((z == 0) | (z == ROWS - 1), 1, 0)
    pl.semaphore_wait(barrier, 4 + n_head - 1 + edge)

    def move(src, dst, j, to, lane=None):
        return pltpu.make_async_remote_copy(
            src_ref=kv.at[src, j],
            dst_ref=kv.at[dst, j],
            send_sem=send_sem.at[dst if lane is None else lane, j],
            recv_sem=recv_sem.at[dst, j],
            device_id=(to, h),
            device_id_type=MESH,
        )

    def send(src, dst, j, to, lane=None):
        @pl.when(wanted(to, dst))
        def _():
            move(src, dst, j, to, lane).start()

    def arrived(d, j):
        @pl.when(wanted(s, d))
        def _():
            move(d, d, j, after).wait_recv()

    def sent(d, j, to, lane=None):
        @pl.when(wanted(to, d))
        def _():
            move(d, d, j, to, lane).wait_send()

    for j in range(PIECES):
        send(0, FAR, j, up)

        send(0, 1, j, after)

        @pl.when(z == 0)
        def _():
            send(0, FAR - 1, j, last_col)

    loads[PIECES + 1].wait()
    lengths = doc_in[...]
    count = lengths.shape[1]
    shape = (count, count)
    upto = lax.broadcasted_iota(jnp.int32, shape, 1) <= lax.broadcasted_iota(jnp.int32, shape, 0)
    ends = jnp.sum(
        jnp.where(upto, jnp.broadcast_to(lengths, shape), 0).astype(jnp.float32),
        axis=1,
        keepdims=True,
    ).astype(jnp.int32)
    for i in range(PIECES):
        block = s * PIECES + i
        start = jnp.max(
            jnp.where(ends <= block, ends, 0).astype(jnp.float32), axis=0, keepdims=True
        ).astype(jnp.int32)
        reach[i] = jnp.broadcast_to(block - start, (1, COLS))

    loads[PIECES + 2].wait()
    for i in range(PIECES):
        for g in range(GROUP):
            rows = q_in[i * B : (i + 1) * B, g * HD : (g + 1) * HD]
            scaled = rows.astype(jnp.float32).T * SCALE
            high = scaled.astype(jnp.bfloat16)
            q_t[i, :HD, g * B : (g + 1) * B] = high
            q_t[i, HD:, g * B : (g + 1) * B] = (scaled - high.astype(jnp.float32)).astype(jnp.bfloat16)

    def update(which, chunks, first=False):
        ones = jnp.ones((EXTRA, B), jnp.bfloat16)
        keys, values, pairs = [], [], []
        for d, blocks in chunks:
            n = len(blocks)
            part = kv[d, blocks[0] : blocks[0] + n, 0].reshape(n * B, HD)
            keys.append(jnp.concatenate([part, part], axis=1))
            values += [jnp.concatenate([kv[d, j, 1], ones], axis=0) for j in blocks]
            pairs += [(d, j) for j in blocks]
        keys = jnp.concatenate(keys, axis=0)
        values = jnp.concatenate(values, axis=1)
        queries = [q_t[i] for i in which]
        reaches = [reach[i] for i in which]
        if not first:
            peaks = [top[i] for i in which]
            sums = [acc[i] for i in which]
        products = [jnp.dot(keys, q, preferred_element_type=jnp.float32) for q in queries]
        results = []
        for n, (i, far, product) in enumerate(zip(which, reaches, products)):
            scores, shown = [], []
            for b, (d, j) in enumerate(pairs):
                block = product[b * B : (b + 1) * B]
                delta = PIECES * d + i - j
                show = delta <= far
                if first:
                    key = lax.broadcasted_iota(jnp.int32, (B, COLS), 0) + j * B
                    query = lax.rem(lax.broadcasted_iota(jnp.int32, (B, COLS), 1), B) + i * B
                    block = jnp.where(key <= query, block, NEG)
                    show = show & (delta >= 0)
                shown.append(show)
                scores.append(block)
            peak = None
            for block, show in zip(scores, shown):
                here = jnp.where(show, jnp.max(block, axis=0, keepdims=True), NEG)
                peak = here if peak is None else jnp.maximum(peak, here)
            if not first:
                peak = jnp.maximum(peaks[n], peak)
                shrink = jnp.exp2(peaks[n] - peak)
            weights = [
                jnp.exp2(block - jnp.where(show, peak, -NEG)).astype(jnp.bfloat16)
                for block, show in zip(scores, shown)
            ]
            added = jnp.dot(
                values, jnp.concatenate(weights, axis=0), preferred_element_type=jnp.float32
            )
            results.append((peak, added if first else sums[n] * shrink + added))
        for i, (peak, total) in zip(which, results):
            top[i] = peak
            acc[i] = total
        return [total for _, total in results]

    every = tuple(range(PIECES))
    half = PIECES // 2

    @pl.loop(0, PIECES // 2)
    def _(i):
        update((2 * i, 2 * i + 1), [(0, every)], first=True)

    far_steps = 4 * PIECES
    lag = jnp.where(z < 2, LAG_WRAP, LAG)
    work_from = lag + 1

    @pl.loop(0, 3 * PIECES + 1 + LAG_WRAP)
    def _(t):
        j = lax.rem(t, PIECES)
        d = FAR - t // PIECES

        @pl.when((t < far_steps) & ((d < FAR) | (z != 0)))
        def _():
            arrived(d, j)

            @pl.when(d > 5)
            def _():
                send(d, d - 1, j, before)

            @pl.when((d == 5) & (z == 1) & (j >= half))
            def _():
                send(5, 4, j, before, 0)

        @pl.when((z == 0) & (t == work_from))
        def _():
            for k in range(PIECES):
                arrived(FAR, k)

        u = t - lag
        near = u // PIECES + 1
        k = lax.rem(u + PIECES, PIECES)

        @pl.when((u >= 0) & (u < 3 * PIECES))
        def _():
            arrived(near, k)

            @pl.when((near < 3) | (z != ROWS - 1) | (k < half))
            def _():
                send(near, near + 1, k, after)

        w = t - work_from

        @pl.when((w >= 0) & (w < 3 * PIECES))
        def _():
            p = w // PIECES + 1
            i = 2 * lax.rem(w, 2)
            chunk = jnp.where(lax.rem(w, PIECES) < 2, FAR + 1 - p, p)
            update((i, i + 1), [(chunk, every)])

    @pl.loop(0, PIECES // 2)
    def _(i):
        update((2 * i, 2 * i + 1), [(5, every)])

    for j in every[:half]:
        arrived(4, j)

    @pl.loop(0, PIECES // 2)
    def _(i):
        update((2 * i, 2 * i + 1), [(4, every[:half])])

    for j in every[half:]:
        arrived(4, j)

    own = pltpu.make_async_copy(
        out_buf.at[h],
        out_ref.at[:, pl.ds(pl.multiple_of(h * COLS, COLS), COLS)],
        load_sem.at[0],
    )
    for hops in ((2, 1), (3, 0)):
        which = [lax.rem(x + hop, chips) for hop in hops]
        totals = update(which, [(4, every[half:])])
        for hop, i, total in zip(hops, which, totals):
            final = (total[:HD] * (1.0 / total[HD : HD + 1])).astype(jnp.bfloat16)
            part = B // CORES
            for g in range(GROUP):
                rows = final[:, g * B : (g + 1) * B].T
                for core in range(CORES):
                    out_buf[i * CORES + core, :, g * HD : (g + 1) * HD] = rows[
                        core * part : (core + 1) * part
                    ]
            for core in range(CORES):
                target = i * CORES + core
                there = pltpu.make_async_remote_copy(
                    src_ref=out_buf.at[target],
                    dst_ref=out_ref.at[:, pl.ds(pl.multiple_of(h * COLS, COLS), COLS)],
                    send_sem=out_send.at[target],
                    recv_sem=out_recv.at[h],
                    device_id=(s, target),
                    device_id_type=MESH,
                )
                if hop:
                    there.start()
                else:

                    @pl.when(h != target)
                    def _():
                        there.start()

                    @pl.when(h == target)
                    def _():
                        own.start()

    @pl.loop(0, PIECES)
    def _(j):
        for d in (1, 2, 3):
            sent(d, j, after)
        for d in (5, 6):
            sent(d, j, before)
        sent(7, j, jnp.where(z == 0, last_col, before))
        sent(FAR, j, up)

        @pl.when((z != ROWS - 1) | (j < half))
        def _():
            sent(4, j, after)

        @pl.when((z == 1) & (j >= half))
        def _():
            sent(4, j, before, 0)

    for step in range(1, n_head):
        peer = lax.rem(h + step, n_head)
        other = pltpu.make_async_remote_copy(
            src_ref=out_buf.at[peer],
            dst_ref=out_ref.at[:, pl.ds(pl.multiple_of(peer * COLS, COLS), COLS)],
            send_sem=out_send.at[peer],
            recv_sem=out_recv.at[peer],
            device_id=(s, peer),
            device_id_type=MESH,
        )
        other.wait_send()
        other.wait_recv()
    own.wait()


def body(n_seq, n_head, queries, key_rows, value_rows, doc_blocks):
    tokens = queries.shape[0]
    part = tokens // n_head
    any_space = pl.BlockSpec(memory_space=pl.ANY)
    bf16, f32 = jnp.bfloat16, jnp.float32
    pairs = tokens * PIECES * FAR * B * GROUP
    return pl.pallas_call(
        functools.partial(kernel, n_seq, n_head),
        out_shape=jax.ShapeDtypeStruct((part, n_head * COLS), bf16),
        in_specs=[any_space] * 4,
        out_specs=any_space,
        scratch_shapes=[
            pltpu.VMEM((tokens, COLS), bf16),
            pltpu.VMEM((tokens, HD), bf16),
            pltpu.VMEM((1, doc_blocks.shape[0]), jnp.int32),
            pltpu.VMEM((PIECES, 2 * HD, COLS), bf16),
            pltpu.VMEM((FAR + 1, PIECES, 2, B, HD), bf16),
            pltpu.VMEM((PIECES, 1, COLS), f32),
            pltpu.VMEM((PIECES, HD + EXTRA, COLS), f32),
            pltpu.VMEM((PIECES, 1, COLS), jnp.int32),
            pltpu.VMEM((n_head, part, COLS), bf16),
            pltpu.SemaphoreType.DMA((PIECES + 3,)),
            pltpu.SemaphoreType.DMA((FAR + 1, PIECES)),
            pltpu.SemaphoreType.DMA((FAR + 1, PIECES)),
            pltpu.SemaphoreType.DMA((n_head,)),
            pltpu.SemaphoreType.DMA((n_head,)),
        ],
        compiler_params=pltpu.CompilerParams(
            collective_id=0, has_side_effects=True, vmem_limit_bytes=62 << 20
        ),
        cost_estimate=pl.CostEstimate(
            flops=4 * pairs * HD, bytes_accessed=2 << 20, transcendentals=pairs
        ),
        name="attend",
    )(queries, key_rows, value_rows, doc_blocks.reshape(1, -1))


def solution(mesh):
    in_specs = (P("seq", "head"), P("seq", "head"), P("seq", "head"), P())
    out_specs = P(("seq", "head"), None)
    return jax.shard_map(
        functools.partial(body, mesh.shape["seq"], mesh.shape["head"]),
        mesh=mesh,
        in_specs=in_specs,
        out_specs=out_specs,
        check_vma=False,
    )
```

```python
import functools
import math

import jax
import jax.numpy as jnp
from jax import lax
from jax.experimental import pallas as pl
from jax.experimental.pallas import tpu as pltpu
from jax.sharding import PartitionSpec as P

HD = 128
B = 128
GROUP = 4
ROWS = 8
PIECES = 4
FAR = 8
CORES = 2
COLS = GROUP * B
EXTRA = 16
LAG = 2
LAG_WRAP = 3

NEG = -1e30
SCALE = math.log2(math.e) / math.sqrt(HD)
MESH = pl.DeviceIdType.MESH


def kernel(
    n_seq,
    n_head,
    q_hbm,
    k_hbm,
    v_hbm,
    doc_hbm,
    out_ref,
    q_in,
    v_in,
    doc_in,
    q_t,
    kv,
    top,
    acc,
    reach,
    out_buf,
    load_sem,
    send_sem,
    recv_sem,
    out_send,
    out_recv,
):
    s = lax.axis_index("seq")
    h = lax.axis_index("head")
    z = lax.rem(s, ROWS)
    chips = n_head // CORES
    x = h // CORES

    def ring(distance):
        return lax.rem(s + distance + n_seq, n_seq)

    after, before = ring(1), ring(-1)
    up, down = ring(ROWS), ring(-ROWS)
    first_col = ring(-(ROWS - 1))
    last_col = ring(ROWS - 1)

    def wanted(who, d):
        beyond = d - who
        return (beyond <= 0) | (beyond == ROWS - 2) | (beyond == ROWS - 1)

    @pl.when(s < ROWS)
    def _():
        @pl.loop(1, FAR + 1)
        def _(d):
            kv[d] = jnp.zeros(kv.shape[1:], kv.dtype)

    load_keys = pltpu.make_async_copy(k_hbm, kv.at[0, :, 0], load_sem.at[0])
    load_values = pltpu.make_async_copy(v_hbm, v_in, load_sem.at[1])
    load_lengths = pltpu.make_async_copy(doc_hbm, doc_in, load_sem.at[2])
    load_queries = pltpu.make_async_copy(q_hbm, q_in, load_sem.at[3])
    load_values.start()
    load_keys.start()

    barrier = pltpu.get_barrier_semaphore()

    def greet(to_seq, to_head):
        pl.semaphore_signal(barrier, inc=1, device_id=(to_seq, to_head), device_id_type=MESH)

    for to in (after, before, up, down):
        greet(to, h)
    @pl.when(z == ROWS - 1)
    def _():
        greet(first_col, h)

    @pl.when(z == 0)
    def _():
        greet(last_col, h)

    for step in range(1, n_head):
        greet(s, lax.rem(h + step, n_head))

    load_queries.start()
    load_lengths.start()
    load_values.wait()
    for j in range(PIECES):
        kv[0, j, 1] = v_in[pl.ds(j * B, B), :].T
    load_keys.wait()

    edge = jnp.where((z == 0) | (z == ROWS - 1), 1, 0)
    pl.semaphore_wait(barrier, 4 + n_head - 1 + edge)

    def move(src, dst, j, to, lane=None):
        return pltpu.make_async_remote_copy(
            src_ref=kv.at[src, j],
            dst_ref=kv.at[dst, j],
            send_sem=send_sem.at[dst if lane is None else lane, j],
            recv_sem=recv_sem.at[dst, j],
            device_id=(to, h),
            device_id_type=MESH,
        )

    def send(src, dst, j, to, lane=None):
        @pl.when(wanted(to, dst))
        def _():
            move(src, dst, j, to, lane).start()

    def arrived(d, j):
        @pl.when(wanted(s, d))
        def _():
            move(d, d, j, after).wait_recv()

    def sent(d, j, to, lane=None):
        @pl.when(wanted(to, d))
        def _():
            move(d, d, j, to, lane).wait_send()

    for j in range(PIECES):
        send(0, FAR, j, up)

        send(0, 1, j, after)

        @pl.when(z == 0)
        def _():
            send(0, FAR - 1, j, last_col)

    load_lengths.wait()
    lengths = doc_in[...]
    count = lengths.shape[1]
    shape = (count, count)
    upto = lax.broadcasted_iota(jnp.int32, shape, 1) <= lax.broadcasted_iota(jnp.int32, shape, 0)
    ends = jnp.sum(
        jnp.where(upto, jnp.broadcast_to(lengths, shape), 0).astype(jnp.float32),
        axis=1,
        keepdims=True,
    ).astype(jnp.int32)
    for i in range(PIECES):
        block = s * PIECES + i
        start = jnp.max(
            jnp.where(ends <= block, ends, 0).astype(jnp.float32), axis=0, keepdims=True
        ).astype(jnp.int32)
        reach[i] = jnp.broadcast_to(block - start, (1, COLS))

    load_queries.wait()
    for i in range(PIECES):
        for g in range(GROUP):
            rows = q_in[i * B : (i + 1) * B, g * HD : (g + 1) * HD]
            scaled = rows.astype(jnp.float32).T * SCALE
            high = scaled.astype(jnp.bfloat16)
            q_t[i, :HD, g * B : (g + 1) * B] = high
            q_t[i, HD:, g * B : (g + 1) * B] = (scaled - high.astype(jnp.float32)).astype(jnp.bfloat16)

    def update(which, chunks, first=False):
        ones = jnp.ones((EXTRA, B), jnp.bfloat16)
        keys, values, pairs = [], [], []
        for d, blocks in chunks:
            n = len(blocks)
            part = kv[d, blocks[0] : blocks[0] + n, 0].reshape(n * B, HD)
            keys.append(jnp.concatenate([part, part], axis=1))
            values += [jnp.concatenate([kv[d, j, 1], ones], axis=0) for j in blocks]
            pairs += [(d, j) for j in blocks]
        keys = jnp.concatenate(keys, axis=0)
        values = jnp.concatenate(values, axis=1)
        queries = [q_t[i] for i in which]
        reaches = [reach[i] for i in which]
        if not first:
            peaks = [top[i] for i in which]
            sums = [acc[i] for i in which]
        products = [jnp.dot(keys, q, preferred_element_type=jnp.float32) for q in queries]
        results = []
        for n, (i, far, product) in enumerate(zip(which, reaches, products)):
            scores, shown = [], []
            for b, (d, j) in enumerate(pairs):
                block = product[b * B : (b + 1) * B]
                delta = PIECES * d + i - j
                show = delta <= far
                if first:
                    key = lax.broadcasted_iota(jnp.int32, (B, COLS), 0) + j * B
                    query = lax.rem(lax.broadcasted_iota(jnp.int32, (B, COLS), 1), B) + i * B
                    block = jnp.where(key <= query, block, NEG)
                    show = show & (delta >= 0)
                shown.append(show)
                scores.append(block)
            peak = None
            for block, show in zip(scores, shown):
                here = jnp.where(show, jnp.max(block, axis=0, keepdims=True), NEG)
                peak = here if peak is None else jnp.maximum(peak, here)
            if not first:
                peak = jnp.maximum(peaks[n], peak)
                shrink = jnp.exp2(peaks[n] - peak)
            weights = [
                jnp.exp2(block - jnp.where(show, peak, -NEG)).astype(jnp.bfloat16)
                for block, show in zip(scores, shown)
            ]
            added = jnp.dot(
                values, jnp.concatenate(weights, axis=0), preferred_element_type=jnp.float32
            )
            results.append((peak, added if first else sums[n] * shrink + added))
        for i, (peak, total) in zip(which, results):
            top[i] = peak
            acc[i] = total
        return [total for _, total in results]

    every = tuple(range(PIECES))
    half = PIECES // 2

    @pl.loop(0, PIECES // 2)
    def _(i):
        update((2 * i, 2 * i + 1), [(0, every)], first=True)

    far_steps = 4 * PIECES
    lag = jnp.where(z < 2, LAG_WRAP, LAG)
    work_from = lag + 1

    @pl.loop(0, 3 * PIECES + 1 + LAG_WRAP)
    def _(t):
        j = lax.rem(t, PIECES)
        d = FAR - t // PIECES

        @pl.when((t < far_steps) & ((d < FAR) | (z != 0)))
        def _():
            arrived(d, j)

            @pl.when(d > 5)
            def _():
                send(d, d - 1, j, before)

            @pl.when((d == 5) & (z == 1))
            def _():
                send(5, 4, j, before, 0)

        @pl.when((z == 0) & (t == work_from))
        def _():
            for k in range(PIECES):
                arrived(FAR, k)

        u = t - lag
        near = u // PIECES + 1
        k = lax.rem(u + PIECES, PIECES)

        @pl.when((u >= 0) & (u < 3 * PIECES))
        def _():
            arrived(near, k)

            @pl.when((near < 3) | (z != ROWS - 1))
            def _():
                send(near, near + 1, k, after)

        w = t - work_from

        @pl.when((w >= 0) & (w < 3 * PIECES))
        def _():
            p = w // PIECES + 1
            i = 2 * lax.rem(w, 2)
            chunk = jnp.where(lax.rem(w, PIECES) < 2, FAR + 1 - p, p)
            update((i, i + 1), [(chunk, every)])

    @pl.loop(0, PIECES // 2)
    def _(i):
        update((2 * i, 2 * i + 1), [(5, every)])

    for j in every[:half]:
        arrived(4, j)

    @pl.loop(0, PIECES // 2)
    def _(i):
        update((2 * i, 2 * i + 1), [(4, every[:half])])

    for j in every[half:]:
        arrived(4, j)

    own = pltpu.make_async_copy(
        out_buf.at[h],
        out_ref.at[:, pl.ds(pl.multiple_of(h * COLS, COLS), COLS)],
        load_sem.at[0],
    )
    for hops in ((2, 1), (3, 0)):
        which = [lax.rem(x + hop, chips) for hop in hops]
        totals = update(which, [(4, every[half:])])
        for hop, i, total in zip(hops, which, totals):
            final = (total[:HD] * (1.0 / total[HD : HD + 1])).astype(jnp.bfloat16)
            part = B // CORES
            for g in range(GROUP):
                rows = final[:, g * B : (g + 1) * B].T
                for core in range(CORES):
                    out_buf[i * CORES + core, :, g * HD : (g + 1) * HD] = rows[
                        core * part : (core + 1) * part
                    ]
            for core in range(CORES):
                target = i * CORES + core
                there = pltpu.make_async_remote_copy(
                    src_ref=out_buf.at[target],
                    dst_ref=out_ref.at[:, pl.ds(pl.multiple_of(h * COLS, COLS), COLS)],
                    send_sem=out_send.at[target],
                    recv_sem=out_recv.at[h],
                    device_id=(s, target),
                    device_id_type=MESH,
                )
                if hop:
                    there.start()
                else:

                    @pl.when(h != target)
                    def _():
                        there.start()

                    @pl.when(h == target)
                    def _():
                        own.start()

    @pl.loop(0, PIECES)
    def _(j):
        for d in (1, 2, 3):
            sent(d, j, after)
        for d in (5, 6):
            sent(d, j, before)
        sent(7, j, jnp.where(z == 0, last_col, before))
        sent(FAR, j, up)

        @pl.when(z != ROWS - 1)
        def _():
            sent(4, j, after)

        @pl.when(z == 1)
        def _():
            sent(4, j, before, 0)

    for step in range(1, n_head):
        peer = lax.rem(h + step, n_head)
        other = pltpu.make_async_remote_copy(
            src_ref=out_buf.at[peer],
            dst_ref=out_ref.at[:, pl.ds(pl.multiple_of(peer * COLS, COLS), COLS)],
            send_sem=out_send.at[peer],
            recv_sem=out_recv.at[peer],
            device_id=(s, peer),
            device_id_type=MESH,
        )
        other.wait_send()
        other.wait_recv()
    own.wait()


def body(n_seq, n_head, queries, key_rows, value_rows, doc_blocks):
    tokens = queries.shape[0]
    part = tokens // n_head
    any_space = pl.BlockSpec(memory_space=pl.ANY)
    bf16, f32 = jnp.bfloat16, jnp.float32
    pairs = tokens * PIECES * FAR * B * GROUP
    return pl.pallas_call(
        functools.partial(kernel, n_seq, n_head),
        out_shape=jax.ShapeDtypeStruct((part, n_head * COLS), bf16),
        in_specs=[any_space] * 4,
        out_specs=any_space,
        scratch_shapes=[
            pltpu.VMEM((tokens, COLS), bf16),
            pltpu.VMEM((tokens, HD), bf16),
            pltpu.VMEM((1, doc_blocks.shape[0]), jnp.int32),
            pltpu.VMEM((PIECES, 2 * HD, COLS), bf16),
            pltpu.VMEM((FAR + 1, PIECES, 2, B, HD), bf16),
            pltpu.VMEM((PIECES, 1, COLS), f32),
            pltpu.VMEM((PIECES, HD + EXTRA, COLS), f32),
            pltpu.VMEM((PIECES, 1, COLS), jnp.int32),
            pltpu.VMEM((n_head, part, COLS), bf16),
            pltpu.SemaphoreType.DMA((4,)),
            pltpu.SemaphoreType.DMA((FAR + 1, PIECES)),
            pltpu.SemaphoreType.DMA((FAR + 1, PIECES)),
            pltpu.SemaphoreType.DMA((n_head,)),
            pltpu.SemaphoreType.DMA((n_head,)),
        ],
        compiler_params=pltpu.CompilerParams(
            collective_id=0, has_side_effects=True, vmem_limit_bytes=62 << 20
        ),
        cost_estimate=pl.CostEstimate(
            flops=4 * pairs * HD, bytes_accessed=2 << 20, transcendentals=pairs
        ),
        name="attend",
    )(queries, key_rows.reshape(PIECES, B, HD), value_rows, doc_blocks.reshape(1, -1))


def solution(mesh):
    in_specs = (P("seq", "head"), P("seq", "head"), P("seq", "head"), P())
    out_specs = P(("seq", "head"), None)
    return jax.shard_map(
        functools.partial(body, mesh.shape["seq"], mesh.shape["head"]),
        mesh=mesh,
        in_specs=in_specs,
        out_specs=out_specs,
        check_vma=False,
    )
```

```python
import functools
import math

import jax
import jax.numpy as jnp
from jax import lax
from jax.experimental import pallas as pl
from jax.experimental.pallas import tpu as pltpu
from jax.sharding import PartitionSpec as P

HD = 128
B = 128
GROUP = 4
ROWS = 8
PIECES = 4
FAR = 8
CORES = 2
COLS = GROUP * B
EXTRA = 16
LAG = 2
LAG_WRAP = 4

NEG = -1e30
SCALE = math.log2(math.e) / math.sqrt(HD)
MESH = pl.DeviceIdType.MESH


def kernel(
    n_seq,
    n_head,
    q_hbm,
    k_hbm,
    v_hbm,
    doc_hbm,
    out_ref,
    q_in,
    v_in,
    doc_in,
    q_t,
    kv,
    top,
    acc,
    reach,
    out_buf,
    load_sem,
    send_sem,
    recv_sem,
    out_send,
    out_recv,
):
    s = lax.axis_index("seq")
    h = lax.axis_index("head")
    z = lax.rem(s, ROWS)
    chips = n_head // CORES
    x = h // CORES

    def ring(distance):
        return lax.rem(s + distance + n_seq, n_seq)

    after, before = ring(1), ring(-1)
    up, down = ring(ROWS), ring(-ROWS)
    first_col = ring(-(ROWS - 1))
    last_col = ring(ROWS - 1)

    def wanted(who, d):
        beyond = d - who
        return (beyond <= 0) | (beyond == ROWS - 2) | (beyond == ROWS - 1)

    @pl.when(s < ROWS)
    def _():
        @pl.loop(1, FAR + 1)
        def _(d):
            kv[d] = jnp.zeros(kv.shape[1:], kv.dtype)

    loads = [
        pltpu.make_async_copy(
            k_hbm.at[pl.ds(j * B, B), :], kv.at[0, j, 0], load_sem.at[j]
        )
        for j in range(PIECES)
    ]
    loads.append(pltpu.make_async_copy(v_hbm, v_in, load_sem.at[PIECES]))
    loads.append(pltpu.make_async_copy(doc_hbm, doc_in, load_sem.at[PIECES + 1]))
    loads.append(pltpu.make_async_copy(q_hbm, q_in, load_sem.at[PIECES + 2]))
    barrier = pltpu.get_barrier_semaphore()

    def greet(to_seq, to_head):
        pl.semaphore_signal(barrier, inc=1, device_id=(to_seq, to_head), device_id_type=MESH)

    for to in (after, before, up, down):
        greet(to, h)
    for step in range(1, n_head):
        greet(s, lax.rem(h + step, n_head))

    @pl.when(z == ROWS - 1)
    def _():
        greet(first_col, h)

    @pl.when(z == 0)
    def _():
        greet(last_col, h)

    for copy in loads:
        copy.start()
    for copy in loads[: PIECES + 1]:
        copy.wait()
    for j in range(PIECES):
        kv[0, j, 1] = v_in[pl.ds(j * B, B), :].T

    edge = jnp.where((z == 0) | (z == ROWS - 1), 1, 0)
    pl.semaphore_wait(barrier, 4 + n_head - 1 + edge)

    def move(src, dst, j, to, lane=None):
        return pltpu.make_async_remote_copy(
            src_ref=kv.at[src, j],
            dst_ref=kv.at[dst, j],
            send_sem=send_sem.at[dst if lane is None else lane, j],
            recv_sem=recv_sem.at[dst, j],
            device_id=(to, h),
            device_id_type=MESH,
        )

    def send(src, dst, j, to, lane=None):
        @pl.when(wanted(to, dst))
        def _():
            move(src, dst, j, to, lane).start()

    def arrived(d, j):
        @pl.when(wanted(s, d))
        def _():
            move(d, d, j, after).wait_recv()

    def sent(d, j, to, lane=None):
        @pl.when(wanted(to, d))
        def _():
            move(d, d, j, to, lane).wait_send()

    for j in range(PIECES):
        @pl.when(z != 0)
        def _():
            send(0, FAR, j, up)

        send(0, 1, j, after)

        @pl.when(z == 0)
        def _():
            send(0, FAR - 1, j, last_col)

    loads[PIECES + 1].wait()
    lengths = doc_in[...]
    count = lengths.shape[1]
    shape = (count, count)
    upto = lax.broadcasted_iota(jnp.int32, shape, 1) <= lax.broadcasted_iota(jnp.int32, shape, 0)
    ends = jnp.sum(
        jnp.where(upto, jnp.broadcast_to(lengths, shape), 0).astype(jnp.float32),
        axis=1,
        keepdims=True,
    ).astype(jnp.int32)
    for i in range(PIECES):
        block = s * PIECES + i
        start = jnp.max(
            jnp.where(ends <= block, ends, 0).astype(jnp.float32), axis=0, keepdims=True
        ).astype(jnp.int32)
        reach[i] = jnp.broadcast_to(block - start, (1, COLS))

    loads[PIECES + 2].wait()
    for i in range(PIECES):
        for g in range(GROUP):
            rows = q_in[i * B : (i + 1) * B, g * HD : (g + 1) * HD]
            scaled = rows.astype(jnp.float32).T * SCALE
            high = scaled.astype(jnp.bfloat16)
            q_t[i, :HD, g * B : (g + 1) * B] = high
            q_t[i, HD:, g * B : (g + 1) * B] = (scaled - high.astype(jnp.float32)).astype(jnp.bfloat16)

    def update(which, chunks, first=False):
        ones = jnp.ones((EXTRA, B), jnp.bfloat16)
        keys, values, pairs = [], [], []
        for d, blocks in chunks:
            n = len(blocks)
            part = kv[d, blocks[0] : blocks[0] + n, 0].reshape(n * B, HD)
            keys.append(jnp.concatenate([part, part], axis=1))
            values += [jnp.concatenate([kv[d, j, 1], ones], axis=0) for j in blocks]
            pairs += [(d, j) for j in blocks]
        keys = jnp.concatenate(keys, axis=0)
        values = jnp.concatenate(values, axis=1)
        queries = [q_t[i] for i in which]
        reaches = [reach[i] for i in which]
        if not first:
            peaks = [top[i] for i in which]
            sums = [acc[i] for i in which]
        products = [jnp.dot(keys, q, preferred_element_type=jnp.float32) for q in queries]
        results = []
        for n, (i, far, product) in enumerate(zip(which, reaches, products)):
            scores, shown = [], []
            for b, (d, j) in enumerate(pairs):
                block = product[b * B : (b + 1) * B]
                delta = PIECES * d + i - j
                show = delta <= far
                if first:
                    key = lax.broadcasted_iota(jnp.int32, (B, COLS), 0) + j * B
                    query = lax.rem(lax.broadcasted_iota(jnp.int32, (B, COLS), 1), B) + i * B
                    block = jnp.where(key <= query, block, NEG)
                    show = show & (delta >= 0)
                shown.append(show)
                scores.append(block)
            peak = None
            for block, show in zip(scores, shown):
                here = jnp.where(show, jnp.max(block, axis=0, keepdims=True), NEG)
                peak = here if peak is None else jnp.maximum(peak, here)
            if not first:
                peak = jnp.maximum(peaks[n], peak)
                shrink = jnp.exp2(peaks[n] - peak)
            weights = [
                jnp.exp2(block - jnp.where(show, peak, -NEG)).astype(jnp.bfloat16)
                for block, show in zip(scores, shown)
            ]
            added = jnp.dot(
                values, jnp.concatenate(weights, axis=0), preferred_element_type=jnp.float32
            )
            results.append((peak, added if first else sums[n] * shrink + added))
        for i, (peak, total) in zip(which, results):
            top[i] = peak
            acc[i] = total
        return [total for _, total in results]

    every = tuple(range(PIECES))
    half = PIECES // 2

    @pl.loop(0, PIECES // 2)
    def _(i):
        update((2 * i, 2 * i + 1), [(0, every)], first=True)

    far_steps = 4 * PIECES
    lag = jnp.where(z < 2, LAG_WRAP, LAG)
    work_from = lag + jnp.where(z == 0, PIECES - 1, 1)

    @pl.loop(0, 4 * PIECES - 1 + LAG_WRAP)
    def _(t):
        j = lax.rem(t, PIECES)
        d = FAR - t // PIECES

        @pl.when((t < far_steps) & ((d < FAR) | (z != 0)))
        def _():
            arrived(d, j)

            @pl.when(d > 5)
            def _():
                send(d, d - 1, j, before)

            @pl.when((d == 5) & (z == 1))
            def _():
                send(5, 4, j, before, 0)

        @pl.when((z == 0) & (t >= PIECES) & (t < 2 * PIECES))
        def _():
            send(0, FAR, j, up)

        u = t - lag
        near = u // PIECES + 1
        k = lax.rem(u + PIECES, PIECES)

        @pl.when((u >= 0) & (u < 3 * PIECES))
        def _():
            arrived(near, k)

            @pl.when((near < 3) | (z != ROWS - 1))
            def _():
                send(near, near + 1, k, after)

        w = t - work_from

        @pl.when((w >= 0) & (w < 3 * PIECES))
        def _():
            p = w // PIECES + 1
            i = 2 * lax.rem(w, 2)
            early = lax.rem(w, PIECES) < 2
            chunk = jnp.where(z == 0, jnp.where(early, p, FAR - p), jnp.where(early, FAR + 1 - p, p))
            update((i, i + 1), [(chunk, every)])

    @pl.when(z == 0)
    def _():
        for j in every:
            arrived(FAR, j)

    @pl.loop(0, PIECES // 2)
    def _(i):
        update((2 * i, 2 * i + 1), [(jnp.where(z == 0, FAR, 5), every)])

    for j in every[:half]:
        arrived(4, j)

    @pl.loop(0, PIECES // 2)
    def _(i):
        update((2 * i, 2 * i + 1), [(4, every[:half])])

    for j in every[half:]:
        arrived(4, j)

    own = pltpu.make_async_copy(
        out_buf.at[h],
        out_ref.at[:, pl.ds(pl.multiple_of(h * COLS, COLS), COLS)],
        load_sem.at[0],
    )
    for hops in ((2, 1), (3, 0)):
        which = [lax.rem(x + hop, chips) for hop in hops]
        totals = update(which, [(4, every[half:])])
        for hop, i, total in zip(hops, which, totals):
            final = (total[:HD] * (1.0 / total[HD : HD + 1])).astype(jnp.bfloat16)
            part = B // CORES
            for g in range(GROUP):
                rows = final[:, g * B : (g + 1) * B].T
                for core in range(CORES):
                    out_buf[i * CORES + core, :, g * HD : (g + 1) * HD] = rows[
                        core * part : (core + 1) * part
                    ]
            for core in range(CORES):
                target = i * CORES + core
                there = pltpu.make_async_remote_copy(
                    src_ref=out_buf.at[target],
                    dst_ref=out_ref.at[:, pl.ds(pl.multiple_of(h * COLS, COLS), COLS)],
                    send_sem=out_send.at[target],
                    recv_sem=out_recv.at[h],
                    device_id=(s, target),
                    device_id_type=MESH,
                )
                if hop:
                    there.start()
                else:

                    @pl.when(h != target)
                    def _():
                        there.start()

                    @pl.when(h == target)
                    def _():
                        own.start()

    @pl.loop(0, PIECES)
    def _(j):
        for d in (1, 2, 3):
            sent(d, j, after)
        for d in (5, 6):
            sent(d, j, before)
        sent(7, j, jnp.where(z == 0, last_col, before))
        sent(FAR, j, up)

        @pl.when(z != ROWS - 1)
        def _():
            sent(4, j, after)

        @pl.when(z == 1)
        def _():
            sent(4, j, before, 0)

    for step in range(1, n_head):
        peer = lax.rem(h + step, n_head)
        other = pltpu.make_async_remote_copy(
            src_ref=out_buf.at[peer],
            dst_ref=out_ref.at[:, pl.ds(pl.multiple_of(peer * COLS, COLS), COLS)],
            send_sem=out_send.at[peer],
            recv_sem=out_recv.at[peer],
            device_id=(s, peer),
            device_id_type=MESH,
        )
        other.wait_send()
        other.wait_recv()
    own.wait()


def body(n_seq, n_head, queries, key_rows, value_rows, doc_blocks):
    tokens = queries.shape[0]
    part = tokens // n_head
    any_space = pl.BlockSpec(memory_space=pl.ANY)
    bf16, f32 = jnp.bfloat16, jnp.float32
    pairs = tokens * PIECES * FAR * B * GROUP
    return pl.pallas_call(
        functools.partial(kernel, n_seq, n_head),
        out_shape=jax.ShapeDtypeStruct((part, n_head * COLS), bf16),
        in_specs=[any_space] * 4,
        out_specs=any_space,
        scratch_shapes=[
            pltpu.VMEM((tokens, COLS), bf16),
            pltpu.VMEM((tokens, HD), bf16),
            pltpu.VMEM((1, doc_blocks.shape[0]), jnp.int32),
            pltpu.VMEM((PIECES, 2 * HD, COLS), bf16),
            pltpu.VMEM((FAR + 1, PIECES, 2, B, HD), bf16),
            pltpu.VMEM((PIECES, 1, COLS), f32),
            pltpu.VMEM((PIECES, HD + EXTRA, COLS), f32),
            pltpu.VMEM((PIECES, 1, COLS), jnp.int32),
            pltpu.VMEM((n_head, part, COLS), bf16),
            pltpu.SemaphoreType.DMA((PIECES + 3,)),
            pltpu.SemaphoreType.DMA((FAR + 1, PIECES)),
            pltpu.SemaphoreType.DMA((FAR + 1, PIECES)),
            pltpu.SemaphoreType.DMA((n_head,)),
            pltpu.SemaphoreType.DMA((n_head,)),
        ],
        compiler_params=pltpu.CompilerParams(
            collective_id=0, has_side_effects=True, vmem_limit_bytes=62 << 20
        ),
        cost_estimate=pl.CostEstimate(
            flops=4 * pairs * HD, bytes_accessed=2 << 20, transcendentals=pairs
        ),
        name="attend",
    )(queries, key_rows, value_rows, doc_blocks.reshape(1, -1))


def solution(mesh):
    in_specs = (P("seq", "head"), P("seq", "head"), P("seq", "head"), P())
    out_specs = P(("seq", "head"), None)
    return jax.shard_map(
        functools.partial(body, mesh.shape["seq"], mesh.shape["head"]),
        mesh=mesh,
        in_specs=in_specs,
        out_specs=out_specs,
        check_vma=False,
    )
```

```python
import functools
import math

import jax
import jax.numpy as jnp
from jax import lax
from jax.experimental import pallas as pl
from jax.experimental.pallas import tpu as pltpu
from jax.sharding import PartitionSpec as P

HD = 128
B = 128
GROUP = 4
ROWS = 8
PIECES = 4
FAR = 8
CORES = 2
COLS = GROUP * B
EXTRA = 16
LAG = 2
LAG_WRAP = 4

NEG = -1e30
SCALE = math.log2(math.e) / math.sqrt(HD)
MESH = pl.DeviceIdType.MESH


def kernel(
    n_seq,
    n_head,
    q_hbm,
    k_hbm,
    v_hbm,
    doc_hbm,
    out_ref,
    q_in,
    v_in,
    doc_in,
    q_t,
    kv,
    top,
    acc,
    reach,
    out_buf,
    load_sem,
    send_sem,
    recv_sem,
    out_send,
    out_recv,
):
    s = lax.axis_index("seq")
    h = lax.axis_index("head")
    z = lax.rem(s, ROWS)
    chips = n_head // CORES
    x = h // CORES

    def ring(distance):
        return lax.rem(s + distance + n_seq, n_seq)

    after, before = ring(1), ring(-1)
    up, down = ring(ROWS), ring(-ROWS)
    first_col = ring(-(ROWS - 1))
    last_col = ring(ROWS - 1)

    def wanted(who, d):
        beyond = d - who
        return (beyond <= 0) | (beyond == ROWS - 2) | (beyond == ROWS - 1)

    @pl.when(s < ROWS)
    def _():
        @pl.loop(1, FAR + 1)
        def _(d):
            kv[d] = jnp.zeros(kv.shape[1:], kv.dtype)

    loads = [
        pltpu.make_async_copy(
            k_hbm.at[pl.ds(j * B, B), :], kv.at[0, j, 0], load_sem.at[j]
        )
        for j in range(PIECES)
    ]
    loads.append(pltpu.make_async_copy(v_hbm, v_in, load_sem.at[PIECES]))
    loads.append(pltpu.make_async_copy(doc_hbm, doc_in, load_sem.at[PIECES + 1]))
    loads.append(pltpu.make_async_copy(q_hbm, q_in, load_sem.at[PIECES + 2]))
    barrier = pltpu.get_barrier_semaphore()

    def greet(to_seq, to_head):
        pl.semaphore_signal(barrier, inc=1, device_id=(to_seq, to_head), device_id_type=MESH)

    for to in (after, before, up, down):
        greet(to, h)
    for step in range(1, n_head):
        greet(s, lax.rem(h + step, n_head))

    @pl.when(z == ROWS - 1)
    def _():
        greet(first_col, h)

    @pl.when(z == 0)
    def _():
        greet(last_col, h)

    for copy in loads:
        copy.start()
    for copy in loads[: PIECES + 1]:
        copy.wait()
    for j in range(PIECES):
        kv[0, j, 1] = v_in[pl.ds(j * B, B), :].T

    edge = jnp.where((z == 0) | (z == ROWS - 1), 1, 0)
    pl.semaphore_wait(barrier, 4 + n_head - 1 + edge)

    def move(src, dst, j, to, lane=None):
        return pltpu.make_async_remote_copy(
            src_ref=kv.at[src, j],
            dst_ref=kv.at[dst, j],
            send_sem=send_sem.at[dst if lane is None else lane, j],
            recv_sem=recv_sem.at[dst, j],
            device_id=(to, h),
            device_id_type=MESH,
        )

    def send(src, dst, j, to, lane=None):
        @pl.when(wanted(to, dst))
        def _():
            move(src, dst, j, to, lane).start()

    def arrived(d, j):
        @pl.when(wanted(s, d))
        def _():
            move(d, d, j, after).wait_recv()

    def sent(d, j, to, lane=None):
        @pl.when(wanted(to, d))
        def _():
            move(d, d, j, to, lane).wait_send()

    for j in range(PIECES):
        send(0, FAR, j, up)

        send(0, 1, j, after)

        @pl.when(z == 0)
        def _():
            send(0, FAR - 1, j, last_col)

    loads[PIECES + 1].wait()
    lengths = doc_in[...]
    count = lengths.shape[1]
    shape = (count, count)
    upto = lax.broadcasted_iota(jnp.int32, shape, 1) <= lax.broadcasted_iota(jnp.int32, shape, 0)
    ends = jnp.sum(
        jnp.where(upto, jnp.broadcast_to(lengths, shape), 0).astype(jnp.float32),
        axis=1,
        keepdims=True,
    ).astype(jnp.int32)
    for i in range(PIECES):
        block = s * PIECES + i
        start = jnp.max(
            jnp.where(ends <= block, ends, 0).astype(jnp.float32), axis=0, keepdims=True
        ).astype(jnp.int32)
        reach[i] = jnp.broadcast_to(block - start, (1, COLS))

    loads[PIECES + 2].wait()
    for i in range(PIECES):
        for g in range(GROUP):
            rows = q_in[i * B : (i + 1) * B, g * HD : (g + 1) * HD]
            scaled = rows.astype(jnp.float32).T * SCALE
            high = scaled.astype(jnp.bfloat16)
            q_t[i, :HD, g * B : (g + 1) * B] = high
            q_t[i, HD:, g * B : (g + 1) * B] = (scaled - high.astype(jnp.float32)).astype(jnp.bfloat16)

    def update(which, chunks, first=False):
        ones = jnp.ones((EXTRA, B), jnp.bfloat16)
        keys, values, pairs = [], [], []
        for d, blocks in chunks:
            n = len(blocks)
            part = kv[d, blocks[0] : blocks[0] + n, 0].reshape(n * B, HD)
            keys.append(jnp.concatenate([part, part], axis=1))
            values += [jnp.concatenate([kv[d, j, 1], ones], axis=0) for j in blocks]
            pairs += [(d, j) for j in blocks]
        keys = jnp.concatenate(keys, axis=0)
        values = jnp.concatenate(values, axis=1)
        queries = [q_t[i] for i in which]
        reaches = [reach[i] for i in which]
        if not first:
            peaks = [top[i] for i in which]
            sums = [acc[i] for i in which]
        products = [jnp.dot(keys, q, preferred_element_type=jnp.float32) for q in queries]
        results = []
        for n, (i, far, product) in enumerate(zip(which, reaches, products)):
            scores, shown = [], []
            for b, (d, j) in enumerate(pairs):
                block = product[b * B : (b + 1) * B]
                delta = PIECES * d + i - j
                show = delta <= far
                if first:
                    key = lax.broadcasted_iota(jnp.int32, (B, COLS), 0) + j * B
                    query = lax.rem(lax.broadcasted_iota(jnp.int32, (B, COLS), 1), B) + i * B
                    block = jnp.where(key <= query, block, NEG)
                    show = show & (delta >= 0)
                shown.append(show)
                scores.append(block)
            peak = None
            for block, show in zip(scores, shown):
                here = jnp.where(show, jnp.max(block, axis=0, keepdims=True), NEG)
                peak = here if peak is None else jnp.maximum(peak, here)
            if not first:
                peak = jnp.maximum(peaks[n], peak)
                shrink = jnp.exp2(peaks[n] - peak)
            weights = [
                jnp.exp2(block - jnp.where(show, peak, -NEG)).astype(jnp.bfloat16)
                for block, show in zip(scores, shown)
            ]
            added = jnp.dot(
                values, jnp.concatenate(weights, axis=0), preferred_element_type=jnp.float32
            )
            results.append((peak, added if first else sums[n] * shrink + added))
        for i, (peak, total) in zip(which, results):
            top[i] = peak
            acc[i] = total
        return [total for _, total in results]

    every = tuple(range(PIECES))
    half = PIECES // 2

    @pl.loop(0, PIECES // 2)
    def _(i):
        update((2 * i, 2 * i + 1), [(0, every)], first=True)

    far_steps = 4 * PIECES
    lag = jnp.where(z < 2, LAG_WRAP, LAG)
    work_from = lag + 1

    @pl.loop(0, 3 * PIECES + 1 + LAG_WRAP)
    def _(t):
        j = lax.rem(t, PIECES)
        d = FAR - t // PIECES

        @pl.when((t < far_steps) & ((d < FAR) | (z != 0)))
        def _():
            arrived(d, j)

            @pl.when(d > 5)
            def _():
                send(d, d - 1, j, before)

            @pl.when((d == 5) & (z == 1))
            def _():
                send(5, 4, j, before, 0)

        @pl.when((z == 0) & (t == work_from))
        def _():
            for k in range(PIECES):
                arrived(FAR, k)

        u = t - lag
        near = u // PIECES + 1
        k = lax.rem(u + PIECES, PIECES)

        @pl.when((u >= 0) & (u < 3 * PIECES))
        def _():
            arrived(near, k)

            @pl.when((near < 3) | (z != ROWS - 1))
            def _():
                send(near, near + 1, k, after)

        w = t - work_from

        @pl.when(w == 0)
        def _():
            update((0, 1), [(FAR, every[1:])])

        @pl.when(w == 1)
        def _():
            update((2, 3), [(FAR, every[3:])])

        @pl.when((w >= 2) & (w < 3 * PIECES))
        def _():
            p = w // PIECES + 1
            i = 2 * lax.rem(w, 2)
            chunk = jnp.where(lax.rem(w, PIECES) < 2, FAR + 1 - p, p)
            update((i, i + 1), [(chunk, every)])

    @pl.loop(0, PIECES // 2)
    def _(i):
        update((2 * i, 2 * i + 1), [(5, every)])

    for j in every[:half]:
        arrived(4, j)

    @pl.loop(0, PIECES // 2)
    def _(i):
        update((2 * i, 2 * i + 1), [(4, every[:half])])

    for j in every[half:]:
        arrived(4, j)

    own = pltpu.make_async_copy(
        out_buf.at[h],
        out_ref.at[:, pl.ds(pl.multiple_of(h * COLS, COLS), COLS)],
        load_sem.at[0],
    )
    for hops in ((2, 1), (3, 0)):
        which = [lax.rem(x + hop, chips) for hop in hops]
        totals = update(which, [(4, every[half:])])
        for hop, i, total in zip(hops, which, totals):
            final = (total[:HD] * (1.0 / total[HD : HD + 1])).astype(jnp.bfloat16)
            part = B // CORES
            for g in range(GROUP):
                rows = final[:, g * B : (g + 1) * B].T
                for core in range(CORES):
                    out_buf[i * CORES + core, :, g * HD : (g + 1) * HD] = rows[
                        core * part : (core + 1) * part
                    ]
            for core in range(CORES):
                target = i * CORES + core
                there = pltpu.make_async_remote_copy(
                    src_ref=out_buf.at[target],
                    dst_ref=out_ref.at[:, pl.ds(pl.multiple_of(h * COLS, COLS), COLS)],
                    send_sem=out_send.at[target],
                    recv_sem=out_recv.at[h],
                    device_id=(s, target),
                    device_id_type=MESH,
                )
                if hop:
                    there.start()
                else:

                    @pl.when(h != target)
                    def _():
                        there.start()

                    @pl.when(h == target)
                    def _():
                        own.start()

    @pl.loop(0, PIECES)
    def _(j):
        for d in (1, 2, 3):
            sent(d, j, after)
        for d in (5, 6):
            sent(d, j, before)
        sent(7, j, jnp.where(z == 0, last_col, before))
        sent(FAR, j, up)

        @pl.when(z != ROWS - 1)
        def _():
            sent(4, j, after)

        @pl.when(z == 1)
        def _():
            sent(4, j, before, 0)

    for step in range(1, n_head):
        peer = lax.rem(h + step, n_head)
        other = pltpu.make_async_remote_copy(
            src_ref=out_buf.at[peer],
            dst_ref=out_ref.at[:, pl.ds(pl.multiple_of(peer * COLS, COLS), COLS)],
            send_sem=out_send.at[peer],
            recv_sem=out_recv.at[peer],
            device_id=(s, peer),
            device_id_type=MESH,
        )
        other.wait_send()
        other.wait_recv()
    own.wait()


def body(n_seq, n_head, queries, key_rows, value_rows, doc_blocks):
    tokens = queries.shape[0]
    part = tokens // n_head
    any_space = pl.BlockSpec(memory_space=pl.ANY)
    bf16, f32 = jnp.bfloat16, jnp.float32
    pairs = tokens * PIECES * FAR * B * GROUP
    return pl.pallas_call(
        functools.partial(kernel, n_seq, n_head),
        out_shape=jax.ShapeDtypeStruct((part, n_head * COLS), bf16),
        in_specs=[any_space] * 4,
        out_specs=any_space,
        scratch_shapes=[
            pltpu.VMEM((tokens, COLS), bf16),
            pltpu.VMEM((tokens, HD), bf16),
            pltpu.VMEM((1, doc_blocks.shape[0]), jnp.int32),
            pltpu.VMEM((PIECES, 2 * HD, COLS), bf16),
            pltpu.VMEM((FAR + 1, PIECES, 2, B, HD), bf16),
            pltpu.VMEM((PIECES, 1, COLS), f32),
            pltpu.VMEM((PIECES, HD + EXTRA, COLS), f32),
            pltpu.VMEM((PIECES, 1, COLS), jnp.int32),
            pltpu.VMEM((n_head, part, COLS), bf16),
            pltpu.SemaphoreType.DMA((PIECES + 3,)),
            pltpu.SemaphoreType.DMA((FAR + 1, PIECES)),
            pltpu.SemaphoreType.DMA((FAR + 1, PIECES)),
            pltpu.SemaphoreType.DMA((n_head,)),
            pltpu.SemaphoreType.DMA((n_head,)),
        ],
        compiler_params=pltpu.CompilerParams(
            collective_id=0, has_side_effects=True, vmem_limit_bytes=62 << 20
        ),
        cost_estimate=pl.CostEstimate(
            flops=4 * pairs * HD, bytes_accessed=2 << 20, transcendentals=pairs
        ),
        name="attend",
    )(queries, key_rows, value_rows, doc_blocks.reshape(1, -1))


def solution(mesh):
    in_specs = (P("seq", "head"), P("seq", "head"), P("seq", "head"), P())
    out_specs = P(("seq", "head"), None)
    return jax.shard_map(
        functools.partial(body, mesh.shape["seq"], mesh.shape["head"]),
        mesh=mesh,
        in_specs=in_specs,
        out_specs=out_specs,
        check_vma=False,
    )
```
